32 devices in a mesh: ra: 8 (over y, x, core), dec: 4 (over z).
Axes of the slice: x: 2, y: 2, z: 4, core: 2. Of those that a mesh axis runs over, the one named last changes fastest.
Arguments:
- completeness: float32 [64, 64, 512], P(None, 'ra', 'dec'), may hold values from 0.3 to 1
- stencil: float32 [25, 64], replicated, may hold values from 0.02 to 0.08
- features: bfloat16 [96, 16384], P(None, ('ra', 'dec')), may hold values from -6 to 6
- frequencies: bfloat16 [96, 256], replicated, may hold values from -2 to 2
- gal_cell: int32 [16384], P(('ra', 'dec')), may hold values from 0 to 65535
- pip: bfloat16 [128, 12, 128, 128], P(('ra', 'dec')), may hold values from 0.019897461 to 0.19921875
- pair_src: int32 [128, 12], P(('ra', 'dec')), may hold values from 0 to 35
- pair_count: int32 [128], P(('ra', 'dec')), may hold values from 4 to 12
Outputs:
- basis_sums: bfloat16 [256, 16384], P(None, ('ra', 'dec'))
The draws below stay inside these ranges and needn't reach their ends.
Inputs may be any that keep to these rules, and one draw needn't show every extreme that they name: pair_src = slot * 4 + block; slot q names the tile offset q // 3 - 1 along ra and q % 3 - 1 along dec, block a block of that tile. gal_cell = band * 8 * 128 + row * 128 + column of the galaxy's cell within its own tile. Slots at or past pair_count are ignored.
All inputs are finite; a program needn't handle non-finite values.
Results may differ from the reference program's by a relative error of at most 0.017.
Values may be sent and summed in bfloat16 or wider, within the bound.
No kernel may reach another device: no remote copies, remote signals or barrier semaphores. Data moves between devices by JAX's collectives and lax.ppermute only.
A program may use at most 64 MiB of HBM per device.

```python
import math
import jax
import jax.numpy as jnp
from jax import lax

F = 96
NF = 256
BANDS = 64
BLOCK = 128
PB = 12
BLK_DEV = 4
CX = 8
CY = 128
GAL_DEV = 512
GALS = 16384
BLOCKS = 128
NX = 64
NY = 512
N_RA = 8
N_DEC = 4


def set_ends(array, stream_key, low, largest):
    longest = array.shape.index(max(array.shape))
    spots = []
    for shift in (0, 1):
        where = [jax.random.randint(jax.random.fold_in(stream_key, axis), (), 0, length) for axis, length in enumerate(array.shape)]
        where[longest] = (where[longest] + shift) % array.shape[longest]
        spots.append(tuple(where))
    return array.at[spots[0]].set(low).at[spots[1]].set(largest)


def steps_of(key, extent, split, least, top_value):
    def one(dim, shards_of):
        heights = jax.random.uniform(jax.random.fold_in(jax.random.fold_in(key, 6), dim), (shards_of,), jnp.float32, least / len(split), top_value / len(split))
        return jnp.repeat(jnp.exp(heights), extent[dim] // shards_of).reshape((-1,) + (1,) * (len(extent) - dim - 1))

    gain = one(*split[0])
    for cut in split[1:]:
        gain = gain * one(*cut)
    return gain


def centred(key, extent, spread, bound, pieces=(), held_as=jnp.bfloat16):
    factor_of = steps_of(key, extent, pieces, -0.22, 0.18) if pieces else 1.0
    drawn = jax.random.normal(key, extent, jnp.float32) * spread * factor_of
    return jnp.minimum(jnp.maximum(drawn, -bound), bound).astype(held_as)


def setup_inputs(seed: int = 0) -> dict:
    key_list = jax.random.split(jax.random.key(seed), 9)
    return {
        "completeness": jnp.clip(0.3 + 0.7 * jax.random.uniform(key_list[0], (BANDS, NX, NY), jnp.float32) ** steps_of(key_list[0], (BANDS, NX, NY), ((1, 8), (2, 4)), -0.2, 0.2), 0.3, 1.0),
        "stencil": jnp.clip(jnp.exp(jax.random.uniform(key_list[1], (25, BANDS), jnp.float32, math.log(0.02), math.log(0.08))), 0.02, 0.08),
        "features": centred(key_list[2], (F, GALS), 1.0, 6.0, ((1, 32),)),
        "frequencies": centred(key_list[3], (F, NF), 0.3, 2.0),
        "gal_cell": set_ends(jax.random.randint(key_list[4], (GALS,), 0, BANDS * CX * CY), jax.random.fold_in(key_list[4], 1), 0, (BANDS * CX * CY) - 1).astype(jnp.int32),
        "pip": jnp.clip(jnp.exp(math.log(0.19921875) - 2.3038113 * jax.random.uniform(key_list[5], (BLOCKS, PB, BLOCK, BLOCK), jnp.float32) ** steps_of(key_list[5], (BLOCKS, PB, BLOCK, BLOCK), ((0, 32),), -0.2, 0.2)), 0.019897461, 0.19921875).astype(jnp.bfloat16),
        "pair_src": set_ends(jax.random.randint(key_list[6], (BLOCKS, PB), 0, 9 * BLK_DEV), jax.random.fold_in(key_list[6], 1), 0, (9 * BLK_DEV) - 1).astype(jnp.int32),
        "pair_count": set_ends(jax.random.randint(key_list[7], (BLOCKS,), max(1, PB // 3), PB + 1), jax.random.fold_in(key_list[7], 1), max(1, PB // 3), PB).astype(jnp.int32),
    }


def reference(completeness, stencil, features, frequencies, gal_cell, pip, pair_src, pair_count):
    grid = jnp.pad(completeness, ((0, 0), (2, 2), (2, 2)))
    smooth = jnp.zeros(completeness.shape, jnp.float32)
    for shift_a in range(5):
        for shift_c in range(5):
            smooth = smooth + stencil[5 * shift_a + shift_c][:, None, None] * grid[:, shift_a:shift_a + NX, shift_c:shift_c + NY]
    tile_of = jnp.arange(GALS, dtype=jnp.int32) // GAL_DEV
    tile_row = tile_of // N_DEC
    tile_col = tile_of % N_DEC
    band = gal_cell // (CX * CY)
    xin = gal_cell // CY % CX
    yin = gal_cell % CY
    flat = band * (NX * NY) + (tile_row * CX + xin) * NY + tile_col * CY + yin
    gweight = lax.rsqrt(smooth.reshape(-1)[flat]).astype(jnp.bfloat16)
    theta = jnp.dot(frequencies.T, features, preferred_element_type=jnp.float32)
    wfloat = gweight.astype(jnp.float32)
    basis = jnp.concatenate([wfloat * jnp.cos(theta), wfloat * jnp.sin(theta)], 0).astype(jnp.bfloat16)
    padded = jnp.pad(basis.reshape(2 * NF, N_RA, N_DEC, GAL_DEV), ((0, 0), (1, 1), (1, 1), (0, 0)))
    theta_t = theta.reshape(NF, N_RA * N_DEC, GAL_DEV)
    weight_t = wfloat.reshape(N_RA * N_DEC, GAL_DEV)
    pip_t = pip.reshape(N_RA * N_DEC, BLK_DEV, PB, BLOCK, BLOCK)
    src_t = pair_src.reshape(N_RA * N_DEC, BLK_DEV, PB)
    count_t = pair_count.reshape(N_RA * N_DEC, BLK_DEV)

    def one_tile(tile):
        row = tile // N_DEC
        col = tile % N_DEC
        zero = jnp.zeros((), jnp.int32)
        near = lax.dynamic_slice(padded, (zero, row.astype(jnp.int32), col.astype(jnp.int32), zero), (2 * NF, 3, 3, GAL_DEV))
        near = near.reshape(2 * NF, 9 * BLK_DEV, BLOCK)
        taken = near[:, src_t[tile]]
        live = (jnp.arange(PB, dtype=jnp.int32)[None, :] < count_t[tile][:, None]).astype(jnp.float32)
        taken = taken.astype(jnp.float32) * live[None, :, :, None]
        sums = jnp.einsum('kbpj,bpij->kbi', taken, pip_t[tile].astype(jnp.float32), precision=lax.Precision.HIGHEST)
        sums = sums.reshape(2 * NF, GAL_DEV)
        own = theta_t[:, tile]
        result = weight_t[tile] * (jnp.cos(own) * sums[:NF] + jnp.sin(own) * sums[NF:])
        return result.astype(jnp.bfloat16)
    outs = lax.map(one_tile, jnp.arange(N_RA * N_DEC, dtype=jnp.int32))
    return jnp.transpose(outs, (1, 0, 2)).reshape(NF, GALS)
```

```python
import functools
import math

import jax
import jax.numpy as jnp
from jax import lax
from jax.experimental import pallas as pl
from jax.experimental.pallas import tpu as pltpu
from jax.sharding import PartitionSpec as P

BF16 = jnp.bfloat16
F32 = jnp.float32
RIM = 16

VMEM = pl.BlockSpec(memory_space=pltpu.VMEM)
SMEM = pl.BlockSpec(memory_space=pltpu.SMEM)
ANY = pl.BlockSpec(memory_space=pl.ANY)

COS = (1.0, -19.739208802178716, 64.93939402266828, -85.45681720669371, 60.24464137187665, -26.42625678337438, 7.903536371318467, -1.7143907110886711)
SIN = (6.283185307179586, -41.34170224039975, 81.60524927607504, -76.70585975306136, 42.05869394489765, -15.094642576822986, 3.8199525848482803)


def params(limit=None, **kw):
    return pltpu.CompilerParams(vmem_limit_bytes=limit or (16 << 20), **kw)


def pairs(count, odd):
    out = []
    for i in range(odd, count - 1, 2):
        out += [(i, i + 1), (i + 1, i)]
    return out


def exchange(odd_payload, even_payload, axis):
    count = lax.axis_size(axis)
    return (
        lax.ppermute(odd_payload, axis, pairs(count, 1)),
        lax.ppermute(even_payload, axis, pairs(count, 0)),
    )


def dot(a, b, ca, cb):
    return lax.dot_general(a, b, (((ca,), (cb,)), ((), ())), preferred_element_type=F32)


def rim_kernel(comp_ref, rim_ref, rows_ref):
    bands, nx, ny = comp_ref.shape
    for x in range(nx):
        rows_ref[x * bands : (x + 1) * bands, :] = comp_ref[:, x, :]
    row = lax.broadcasted_iota(jnp.int32, (RIM, ny), 0)
    lane = lax.broadcasted_iota(jnp.int32, (RIM, ny), 1)
    pick = ((row < 2) & (lane == row)) | ((row >= 2) & (row < 4) & (lane == row + ny - 4))
    rim_ref[...] = dot(pick.astype(F32).astype(BF16), rows_ref[...].astype(BF16), 1, 1).astype(BF16)


def row_kernel(rows_ref, odd_ref, even_ref, to_odd_ref, to_even_ref):
    n = rows_ref.shape[0]
    two = to_odd_ref.shape[0] - 2 * RIM
    is_odd = lax.rem(lax.axis_index("ra"), 2) == 1

    def put(ref, start):
        ref[0:two, :] = rows_ref[start : start + two, :].astype(BF16)
        ref[two : two + RIM, :] = odd_ref[:, start : start + two]
        ref[two + RIM :, :] = even_ref[:, start : start + two]

    @pl.when(is_odd)
    def _():
        put(to_odd_ref, n - two)
        put(to_even_ref, 0)

    @pl.when(jnp.logical_not(is_odd))
    def _():
        put(to_odd_ref, 0)
        put(to_even_ref, n - two)


def weight_kernel(bands, rows_ref, d_odd_ref, d_even_ref, r_odd_ref, r_even_ref, stencil_ref, cell_ref, out_ref, st_ref, ext_ref, smooth_ref):
    n, ny = rows_ref.shape
    nx = n // bands
    two = 2 * bands
    ra_odd = lax.rem(lax.axis_index("ra"), 2) == 1
    dec_odd = lax.rem(lax.axis_index("dec"), 2) == 1

    row = lax.broadcasted_iota(jnp.int32, (RIM, ny), 0)
    lane = lax.broadcasted_iota(jnp.int32, (RIM, ny), 1)
    after = ((row < 2) & (lane == row)).astype(F32).astype(BF16)
    before = ((row >= 2) & (row < 4) & (lane == row + ny - 4)).astype(F32).astype(BF16)
    place_odd = jnp.where(dec_odd, after, before)
    place_even = jnp.where(dec_odd, before, after)

    def halo(odd, even):
        return dot(odd, place_odd, 0, 0) + dot(even, place_even, 0, 0)

    up = jnp.where(ra_odd, r_odd_ref[...], r_even_ref[...])
    down = jnp.where(ra_odd, r_even_ref[...], r_odd_ref[...])

    def extend(start, cells, edge):
        size = cells.shape[0]
        at = lax.broadcasted_iota(jnp.int32, cells.shape, 1)
        ext_ref[2, start : start + size, :] = cells
        ext_ref[3, start : start + size, :] = pltpu.roll(jnp.where(at < 1, edge, cells), ny - 1, 1)
        ext_ref[4, start : start + size, :] = pltpu.roll(jnp.where(at < 2, edge, cells), ny - 2, 1)
        ext_ref[1, start : start + size, :] = pltpu.roll(jnp.where(at > ny - 2, edge, cells), 1, 1)
        ext_ref[0, start : start + size, :] = pltpu.roll(jnp.where(at > ny - 3, edge, cells), 2, 1)

    extend(two, rows_ref[...], halo(d_odd_ref[...], d_even_ref[...]))
    extend(0, down[:two].astype(F32), halo(down[two : two + RIM], down[two + RIM :]))
    extend(two + n, up[:two].astype(F32), halo(up[two : two + RIM], up[two + RIM :]))

    st_ref[...] = jnp.zeros_like(st_ref)
    st_ref[0 : stencil_ref.shape[0], 0:bands] = stencil_ref[...]
    by_band = st_ref[...].T
    for g in range(bands // 8):
        accs = [jnp.zeros((8, ny), F32) for _ in range(nx)]
        for c in range(5):
            for a in range(5):
                k = 5 * a + c
                w = jnp.broadcast_to(by_band[8 * g : 8 * g + 8, k : k + 1], (8, ny))
                for x in range(nx):
                    base = (x + a) * bands + 8 * g
                    accs[x] = accs[x] + w * ext_ref[c, base : base + 8, :]
        for x in range(nx):
            smooth_ref[x * bands + 8 * g : x * bands + 8 * g + 8, :] = accs[x]

    smooth = smooth_ref[...]
    high = smooth.astype(BF16)
    low = (smooth - high.astype(F32)).astype(BF16)
    cell = cell_ref[...]
    galaxies = cell.shape[1]
    slot = (cell // ny % nx) * bands + cell // (nx * ny)
    hit = lax.broadcasted_iota(jnp.int32, (n, galaxies), 0) == slot
    hit = jnp.where(hit, 1.0, 0.0).astype(BF16)
    found = dot(high, hit, 0, 0) + dot(low, hit, 0, 0)
    at = lax.broadcasted_iota(jnp.int32, (ny, galaxies), 0) == cell % ny
    value = jnp.sum(jnp.where(at, found, 0.0), axis=0, keepdims=True)
    out_ref[...] = jnp.broadcast_to(lax.rsqrt(value), out_ref.shape).astype(BF16)


def stack_weight_kernel(own_ref, odd_ref, even_ref, out_ref):
    at = lax.broadcasted_iota(jnp.int32, out_ref.shape, 0)
    out = jnp.where(at == 1, odd_ref[...].astype(F32), own_ref[...].astype(F32))
    out_ref[...] = jnp.where(at == 2, even_ref[...].astype(F32), out).astype(BF16)


def stack_rows_kernel(a_ref, b_ref, c_ref, out_ref):
    n = a_ref.shape[0]
    out_ref[0:n, :] = a_ref[...]
    out_ref[n : 2 * n, :] = b_ref[...]
    out_ref[2 * n :, :] = c_ref[...]


def sincos(theta):
    turns = theta * (0.5 / math.pi)
    magic = 12582912.0
    r = turns - ((turns + magic) - magic)
    z = r * r
    c = jnp.full_like(z, COS[-1])
    for k in COS[-2::-1]:
        c = c * z + k
    s = jnp.full_like(z, SIN[-1])
    for k in SIN[-2::-1]:
        s = s * z + k
    return c, s * r


def basis_kernel(first, tiles, nblk, freq_ref, *refs):
    feat_refs, out_ref, ft_ref = refs[: len(tiles)], refs[-2], refs[-1]
    feats, nfreq = freq_ref.shape
    blk = out_ref.shape[2]
    ft_ref[...] = freq_ref[...].astype(F32).T.astype(BF16)
    at = first
    for feat_ref, count in zip(feat_refs, tiles, strict=True):
        for t in range(count):
            for b in range(nblk):
                x = feat_ref[t * feats : (t + 1) * feats, b * blk : (b + 1) * blk]
                c, s = sincos(dot(ft_ref[...], x, 1, 0))
                out_ref[at, 0:nfreq, :] = c.astype(BF16)
                out_ref[at, nfreq:, :] = s.astype(BF16)
                at += 1


def pair_kernel(src_ref, count_ref, pip_ref, basis_ref, w_own_ref, w_odd_ref, w_even_ref, out_ref, w_ref):
    nblk, slots, blk, _ = pip_ref.shape
    nfreq = out_ref.shape[0]
    ra_odd = lax.rem(lax.axis_index("ra"), 2)
    dec_odd = lax.rem(lax.axis_index("dec"), 2)
    for i, ref in enumerate((w_own_ref, w_odd_ref, w_even_ref)):
        for j in range(3):
            for b in range(nblk):
                at = (3 * i + j) * nblk + b
                w_ref[at : at + 1, :] = ref[j : j + 1, b * blk : (b + 1) * blk].astype(F32)

    def side(step, odd):
        up = 2 - odd
        return jnp.where(step == 1, 0, jnp.where(step == 2, up, 3 - up))

    for a in range(nblk):
        def place(p):
            s = src_ref[a, p]
            q = s // nblk
            return (3 * side(q // 3, ra_odd) + side(q % 3, dec_odd)) * nblk + s % nblk

        total = None
        for p in range(0, slots, 2):
            lhs, rhs = [], []
            for k in (p, p + 1):
                at = place(k)
                live = jnp.where(k < count_ref[a], 1.0, 0.0)
                lhs.append(basis_ref[at])
                rhs.append((pip_ref[a, k].astype(F32) * (w_ref[pl.ds(at, 1), :] * live)).astype(BF16))
            part = dot(jnp.concatenate(lhs, 1), jnp.concatenate(rhs, 1), 1, 1)
            total = part if total is None else total + part
        own = basis_ref[a].astype(F32)
        folded = own[:nfreq] * total[:nfreq] + own[nfreq:] * total[nfreq:]
        out_ref[:, a * blk : (a + 1) * blk] = (folded * w_ref[a : a + 1, :]).astype(BF16)


def vm(shape, dtype):
    return pltpu.VMEM(shape, dtype)


def per_device(completeness, stencil, features, frequencies, gal_cell, pip, pair_src, pair_count):
    bands, nx, ny = completeness.shape
    feats, galaxies = features.shape
    nfreq = frequencies.shape[1]
    nblk, slots, blk, _ = pip.shape
    n = bands * nx
    two = 2 * bands

    rim, rows = pl.pallas_call(
        rim_kernel, out_shape=(vm((RIM, n), BF16), vm((n, ny), F32)), in_specs=[VMEM], out_specs=(VMEM, VMEM),
        compiler_params=params(), name="rim",
    )(completeness)
    d_odd, d_even = exchange(rim, rim, "dec")
    f_odd, f_even = exchange(features, features, "dec")

    to_odd, to_even = pl.pallas_call(
        row_kernel, out_shape=(vm((two + 2 * RIM, ny), BF16),) * 2, in_specs=[VMEM] * 3, out_specs=(VMEM, VMEM),
        compiler_params=params(), name="rows",
    )(rows, d_odd, d_even)
    r_odd, r_even = exchange(to_odd, to_even, "ra")
    column = pl.pallas_call(
        stack_rows_kernel, out_shape=vm((3 * feats, galaxies), BF16), in_specs=[VMEM] * 3, out_specs=VMEM,
        compiler_params=params(), name="stack_features",
    )(features, f_odd, f_even)
    c_odd, c_even = exchange(column, column, "ra")

    def basis(first, tiles, arrays, buffer):
        blocks = 9 * nblk
        shape = vm((blocks, 2 * nfreq, blk), BF16)
        body = functools.partial(basis_kernel, first, tiles, nblk)
        work = sum(tiles) * nfreq * galaxies
        common = dict(
            out_shape=shape, out_specs=VMEM, scratch_shapes=[pltpu.VMEM((nfreq, feats), BF16)], compiler_params=params(),
            cost_estimate=pl.CostEstimate(flops=work * 2 * feats + 24 * work, bytes_accessed=work * 4, transcendentals=0),
            name="basis%d" % first,
        )
        if buffer is None:
            return pl.pallas_call(body, in_specs=[VMEM] * (1 + len(arrays)), **common)(frequencies, *arrays)

        def aliased(freq_ref, *refs):
            body(freq_ref, *refs[: len(arrays)], *refs[len(arrays) + 1 :])

        return pl.pallas_call(
            aliased, in_specs=[VMEM] * (1 + len(arrays)) + [VMEM], input_output_aliases={1 + len(arrays): 0}, **common
        )(frequencies, *arrays, buffer)

    table = basis(0, (1,), (features,), None)
    table = basis(nblk, (1, 1), (f_odd, f_even), table)

    weight = pl.pallas_call(
        functools.partial(weight_kernel, bands), out_shape=vm((RIM, galaxies), BF16), in_specs=[VMEM] * 7, out_specs=VMEM,
        scratch_shapes=[pltpu.VMEM((32, 128), F32), pltpu.VMEM((5, n + 2 * two, ny), F32), pltpu.VMEM((n, ny), F32)],
        compiler_params=params(), name="weight",
    )(rows, d_odd, d_even, r_odd, r_even, stencil, gal_cell.reshape(1, galaxies))
    w_odd, w_even = exchange(weight, weight, "dec")
    w_column = pl.pallas_call(
        stack_weight_kernel, out_shape=vm((RIM, galaxies), BF16), in_specs=[VMEM] * 3, out_specs=VMEM,
        compiler_params=params(), name="stack_weights",
    )(weight, w_odd, w_even)
    table = basis(3 * nblk, (3, 3), (c_odd, c_even), table)
    x_odd, x_even = exchange(w_column, w_column, "ra")
    return pl.pallas_call(
        pair_kernel, out_shape=jax.ShapeDtypeStruct((nfreq, galaxies), BF16), in_specs=[SMEM, SMEM] + [VMEM] * 5, out_specs=VMEM,
        scratch_shapes=[pltpu.VMEM((9 * nblk + 4, blk), F32)],
        compiler_params=params(), name="pairs",
    )(pair_src, pair_count, pip, table, w_column, x_odd, x_even)


def solution(mesh):
    in_specs = (
        P(None, "ra", "dec"),
        P(),
        P(None, ("ra", "dec")),
        P(),
        P(("ra", "dec")),
        P(("ra", "dec"), None, None, None),
        P(("ra", "dec"), None),
        P(("ra", "dec")),
    )
    out_specs = P(None, ("ra", "dec"))
    return jax.shard_map(per_device, mesh=mesh, in_specs=in_specs, out_specs=out_specs, check_vma=False)
```

```python
import functools
import math

import jax
import jax.numpy as jnp
from jax import lax
from jax.experimental import pallas as pl
from jax.experimental.pallas import tpu as pltpu
from jax.sharding import PartitionSpec as P

BF16 = jnp.bfloat16
F32 = jnp.float32
LONG = 1 << 36
RIM = 16

VMEM = pl.BlockSpec(memory_space=pltpu.VMEM)
SMEM = pl.BlockSpec(memory_space=pltpu.SMEM)
ANY = pl.BlockSpec(memory_space=pl.ANY)
HBM = pl.BlockSpec(memory_space=pltpu.HBM)

COS = (0.99999922, -19.73898252, 64.92872662, -85.27239701, 58.79403871, -21.07678212)
SIN = (6.2830558, -41.33121431, 81.36681529, -74.47800454, 32.7814008)


def params(limit=None, **kw):
    return pltpu.CompilerParams(vmem_limit_bytes=limit or (16 << 20), **kw)


def exchange(axis, odd_payload, even_payload):
    ra, dec = lax.axis_size("ra"), lax.axis_size("dec")
    here = (lambda r, d: r * dec + d) if axis == "ra" else (lambda d, r: r * dec + d)
    count, other = (ra, dec) if axis == "ra" else (dec, ra)

    def swap(payload, odd):
        pairs = [(here(i, k), here(i + 1, k)) for i in range(odd, count - 1, 2) for k in range(other)]
        busy = {i for pair in pairs for i in pair}
        for i in (0, count - 1):
            ends = [(here(i, k), here(i, k + 1)) for k in range(0, other - 1, 2)]
            pairs += [pair for pair in ends if not busy & set(pair)]
        return lax.ppermute(payload, ("ra", "dec"), sorted(pairs + [(b, a) for a, b in pairs]))

    if axis == "ra":
        even = swap(even_payload, 0)
        return swap(odd_payload, 1), even
    odd = swap(odd_payload, 1)
    return odd, swap(even_payload, 0)


def sides(axis):
    i, n = lax.axis_index(axis), lax.axis_size(axis)
    odd = lax.rem(i, 2) == 1
    return odd, jnp.logical_and(i > 0, jnp.logical_not(jnp.logical_and(odd, i == n - 1)))


def dot(a, b, ca, cb):
    return lax.dot_general(a, b, (((ca,), (cb,)), ((), ())), preferred_element_type=F32)


def rim_kernel(comp_hbm, feat_hbm, freq_hbm, stencil_hbm, cell_hbm, rim_ref, rows_ref, feat_ref, freq_ref, stencil_ref, cell_ref, comp_ref, sems):
    bands, nx, ny = comp_ref.shape
    pairs = ((comp_hbm, comp_ref), (feat_hbm, feat_ref), (freq_hbm, freq_ref), (stencil_hbm, stencil_ref), (cell_hbm, cell_ref))
    copies = [pltpu.make_async_copy(a, b, sems.at[i]) for i, (a, b) in enumerate(pairs)]
    for copy in copies:
        copy.start()
    row = lax.broadcasted_iota(jnp.int32, (RIM, ny), 0)
    lane = lax.broadcasted_iota(jnp.int32, (RIM, ny), 1)
    pick = ((row < 2) & (lane == row)) | ((row >= 2) & (row < 4) & (lane == row + ny - 4))
    copies[0].wait()
    for x in range(nx):
        rows_ref[x * bands : (x + 1) * bands, :] = comp_ref[:, x, :]
    rim_ref[...] = dot(pick.astype(F32).astype(BF16), rows_ref[...].astype(BF16), 1, 1).astype(BF16)
    for copy in copies[1:]:
        copy.wait()


def ready_kernel(bands, nx, ny, stencil_ref, cell_ref, feat_ref, rim_ref, taps_ref, hit_ref, feat_out_ref, st_ref):
    feat_out_ref[...] = feat_ref[...]
    st_ref[...] = jnp.zeros_like(st_ref)
    count = stencil_ref.shape[0]
    st_ref[0:count, 0:bands] = stencil_ref[...]
    by_band = st_ref[...].T
    for k in range(count):
        taps_ref[k * bands : (k + 1) * bands, :] = jnp.broadcast_to(by_band[0:bands, k : k + 1], (bands, ny))
    cell = cell_ref[...]
    slot = (cell // ny % nx) * bands + cell // (nx * ny)
    hit = lax.broadcasted_iota(jnp.int32, hit_ref.shape, 0) == slot
    hit_ref[...] = jnp.where(hit, 1.0, 0.0).astype(BF16)


def row_kernel(rows_ref, odd_ref, even_ref, taps_ref, hit_ref, to_odd_ref, to_even_ref):
    n = rows_ref.shape[0]
    two = to_odd_ref.shape[0] - 2 * RIM
    is_odd, _ = sides("ra")

    def put(ref, start):
        ref[0:two, :] = rows_ref[start : start + two, :].astype(BF16)
        ref[two : two + RIM, :] = odd_ref[:, start : start + two]
        ref[two + RIM :, :] = even_ref[:, start : start + two]

    @pl.when(is_odd)
    def _():
        put(to_odd_ref, n - two)
        put(to_even_ref, 0)

    @pl.when(jnp.logical_not(is_odd))
    def _():
        put(to_odd_ref, 0)
        put(to_even_ref, n - two)


def places(ny):
    dec_odd, has_odd = sides("dec")
    row = lax.broadcasted_iota(jnp.int32, (RIM, ny), 0)
    lane = lax.broadcasted_iota(jnp.int32, (RIM, ny), 1)
    after = ((row < 2) & (lane == row)).astype(F32)
    before = ((row >= 2) & (row < 4) & (lane == row + ny - 4)).astype(F32)
    odd = jnp.where(has_odd, jnp.where(dec_odd, after, before), 0.0)
    return odd.astype(BF16), jnp.where(dec_odd, before, after).astype(BF16)


def extend(ext_ref, start, cells, edge):
    size, ny = cells.shape
    at = lax.broadcasted_iota(jnp.int32, cells.shape, 1)
    ext_ref[2, start : start + size, :] = cells
    ext_ref[3, start : start + size, :] = pltpu.roll(jnp.where(at < 1, edge, cells), ny - 1, 1)
    ext_ref[4, start : start + size, :] = pltpu.roll(jnp.where(at < 2, edge, cells), ny - 2, 1)
    ext_ref[1, start : start + size, :] = pltpu.roll(jnp.where(at > ny - 2, edge, cells), 1, 1)
    ext_ref[0, start : start + size, :] = pltpu.roll(jnp.where(at > ny - 3, edge, cells), 2, 1)


def inner_kernel(bands, rows_ref, odd_ref, even_ref, taps_ref, to_odd_ref, out_ref, ext_ref):
    n, ny = rows_ref.shape
    nx = n // bands
    place_odd, place_even = places(ny)
    extend(ext_ref, 0, rows_ref[...], dot(odd_ref[...], place_odd, 0, 0) + dot(even_ref[...], place_even, 0, 0))
    for g in range(0, bands, 8):
        accs = [jnp.zeros((8, ny), F32) for _ in range(nx)]
        for c in range(5):
            for a in range(5):
                w = taps_ref[(5 * a + c) * bands + g : (5 * a + c) * bands + g + 8, :]
                for x in range(nx):
                    if 0 <= x + a - 2 < nx:
                        base = (x + a - 2) * bands + g
                        accs[x] = accs[x] + w * ext_ref[c, base : base + 8, :]
        for x in range(nx):
            out_ref[x * bands + g : x * bands + g + 8, :] = accs[x]


def weight_kernel(bands, inner_ref, odd_ref, even_ref, taps_ref, hit_ref, cell_ref, basis_in_ref, out_ref, basis_ref, ext_ref, sum_ref):
    n, ny = inner_ref.shape
    nx = n // bands
    two = 2 * bands
    ra_odd, has_odd = sides("ra")
    place_odd, place_even = places(ny)
    odd = jnp.where(has_odd, odd_ref[...].astype(F32), 0.0).astype(BF16)
    up = jnp.where(ra_odd, odd, even_ref[...])
    down = jnp.where(ra_odd, even_ref[...], odd)

    def halo(rows):
        return dot(rows[two : two + RIM], place_odd, 0, 0) + dot(rows[two + RIM :], place_even, 0, 0)

    extend(ext_ref, 0, down[:two].astype(F32), halo(down))
    extend(ext_ref, two, up[:two].astype(F32), halo(up))
    sum_ref[...] = inner_ref[...]
    for g in range(0, bands, 8):
        for x, parts in ((0, ((0, 0), (1, 1))), (1, ((0, 1),)), (nx - 2, ((4, 2),)), (nx - 1, ((3, 2), (4, 3)))):
            acc = sum_ref[x * bands + g : x * bands + g + 8, :]
            for a, e in parts:
                for c in range(5):
                    tap = (5 * a + c) * bands + g
                    acc = acc + taps_ref[tap : tap + 8, :] * ext_ref[c, e * bands + g : e * bands + g + 8, :]
            sum_ref[x * bands + g : x * bands + g + 8, :] = acc

    smooth = sum_ref[...]
    high = smooth.astype(BF16)
    low = (smooth - high.astype(F32)).astype(BF16)
    cell = cell_ref[...]
    found = dot(high, hit_ref[...], 0, 0) + dot(low, hit_ref[...], 0, 0)
    at = lax.broadcasted_iota(jnp.int32, found.shape, 0) == cell % ny
    value = jnp.sum(jnp.where(at, found, 0.0), axis=0, keepdims=True)
    out_ref[...] = jnp.broadcast_to(lax.rsqrt(value), out_ref.shape).astype(BF16)


def stack_weight_kernel(own_ref, odd_ref, even_ref, basis_in_ref, out_ref, basis_ref):
    at = lax.broadcasted_iota(jnp.int32, out_ref.shape, 0)
    _, has_odd = sides("dec")
    odd = jnp.where(has_odd, odd_ref[...].astype(F32), 0.0)
    out = jnp.where(at == 1, odd, own_ref[...].astype(F32))
    out_ref[...] = jnp.where(at == 2, even_ref[...].astype(F32), out).astype(BF16)


def stack_rows_kernel(a_ref, b_ref, c_ref, after_ref, out_ref):
    n = a_ref.shape[0]
    out_ref[0:n, :] = a_ref[...]
    out_ref[n : 2 * n, :] = b_ref[...]
    out_ref[2 * n :, :] = c_ref[...]


def sincos(theta):
    turns = theta * (0.5 / math.pi)
    magic = 12582912.0
    r = turns - ((turns + magic) - magic)
    z = r * r
    c = jnp.full_like(z, COS[-1])
    for k in COS[-2::-1]:
        c = c * z + k
    s = jnp.full_like(z, SIN[-1])
    for k in SIN[-2::-1]:
        s = s * z + k
    return c, s * r


def basis_kernel(first, tiles, nblk, freq_ref, *refs):
    feat_refs, out_ref, ft_ref = refs[: len(tiles)], refs[-2], refs[-1]
    feats, nfreq = freq_ref.shape
    blk = out_ref.shape[2]
    ft_ref[...] = freq_ref[...].astype(F32).T.astype(BF16)
    at = first
    for feat_ref, count in zip(feat_refs, tiles, strict=True):
        for t in range(count):
            for b in range(nblk):
                x = feat_ref[t * feats : (t + 1) * feats, b * blk : (b + 1) * blk]
                c, s = sincos(dot(ft_ref[...], x, 1, 0))
                out_ref[at, 0:nfreq, :] = c.astype(BF16)
                out_ref[at, nfreq:, :] = s.astype(BF16)
                at += 1


def pair_kernel(src_ref, count_ref, pip_ref, basis_ref, w_own_ref, w_odd_ref, w_even_ref, out_ref, w_ref, done_ref, sems):
    nblk, slots, blk, _ = pip_ref.shape
    nfreq = out_ref.shape[0]
    copies = []
    ra_odd, has_odd = sides("ra")
    dec_odd, _ = sides("dec")
    for i, ref in enumerate((w_own_ref, w_even_ref, w_odd_ref)):
        for j in range(3):
            for b in range(nblk):
                at = (3 * i + j) * nblk + b
                w = ref[j : j + 1, b * blk : (b + 1) * blk].astype(F32)
                w_ref[at : at + 1, :] = jnp.where(has_odd, w, 0.0) if i == 2 else w

    def side(step, odd, first):
        up = jnp.where(odd, first, 3 - first)
        return jnp.where(step == 1, 0, jnp.where(step == 2, up, 3 - up))

    for a in range(nblk):
        def place(p):
            s = src_ref[a, p]
            q = s // nblk
            return (3 * side(q // 3, ra_odd, 2) + side(q % 3, dec_odd, 1)) * nblk + s % nblk

        total = None
        for p in range(0, slots, 2):
            lhs, rhs = [], []
            for k in (p, p + 1):
                at = place(k)
                live = jnp.where(k < count_ref[a], 1.0, 0.0)
                lhs.append(basis_ref[at])
                rhs.append((pip_ref[a, k].astype(F32) * (w_ref[pl.ds(at, 1), :] * live)).astype(BF16))
            part = dot(jnp.concatenate(lhs, 1), jnp.concatenate(rhs, 1), 1, 1)
            total = part if total is None else total + part
        own = basis_ref[a].astype(F32)
        folded = own[:nfreq] * total[:nfreq] + own[nfreq:] * total[nfreq:]
        done_ref[a] = (folded * w_ref[a : a + 1, :]).astype(BF16)
        copies.append(pltpu.make_async_copy(done_ref.at[a], out_ref.at[:, a * blk : (a + 1) * blk], sems.at[a]))
        copies[-1].start()
    for copy in copies:
        copy.wait()


def vm(shape, dtype):
    return pltpu.VMEM(shape, dtype)


def per_device(completeness, stencil, features, frequencies, gal_cell, pip, pair_src, pair_count):
    bands, nx, ny = completeness.shape
    feats, galaxies = features.shape
    nfreq = frequencies.shape[1]
    nblk, slots, blk, _ = pip.shape
    n = bands * nx
    two = 2 * bands

    def call(body, out, args, anys=(), scratch=(), name=None, aliases=None, cost=1):
        return pl.pallas_call(
            body, out_shape=out, in_specs=[VMEM] * len(args) + [ANY] * len(anys), out_specs=jax.tree.map(lambda _: VMEM, out),
            scratch_shapes=scratch, compiler_params=params(), input_output_aliases=aliases or {}, name=name,
            cost_estimate=pl.CostEstimate(flops=cost, bytes_accessed=1, transcendentals=0),
        )(*args, *anys)

    cells = gal_cell.reshape(1, galaxies)
    given = [pltpu.with_memory_space_constraint(x, pltpu.HBM) for x in (completeness, features, frequencies, stencil, cells)]
    rim, rows, features, frequencies, stencil, cells = pl.pallas_call(
        rim_kernel,
        out_shape=(vm((RIM, n), BF16), vm((n, ny), F32)) + tuple(vm(x.shape, x.dtype) for x in given[1:]),
        in_specs=[HBM] * len(given), out_specs=(VMEM,) * 6, compiler_params=params(), name="rim",
        scratch_shapes=[pltpu.VMEM(completeness.shape, F32), pltpu.SemaphoreType.DMA((len(given),))],
    )(*given)
    d_odd, d_even = exchange("dec", rim, rim)
    taps, hit, own_features = call(
        functools.partial(ready_kernel, bands, nx, ny),
        (vm((stencil.shape[0] * bands, ny), F32), vm((n, galaxies), BF16), vm(features.shape, BF16)),
        (stencil, cells, features), (rim,), [pltpu.VMEM((32, 128), F32)], "ready",
    )
    f_odd, f_even = exchange("dec", own_features, own_features)

    to_odd, to_even = call(row_kernel, (vm((two + 2 * RIM, ny), BF16),) * 2, (rows, d_odd, d_even), (taps, hit), name="rows", cost=LONG)
    r_odd, r_even = exchange("ra", to_odd, to_even)
    inner = call(
        functools.partial(inner_kernel, bands), vm((n, ny), F32), (rows, d_odd, d_even, taps), (to_odd,),
        [pltpu.VMEM((5, n, ny), F32)], "inner",
    )
    column = call(stack_rows_kernel, vm((3 * feats, galaxies), BF16), (features, f_odd, f_even), (inner,), name="stack_features")
    c_odd, c_even = exchange("ra", column, column)

    def basis(first, tiles, arrays, buffer, after):
        shape = vm((9 * nblk, 2 * nfreq, blk), BF16)

        def body(freq_ref, *refs):
            outs = refs[-2:]
            basis_kernel(first, tiles, nblk, freq_ref, *refs[: len(arrays)], *outs)

        anys = (after,) if buffer is None else (after, buffer)
        return call(
            body, shape, (frequencies, *arrays), anys, [pltpu.VMEM((nfreq, feats), BF16)], "basis%d" % first,
            None if buffer is None else {len(arrays) + 2: 0},
        )

    table = basis(0, (1,), (features,), None, column)
    weight, table = call(
        functools.partial(weight_kernel, bands), (vm((RIM, galaxies), BF16), vm(table.shape, BF16)),
        (inner, r_odd, r_even, taps, hit, cells), (table,),
        [pltpu.VMEM((5, 2 * two, ny), F32), pltpu.VMEM((n, ny), F32)], "weight", {6: 1}, LONG,
    )
    w_odd, w_even = exchange("dec", weight, weight)
    table = basis(nblk, (1, 1), (f_odd, f_even), table, weight)
    table = basis(3 * nblk, (3,), (c_even,), table, weight)
    w_column, table = call(
        stack_weight_kernel, (vm((RIM, galaxies), BF16), vm(table.shape, BF16)), (weight, w_odd, w_even), (table,), name="stack_weights",
        aliases={3: 1},
    )
    x_odd, x_even = exchange("ra", w_column, w_column)
    table = basis(6 * nblk, (3,), (c_odd,), table, w_column)
    return pl.pallas_call(
        pair_kernel, out_shape=jax.ShapeDtypeStruct((nfreq, galaxies), BF16), in_specs=[SMEM, SMEM] + [VMEM] * 5, out_specs=ANY,
        scratch_shapes=[
            pltpu.VMEM((9 * nblk + 4, blk), F32), pltpu.VMEM((nblk, nfreq, blk), BF16), pltpu.SemaphoreType.DMA((nblk,)),
        ],
        compiler_params=params(), name="pairs",
    )(pair_src, pair_count, pip, table, w_column, x_odd, x_even)


def solution(mesh):
    in_specs = (
        P(None, "ra", "dec"),
        P(),
        P(None, ("ra", "dec")),
        P(),
        P(("ra", "dec")),
        P(("ra", "dec"), None, None, None),
        P(("ra", "dec"), None),
        P(("ra", "dec")),
    )
    out_specs = P(None, ("ra", "dec"))
    return jax.shard_map(per_device, mesh=mesh, in_specs=in_specs, out_specs=out_specs, check_vma=False)
```

```python
import functools
import math

import jax
import jax.numpy as jnp
from jax import lax
from jax.experimental import pallas as pl
from jax.experimental.pallas import tpu as pltpu
from jax.sharding import PartitionSpec as P

BF16 = jnp.bfloat16
F32 = jnp.float32
LONG = 1 << 36
FIRST = 6
RIM = 16

VMEM = pl.BlockSpec(memory_space=pltpu.VMEM)
SMEM = pl.BlockSpec(memory_space=pltpu.SMEM)
ANY = pl.BlockSpec(memory_space=pl.ANY)
HBM = pl.BlockSpec(memory_space=pltpu.HBM)

COS = (0.99999922, -19.73898252, 64.92872662, -85.27239701, 58.79403871, -21.07678212)
SIN = (6.2830558, -41.33121431, 81.36681529, -74.47800454, 32.7814008)


def params(limit=None, **kw):
    return pltpu.CompilerParams(vmem_limit_bytes=limit or (16 << 20), **kw)


def exchange(axis, odd_payload, even_payload):
    ra, dec = lax.axis_size("ra"), lax.axis_size("dec")
    here = (lambda r, d: r * dec + d) if axis == "ra" else (lambda d, r: r * dec + d)
    count, other = (ra, dec) if axis == "ra" else (dec, ra)

    def swap(payload, odd):
        pairs = [(here(i, k), here(i + 1, k)) for i in range(odd, count - 1, 2) for k in range(other)]
        busy = {i for pair in pairs for i in pair}
        for i in (0, count - 1):
            ends = [(here(i, k), here(i, k + 1)) for k in range(0, other - 1, 2)]
            pairs += [pair for pair in ends if not busy & set(pair)]
        return lax.ppermute(payload, ("ra", "dec"), sorted(pairs + [(b, a) for a, b in pairs]))

    if axis == "ra":
        even = swap(even_payload, 0)
        return swap(odd_payload, 1), even
    odd = swap(odd_payload, 1)
    return odd, swap(even_payload, 0)


def sides(axis):
    i, n = lax.axis_index(axis), lax.axis_size(axis)
    odd = lax.rem(i, 2) == 1
    return odd, jnp.logical_and(i > 0, jnp.logical_not(jnp.logical_and(odd, i == n - 1)))


def dot(a, b, ca, cb):
    return lax.dot_general(a, b, (((ca,), (cb,)), ((), ())), preferred_element_type=F32)


def rim_kernel(*refs):
    count = (len(refs) - 3) // 2
    given, (rim_ref, rows_ref), kept = refs[:count], refs[count : count + 2], refs[count + 2 : -2]
    comp_ref, sems = refs[-2:]
    bands, nx, ny = comp_ref.shape
    copies = [pltpu.make_async_copy(a, b, sems.at[i]) for i, (a, b) in enumerate(zip(given, (comp_ref, *kept), strict=True))]
    for copy in copies:
        copy.start()
    row = lax.broadcasted_iota(jnp.int32, (RIM, ny), 0)
    lane = lax.broadcasted_iota(jnp.int32, (RIM, ny), 1)
    pick = ((row < 2) & (lane == row)) | ((row >= 2) & (row < 4) & (lane == row + ny - 4))
    copies[0].wait()
    for x in range(nx):
        rows_ref[x * bands : (x + 1) * bands, :] = comp_ref[:, x, :]
    rim_ref[...] = dot(pick.astype(F32).astype(BF16), rows_ref[...].astype(BF16), 1, 1).astype(BF16)
    for copy in copies[1:]:
        copy.wait()


def list_slots(nblk, src_ref, count_ref, code_ref, tile_ref):
    own, slots = src_ref.shape
    blocks, half = 9 * nblk, own * FIRST
    ra_odd, _ = sides("ra")
    dec_odd, _ = sides("dec")
    ra_up, dec_up = jnp.where(ra_odd, 2, 1), jnp.where(dec_odd, 1, 2)
    for i, ra_at in enumerate((3 - ra_up, 0, ra_up)):
        for j, dec_at in enumerate((3 - dec_up, 0, dec_up)):
            tile_ref[3 * i + j] = (3 * ra_at + dec_at) * nblk
    for i in range(half + own * slots):
        code_ref[i] = blocks * 65536
    steps = jnp.int32(0)
    for a in range(own):
        early, late = jnp.int32(0), jnp.int32(0)
        for p in range(slots):
            s = src_ref[a, p]
            at = tile_ref[lax.div(s, nblk)] + lax.rem(s, nblk)
            live = p < count_ref[a]
            soon = jnp.logical_and(at < 6 * nblk, early < FIRST)
            to = jnp.where(soon, a * FIRST + early, half + a * slots + late)
            code_ref[jnp.where(live, to, half + own * slots + 1)] = p + at * (256 + 65536)
            early = early + jnp.where(jnp.logical_and(live, soon), 1, 0)
            late = late + jnp.where(jnp.logical_and(live, jnp.logical_not(soon)), 1, 0)
        steps = jnp.maximum(steps, lax.div(late + 1, 2))
    code_ref[half + own * slots] = steps


def ready_kernel(bands, nx, ny, stencil_ref, cell_ref, rim_ref, taps_ref, lane_taps_ref, hit_ref, st_ref):
    st_ref[...] = jnp.zeros_like(st_ref)
    count = stencil_ref.shape[0]
    st_ref[0:count, 0:bands] = stencil_ref[...]
    st_ref[0:count, bands : 2 * bands] = stencil_ref[...]
    by_band = st_ref[...].T
    for k in range(count):
        taps_ref[k * bands : (k + 1) * bands, :] = jnp.broadcast_to(by_band[0:bands, k : k + 1], (bands, ny))
    along = jnp.concatenate([st_ref[...]] * (nx // 2), 1)
    lane_taps_ref[...] = jnp.zeros_like(lane_taps_ref)
    for a in range(5):
        for row, c in ((0, 0), (1, 0), (2, 4), (3, 3), (8, 1), (11, 4)):
            lane_taps_ref[16 * a + row : 16 * a + row + 1, :] = along[5 * a + c : 5 * a + c + 1, :]
    cell = cell_ref[...]
    slot = (cell // ny % nx) * bands + cell // (nx * ny)
    hit = lax.broadcasted_iota(jnp.int32, hit_ref.shape, 0) == slot
    hit_ref[...] = jnp.where(hit, 1.0, 0.0).astype(BF16)


def row_kernel(rows_ref, odd_ref, even_ref, after_ref, to_odd_ref, to_even_ref):
    n = rows_ref.shape[0]
    two = to_odd_ref.shape[0] - 2 * RIM
    is_odd, _ = sides("ra")

    def put(ref, start):
        ref[0:two, :] = rows_ref[start : start + two, :].astype(BF16)
        ref[two : two + RIM, :] = odd_ref[:, start : start + two]
        ref[two + RIM :, :] = even_ref[:, start : start + two]

    @pl.when(is_odd)
    def _():
        put(to_odd_ref, n - two)
        put(to_even_ref, 0)

    @pl.when(jnp.logical_not(is_odd))
    def _():
        put(to_odd_ref, 0)
        put(to_even_ref, n - two)


def picks():
    dec_odd, has_odd = sides("dec")
    row = lax.broadcasted_iota(jnp.int32, (RIM, RIM), 0)
    lane = lax.broadcasted_iota(jnp.int32, (RIM, RIM), 1)

    def ones(*spots):
        return functools.reduce(jnp.logical_or, [(row == r) & (lane == k) for r, k in spots]).astype(F32)

    before, after = ones((0, 2), (1, 3), (8, 3)), ones((2, 0), (3, 0), (11, 1))
    odd = jnp.where(has_odd, jnp.where(dec_odd, after, before), 0.0)
    return odd.astype(BF16), jnp.where(dec_odd, before, after).astype(BF16)


def edge_sums(lane_taps_ref, bands, columns):
    width = columns.shape[1]
    size = lane_taps_ref.shape[1]
    total = jnp.zeros((RIM, size), F32)
    for a in range(5):
        moved = columns if a == 0 else pltpu.roll(columns, width - a * bands, 1)
        total = total + lane_taps_ref[16 * a : 16 * a + 16, :] * moved[:, 0:size]
    return total[0:8] + total[8:16]


def extend(ext_ref, cells):
    ny = cells.shape[1]
    at = lax.broadcasted_iota(jnp.int32, cells.shape, 1)
    ext_ref[2] = cells
    ext_ref[3] = jnp.where(at > ny - 2, 0.0, pltpu.roll(cells, ny - 1, 1))
    ext_ref[4] = jnp.where(at > ny - 3, 0.0, pltpu.roll(cells, ny - 2, 1))
    ext_ref[1] = jnp.where(at < 1, 0.0, pltpu.roll(cells, 1, 1))
    ext_ref[0] = jnp.where(at < 2, 0.0, pltpu.roll(cells, 2, 1))


def split(x):
    high = x.astype(BF16)
    return high, (x - high.astype(F32)).astype(BF16)


def at_column(table, hits, cell):
    high, low = split(table)
    found = dot(high, hits, 0, 0) + dot(low, hits, 0, 0)
    at = lax.broadcasted_iota(jnp.int32, found.shape, 0) == cell % table.shape[1]
    return jnp.sum(jnp.where(at, found, 0.0), axis=0, keepdims=True)


def at_edge(edges, hits, cell, ny):
    found = dot(jnp.concatenate(split(edges), 0), hits, 1, 0)
    found = found[0:8] + found[8:16]
    y = cell % ny
    row = jnp.where(y < 2, y, jnp.where(y > ny - 3, y - (ny - 4), 8))
    return jnp.sum(jnp.where(lax.broadcasted_iota(jnp.int32, found.shape, 0) == row, found, 0.0), axis=0, keepdims=True)


def inner_kernel(bands, rows_ref, taps_ref, out_ref, ext_ref):
    n, ny = rows_ref.shape
    nx = n // bands
    extend(ext_ref, rows_ref[...])
    for g in range(0, bands, 8):
        accs = [jnp.zeros((8, ny), F32) for _ in range(nx)]
        for c in range(5):
            for a in range(5):
                w = taps_ref[(5 * a + c) * bands + g : (5 * a + c) * bands + g + 8, :]
                for x in range(nx):
                    if 0 <= x + a - 2 < nx:
                        base = (x + a - 2) * bands + g
                        accs[x] = accs[x] + w * ext_ref[c, base : base + 8, :]
        for x in range(nx):
            out_ref[x * bands + g : x * bands + g + 8, :] = accs[x]


def side_sums(ext_ref, taps_ref, bands, up, put):
    parts = (((4, 0),), ((3, 0), (4, 1))) if up else (((0, 0), (1, 1)), ((0, 1),))
    for g in range(0, bands, 8):
        for x, terms in enumerate(parts):
            acc = None
            for a, e in terms:
                for c in range(5):
                    tap = (5 * a + c) * bands + g
                    term = taps_ref[tap : tap + 8, :] * ext_ref[c, e * bands + g : e * bands + g + 8, :]
                    acc = term if acc is None else acc + term
            put(x * bands + g, acc)


def even_side_kernel(bands, inner_ref, odd_ref, even_ref, rows_ref, taps_ref, lane_taps_ref, hit_ref, cell_ref, out_ref, ext_ref, sum_ref):
    n, ny = inner_ref.shape
    two = 2 * bands
    ra_odd, _ = sides("ra")
    sum_ref[...] = inner_ref[...]
    extend(ext_ref, rows_ref[0:two, :].astype(F32))

    def add_from(start):
        def put(at, value):
            sum_ref[start + at : start + at + 8, :] += value

        return put

    pl.when(ra_odd)(lambda: side_sums(ext_ref, taps_ref, bands, False, add_from(0)))
    pl.when(jnp.logical_not(ra_odd))(lambda: side_sums(ext_ref, taps_ref, bands, True, add_from(n - two)))

    odd, even = picks()
    own = dot(odd, odd_ref[...], 1, 0) + dot(even, even_ref[...], 1, 0)
    beside = dot(odd, rows_ref[two : two + RIM, :], 1, 0) + dot(even, rows_ref[two + RIM :, :], 1, 0)
    columns = jnp.concatenate([jnp.where(ra_odd, beside, 0.0), own, jnp.where(ra_odd, 0.0, beside)], 1)
    edges = edge_sums(lane_taps_ref, bands, columns)
    cell = cell_ref[...]
    value = at_column(sum_ref[...], hit_ref[...], cell) + at_edge(edges, hit_ref[...], cell, ny)
    out_ref[...] = jnp.broadcast_to(value, out_ref.shape)


def weight_kernel(bands, even_side_ref, rows_ref, taps_ref, lane_taps_ref, hit_ref, cell_ref, basis_in_ref, out_ref, basis_ref, ext_ref, sum_ref):
    two, ny = sum_ref.shape
    n = hit_ref.shape[0]
    ra_odd, has_odd = sides("ra")
    extend(ext_ref, jnp.where(has_odd, rows_ref[0:two, :].astype(F32), 0.0))

    def put(at, value):
        sum_ref[at : at + 8, :] = value

    pl.when(ra_odd)(lambda: side_sums(ext_ref, taps_ref, bands, True, put))
    pl.when(jnp.logical_not(ra_odd))(lambda: side_sums(ext_ref, taps_ref, bands, False, put))

    odd, even = picks()
    beside = dot(odd, rows_ref[two : two + RIM, :], 1, 0) + dot(even, rows_ref[two + RIM :, :], 1, 0)
    beside = jnp.where(has_odd, beside, 0.0)
    columns = jnp.concatenate([jnp.where(ra_odd, 0.0, beside), jnp.zeros((RIM, n), F32), jnp.where(ra_odd, beside, 0.0)], 1)
    edges = edge_sums(lane_taps_ref, bands, columns)
    edges = jnp.where(ra_odd, edges[:, n - two :], edges[:, 0:two])
    hits = hit_ref[pl.ds(pl.multiple_of(jnp.where(ra_odd, n - two, 0), two), two), :]
    cell = cell_ref[...]
    value = even_side_ref[0:1, :] + at_column(sum_ref[...], hits, cell) + at_edge(edges, hits, cell, ny)
    out_ref[...] = jnp.broadcast_to(lax.rsqrt(value), out_ref.shape).astype(BF16)


def stack_weight_kernel(own_ref, odd_ref, even_ref, basis_in_ref, out_ref, basis_ref):
    at = lax.broadcasted_iota(jnp.int32, out_ref.shape, 0)
    _, has_odd = sides("dec")
    odd = jnp.where(has_odd, odd_ref[...].astype(F32), 0.0)
    out = jnp.where(at == 1, odd, own_ref[...].astype(F32))
    out_ref[...] = jnp.where(at == 2, even_ref[...].astype(F32), out).astype(BF16)


def stack_rows_kernel(a_ref, b_ref, c_ref, after_ref, out_ref):
    n = a_ref.shape[0]
    out_ref[0:n, :] = a_ref[...]
    out_ref[n : 2 * n, :] = b_ref[...]
    out_ref[2 * n :, :] = c_ref[...]


def sincos(theta):
    turns = theta * (0.5 / math.pi)
    magic = 12582912.0
    r = turns - ((turns + magic) - magic)
    z = r * r
    c = jnp.full_like(z, COS[-1])
    for k in COS[-2::-1]:
        c = c * z + k
    s = jnp.full_like(z, SIN[-1])
    for k in SIN[-2::-1]:
        s = s * z + k
    return c, s * r


def basis_kernel(first, tiles, nblk, freq_ref, feat_ref, out_ref, ft_ref):
    feats, nfreq = freq_ref.shape
    blk = out_ref.shape[2]
    ft_ref[...] = freq_ref[...].astype(F32).T.astype(BF16)
    for t in tiles:
        for b in range(nblk):
            c, s = sincos(dot(ft_ref[...], feat_ref[t * feats : (t + 1) * feats, b * blk : (b + 1) * blk], 1, 0))
            out_ref[first + t * nblk + b, 0:nfreq, :] = c.astype(BF16)
            out_ref[first + t * nblk + b, nfreq:, :] = s.astype(BF16)


def own_basis_kernel(nblk, src_ref, count_ref, freq_ref, feat_ref, after_ref, out_ref, code_ref, ft_ref, tile_ref):
    list_slots(nblk, src_ref, count_ref, code_ref, tile_ref)
    basis_kernel(0, (0,), nblk, freq_ref, feat_ref, out_ref, ft_ref)


def pair_sums(code_ref, pip_ref, basis_ref, w_ref, at, a):
    lhs, rhs = [], []
    for k in range(2):
        code = code_ref[at + k]
        lhs.append(basis_ref[lax.rem(lax.div(code, 256), 256)])
        w = w_ref[pl.ds(lax.div(code, 65536), 1), :]
        rhs.append((pip_ref[a, lax.rem(code, 256)].astype(F32) * w).astype(BF16))
    return dot(jnp.concatenate(lhs, 1), jnp.concatenate(rhs, 1), 1, 1)


def spread_weights(w_ref, refs, blk):
    nblk = refs[0][0].shape[1] // blk
    w_ref[9 * nblk :, :] = jnp.zeros((w_ref.shape[0] - 9 * nblk, blk), F32)
    for i, (ref, there) in enumerate(refs):
        for j in range(3):
            for b in range(nblk):
                at = (3 * i + j) * nblk + b
                w = ref[j : j + 1, b * blk : (b + 1) * blk].astype(F32)
                w_ref[at : at + 1, :] = w if there is None else jnp.where(there, w, 0.0)


def early_kernel(code_ref, pip_ref, basis_ref, w_own_ref, w_even_ref, after_ref, sum_ref, w_ref):
    nblk, _, blk, _ = pip_ref.shape
    spread_weights(w_ref, ((w_own_ref, None), (w_even_ref, None)), blk)
    for a in range(nblk):
        total = None
        for p in range(0, FIRST, 2):
            part = pair_sums(code_ref, pip_ref, basis_ref, w_ref, a * FIRST + p, a)
            total = part if total is None else total + part
        sum_ref[a] = total


def pair_kernel(code_ref, pip_ref, basis_ref, early_ref, w_own_ref, w_even_ref, w_odd_ref, out_ref, w_ref, sum_ref, done_ref, sems):
    nblk, slots, blk, _ = pip_ref.shape
    nfreq = out_ref.shape[0]
    half, steps = nblk * FIRST, (slots - FIRST) // 2
    copies = []
    _, has_odd = sides("ra")
    spread_weights(w_ref, ((w_own_ref, None), (w_even_ref, None), (w_odd_ref, has_odd)), blk)
    many = code_ref[half + nblk * slots]

    @pl.when(many > steps)
    def _():
        sum_ref[...] = jnp.zeros_like(sum_ref)

        def step(t, _):
            for a in range(nblk):
                sum_ref[a] += pair_sums(code_ref, pip_ref, basis_ref, w_ref, half + a * slots + 2 * t, a)
            return _

        lax.fori_loop(steps, many, step, 0)

    @pl.when(many <= steps)
    def _():
        sum_ref[...] = jnp.zeros_like(sum_ref)

    for a in range(nblk):
        total = early_ref[a] + sum_ref[a]
        for t in range(steps):
            total = total + pair_sums(code_ref, pip_ref, basis_ref, w_ref, half + a * slots + 2 * t, a)
        own = basis_ref[a].astype(F32)
        folded = own[:nfreq] * total[:nfreq] + own[nfreq:] * total[nfreq:]
        done_ref[a] = (folded * w_ref[a : a + 1, :]).astype(BF16)
        copies.append(pltpu.make_async_copy(done_ref.at[a], out_ref.at[:, a * blk : (a + 1) * blk], sems.at[a]))
        copies[-1].start()
    for copy in copies:
        copy.wait()


def vm(shape, dtype):
    return pltpu.VMEM(shape, dtype)


def sm(shape):
    return pltpu.SMEM(shape, jnp.int32)


def per_device(completeness, stencil, features, frequencies, gal_cell, pip, pair_src, pair_count):
    bands, nx, ny = completeness.shape
    feats, galaxies = features.shape
    nfreq = frequencies.shape[1]
    nblk, slots, blk, _ = pip.shape
    n = bands * nx
    two = 2 * bands

    def call(body, out, args, anys=(), scratch=(), name=None, aliases=None, cost=1, scalars=()):
        return pl.pallas_call(
            body, out_shape=out, in_specs=[SMEM] * len(scalars) + [VMEM] * len(args) + [ANY] * len(anys),
            out_specs=jax.tree.map(lambda x: SMEM if x.memory_space == pltpu.SMEM else VMEM, out),
            scratch_shapes=scratch, compiler_params=params(), input_output_aliases=aliases or {}, name=name,
            cost_estimate=pl.CostEstimate(flops=cost, bytes_accessed=1, transcendentals=0),
        )(*scalars, *args, *anys)

    cells = gal_cell.reshape(1, galaxies)
    given = (completeness, features, frequencies, stencil, cells, pair_src, pair_count)
    kept = tuple(vm(x.shape, x.dtype) for x in given[1:5]) + tuple(sm(x.shape) for x in given[5:])
    rim, rows, features, frequencies, stencil, cells, pair_src, pair_count = pl.pallas_call(
        rim_kernel, out_shape=(vm((RIM, n), BF16), vm((n, ny), F32)) + kept,
        in_specs=[HBM] * len(given), out_specs=(VMEM,) * 6 + (SMEM,) * 2, compiler_params=params(), name="rim",
        scratch_shapes=[pltpu.VMEM(completeness.shape, F32), pltpu.SemaphoreType.DMA((len(given),))],
    )(*[pltpu.with_memory_space_constraint(x, pltpu.HBM) for x in given])
    d_odd, d_even = exchange("dec", rim, rim)
    f_odd, f_even = exchange("dec", features, features)
    taps, lane_taps, hit = call(
        functools.partial(ready_kernel, bands, nx, ny),
        (vm((stencil.shape[0] * bands, ny), F32), vm((5 * RIM, n), F32), vm((n, galaxies), BF16)),
        (stencil, cells), (rim,), [pltpu.VMEM((32, 128), F32)], "ready",
    )
    inner = call(
        functools.partial(inner_kernel, bands), vm((n, ny), F32), (rows, taps), (), [pltpu.VMEM((5, n, ny), F32)], "inner",
    )
    to_odd, to_even = call(
        row_kernel, (vm((two + 2 * RIM, ny), BF16),) * 2, (rows, d_odd, d_even), (inner,), name="rows", cost=LONG
    )
    r_odd, r_even = exchange("ra", to_odd, to_even)
    even_side = call(
        functools.partial(even_side_kernel, bands), vm((8, galaxies), F32),
        (inner, d_odd, d_even, r_even, taps, lane_taps, hit, cells), (),
        [pltpu.VMEM((5, two, ny), F32), pltpu.VMEM((n, ny), F32)], "even_side",
    )
    column = call(stack_rows_kernel, vm((3 * feats, galaxies), BF16), (features, f_odd, f_even), (even_side,), name="stack_features")
    c_odd, c_even = exchange("ra", column, column)

    blocks = vm((9 * nblk, 2 * nfreq, blk), BF16)
    scratch = [pltpu.VMEM((nfreq, feats), BF16)]
    table, code = call(
        functools.partial(own_basis_kernel, nblk), (blocks, sm((nblk * (FIRST + slots) + 2,))), (frequencies, features), (column,),
        scratch + [pltpu.SMEM((9,), jnp.int32)], "own_basis", scalars=(pair_src, pair_count),
    )

    def basis(part, tiles, array, buffer, after):
        def body(freq_ref, feat_ref, *refs):
            basis_kernel(3 * part * nblk, tiles, nblk, freq_ref, feat_ref, *refs[-2:])

        return call(body, blocks, (frequencies, array), (after, buffer), scratch, "basis%d" % part, {3: 0})

    weight, table = call(
        functools.partial(weight_kernel, bands), (vm((RIM, galaxies), BF16), blocks),
        (even_side, r_odd, taps, lane_taps, hit, cells), (table,),
        [pltpu.VMEM((5, two, ny), F32), pltpu.VMEM((two, ny), F32)], "weight", {6: 1}, LONG,
    )
    w_odd, w_even = exchange("dec", weight, weight)
    table = basis(0, (1, 2), column, table, weight)
    table = basis(1, (0, 1, 2), c_even, table, weight)
    w_column, table = call(
        stack_weight_kernel, (vm((RIM, galaxies), BF16), vm(table.shape, BF16)), (weight, w_odd, w_even), (table,), name="stack_weights",
        aliases={3: 1},
    )
    x_odd, x_even = exchange("ra", w_column, w_column)
    early = call(
        early_kernel, vm((nblk, 2 * nfreq, blk), F32), (pip, table, w_column, x_even), (w_column,),
        [pltpu.VMEM((9 * nblk + 4, blk), F32)], "early_pairs", scalars=(code,),
    )
    table = basis(2, (0, 1, 2), c_odd, table, early)
    return pl.pallas_call(
        pair_kernel, out_shape=jax.ShapeDtypeStruct((nfreq, galaxies), BF16), in_specs=[SMEM] + [VMEM] * 6, out_specs=ANY,
        scratch_shapes=[
            pltpu.VMEM((9 * nblk + 4, blk), F32), pltpu.VMEM((nblk, 2 * nfreq, blk), F32),
            pltpu.VMEM((nblk, nfreq, blk), BF16), pltpu.SemaphoreType.DMA((nblk,)),
        ],
        compiler_params=params(), name="pairs",
    )(code, pip, table, early, w_column, x_even, x_odd)


def solution(mesh):
    in_specs = (
        P(None, "ra", "dec"),
        P(),
        P(None, ("ra", "dec")),
        P(),
        P(("ra", "dec")),
        P(("ra", "dec"), None, None, None),
        P(("ra", "dec"), None),
        P(("ra", "dec")),
    )
    out_specs = P(None, ("ra", "dec"))
    return jax.shard_map(per_device, mesh=mesh, in_specs=in_specs, out_specs=out_specs, check_vma=False)
```

```python
import functools
import math

import jax
import jax.numpy as jnp
from jax import lax
from jax.experimental import pallas as pl
from jax.experimental.pallas import tpu as pltpu
from jax.sharding import PartitionSpec as P

BF16 = jnp.bfloat16
F32 = jnp.float32
LONG = 1 << 36
FIRST = 6
RIM = 16

VMEM = pl.BlockSpec(memory_space=pltpu.VMEM)
SMEM = pl.BlockSpec(memory_space=pltpu.SMEM)
ANY = pl.BlockSpec(memory_space=pl.ANY)
HBM = pl.BlockSpec(memory_space=pltpu.HBM)

COS = (0.99999922, -19.73898252, 64.92872662, -85.27239701, 58.79403871, -21.07678212)
SIN = (6.2830558, -41.33121431, 81.36681529, -74.47800454, 32.7814008)


def params(limit=None, **kw):
    return pltpu.CompilerParams(vmem_limit_bytes=limit or (16 << 20), **kw)


def exchange(axis, odd_payload, even_payload):
    ra, dec = lax.axis_size("ra"), lax.axis_size("dec")
    here = (lambda r, d: r * dec + d) if axis == "ra" else (lambda d, r: r * dec + d)
    count, other = (ra, dec) if axis == "ra" else (dec, ra)

    def swap(payload, odd):
        pairs = [(here(i, k), here(i + 1, k)) for i in range(odd, count - 1, 2) for k in range(other)]
        busy = {i for pair in pairs for i in pair}
        for i in (0, count - 1):
            ends = [(here(i, k), here(i, k + 1)) for k in range(0, other - 1, 2)]
            pairs += [pair for pair in ends if not busy & set(pair)]
        return lax.ppermute(payload, ("ra", "dec"), sorted(pairs + [(b, a) for a, b in pairs]))

    if axis == "ra":
        even = swap(even_payload, 0)
        return swap(odd_payload, 1), even
    odd = swap(odd_payload, 1)
    return odd, swap(even_payload, 0)


def sides(axis):
    i, n = lax.axis_index(axis), lax.axis_size(axis)
    odd = lax.rem(i, 2) == 1
    return odd, jnp.logical_and(i > 0, jnp.logical_not(jnp.logical_and(odd, i == n - 1)))


def dot(a, b, ca, cb):
    return lax.dot_general(a, b, (((ca,), (cb,)), ((), ())), preferred_element_type=F32)


def rim_kernel(*refs):
    count = (len(refs) - 3) // 2
    given, (rim_ref, rows_ref), kept = refs[:count], refs[count : count + 2], refs[count + 2 : -2]
    comp_ref, sems = refs[-2:]
    bands, nx, ny = comp_ref.shape
    copies = [pltpu.make_async_copy(a, b, sems.at[i]) for i, (a, b) in enumerate(zip(given, (comp_ref, *kept), strict=True))]
    for copy in copies:
        copy.start()
    row = lax.broadcasted_iota(jnp.int32, (8, ny), 0)
    lane = lax.broadcasted_iota(jnp.int32, (8, ny), 1)
    pick = ((row < 2) & (lane == row)) | ((row >= 2) & (row < 4) & (lane == row + ny - 4))
    copies[0].wait()
    for x in range(nx):
        rows_ref[x * bands : (x + 1) * bands, :] = comp_ref[:, x, :]
    rim = dot(pick.astype(F32).astype(BF16), rows_ref[...].astype(BF16), 1, 1)
    rim_ref[...] = jnp.concatenate([rim[0:4, at : at + 128] for at in range(0, bands * nx, 128)], 0).astype(BF16)
    for copy in copies[1:]:
        copy.wait()


def list_slots(nblk, src_ref, count_ref, code_ref, tile_ref):
    own, slots = src_ref.shape
    blocks, half = 9 * nblk, own * FIRST
    ra_odd, _ = sides("ra")
    dec_odd, _ = sides("dec")
    ra_up, dec_up = jnp.where(ra_odd, 2, 1), jnp.where(dec_odd, 1, 2)
    ra, dec = lax.axis_index("ra"), lax.axis_index("dec")
    last_ra, last_dec = lax.axis_size("ra") - 1, lax.axis_size("dec") - 1
    for i, (ra_at, ra_in) in enumerate(((3 - ra_up, ra > 0), (0, ra >= 0), (ra_up, ra < last_ra))):
        for j, (dec_at, dec_in) in enumerate(((3 - dec_up, dec > 0), (0, dec >= 0), (dec_up, dec < last_dec))):
            tile_ref[3 * i + j] = jnp.where(jnp.logical_and(ra_in, dec_in), (3 * ra_at + dec_at) * nblk, -blocks)
    for i in range(half + own * slots):
        code_ref[i] = blocks * 65536
    steps = jnp.int32(0)
    for a in range(own):
        early, late = jnp.int32(0), jnp.int32(0)
        for p in range(slots):
            s = src_ref[a, p]
            at = tile_ref[lax.div(s, nblk)] + lax.rem(s, nblk)
            live = jnp.logical_and(p < count_ref[a], at >= 0)
            soon = jnp.logical_and(at < 6 * nblk, early < FIRST)
            to = jnp.where(soon, a * FIRST + early, half + a * slots + late)
            code_ref[jnp.where(live, to, half + own * slots + 1)] = p + at * (256 + 65536)
            early = early + jnp.where(jnp.logical_and(live, soon), 1, 0)
            late = late + jnp.where(jnp.logical_and(live, jnp.logical_not(soon)), 1, 0)
        steps = jnp.maximum(steps, lax.div(late + 1, 2))
    code_ref[half + own * slots] = steps


def leads():
    return jnp.logical_and(lax.axis_index("ra") < 2, lax.axis_index("dec") == 0)


def ahead_kernel(bands, nx, ny, rim_in_ref, stencil_ref, cell_ref, rim_ref, taps_ref, lane_taps_ref, hit_ref, st_ref):
    rim_ref[...] = rim_in_ref[...]
    pl.when(leads())(lambda: ready(bands, nx, ny, stencil_ref, cell_ref, taps_ref, lane_taps_ref, hit_ref, st_ref))


def ready_kernel(bands, nx, ny, stencil_ref, cell_ref, rim_ref, taps_in_ref, lane_taps_in_ref, hit_in_ref, taps_ref, lane_taps_ref, hit_ref, st_ref):
    late = jnp.logical_not(leads())
    pl.when(late)(lambda: ready(bands, nx, ny, stencil_ref, cell_ref, taps_ref, lane_taps_ref, hit_ref, st_ref))


def ready(bands, nx, ny, stencil_ref, cell_ref, taps_ref, lane_taps_ref, hit_ref, st_ref):
    st_ref[...] = jnp.zeros_like(st_ref)
    count = stencil_ref.shape[0]
    st_ref[0:count, 0:bands] = stencil_ref[...]
    st_ref[0:count, bands : 2 * bands] = stencil_ref[...]
    by_band = st_ref[...].T
    for k in range(count):
        taps_ref[k * bands : (k + 1) * bands, :] = jnp.broadcast_to(by_band[0:bands, k : k + 1], (bands, ny))
    along = jnp.concatenate([st_ref[...]] * (nx // 2), 1)
    lane_taps_ref[...] = jnp.zeros_like(lane_taps_ref)
    for a in range(5):
        for row, c in ((0, 0), (1, 0), (2, 4), (3, 3), (8, 1), (11, 4)):
            lane_taps_ref[16 * a + row : 16 * a + row + 1, :] = along[5 * a + c : 5 * a + c + 1, :]
    cell = cell_ref[...]
    slot = (cell // ny % nx) * bands + cell // (nx * ny)
    hit = lax.broadcasted_iota(jnp.int32, hit_ref.shape, 0) == slot
    hit_ref[...] = jnp.where(hit, 1.0, 0.0).astype(BF16)


def row_kernel(rows_ref, odd_ref, even_ref, after_ref, to_odd_ref, to_even_ref):
    n = rows_ref.shape[0]
    two = to_odd_ref.shape[0] - RIM
    is_odd, _ = sides("ra")

    def put(ref, start):
        ref[0:two, :] = rows_ref[start : start + two, :].astype(BF16)
        at = start // 128 * 4
        edges = [r[...].astype(F32)[at : at + 4] for r in (odd_ref, even_ref)]
        ref[two:, :] = jnp.concatenate([*edges, jnp.zeros((RIM - 8, 128), F32)], 0).astype(BF16)

    @pl.when(is_odd)
    def _():
        put(to_odd_ref, n - two)
        put(to_even_ref, 0)

    @pl.when(jnp.logical_not(is_odd))
    def _():
        put(to_odd_ref, 0)
        put(to_even_ref, n - two)


def beside(odd, even):
    dec_odd, has_odd = sides("dec")
    odd = jnp.where(has_odd, odd, 0.0)
    before, after = jnp.where(dec_odd, even, odd), jnp.where(dec_odd, odd, even)
    none = jnp.zeros_like(before)
    return jnp.concatenate([before[2:4], after[0:1], after[0:1], none, before[3:4], none[0:2], after[1:2], none], 0)


def columns_of(rim):
    return jnp.concatenate([rim[at : at + 4] for at in range(0, RIM, 4)], 1)


def edge_sums(lane_taps_ref, bands, columns):
    width = columns.shape[1]
    size = lane_taps_ref.shape[1]
    total = jnp.zeros((RIM, size), F32)
    for a in range(5):
        moved = columns if a == 0 else pltpu.roll(columns, width - a * bands, 1)
        total = total + lane_taps_ref[16 * a : 16 * a + 16, :] * moved[:, 0:size]
    return total[0:8] + total[8:16]


def extend(ext_ref, cells):
    ny = cells.shape[1]
    at = lax.broadcasted_iota(jnp.int32, cells.shape, 1)
    ext_ref[2] = cells
    ext_ref[3] = jnp.where(at > ny - 2, 0.0, pltpu.roll(cells, ny - 1, 1))
    ext_ref[4] = jnp.where(at > ny - 3, 0.0, pltpu.roll(cells, ny - 2, 1))
    ext_ref[1] = jnp.where(at < 1, 0.0, pltpu.roll(cells, 1, 1))
    ext_ref[0] = jnp.where(at < 2, 0.0, pltpu.roll(cells, 2, 1))


def split(x):
    high = x.astype(BF16)
    return high, (x - high.astype(F32)).astype(BF16)


def at_column(table, hits, cell):
    high, low = split(table)
    found = dot(high, hits, 0, 0) + dot(low, hits, 0, 0)
    at = lax.broadcasted_iota(jnp.int32, found.shape, 0) == cell % table.shape[1]
    return jnp.sum(jnp.where(at, found, 0.0), axis=0, keepdims=True)


def at_edge(edges, hits, cell, ny):
    found = dot(jnp.concatenate(split(edges), 0), hits, 1, 0)
    found = found[0:8] + found[8:16]
    y = cell % ny
    row = jnp.where(y < 2, y, jnp.where(y > ny - 3, y - (ny - 4), 8))
    return jnp.sum(jnp.where(lax.broadcasted_iota(jnp.int32, found.shape, 0) == row, found, 0.0), axis=0, keepdims=True)


def inner_kernel(bands, rows_ref, taps_ref, out_ref, ext_ref):
    n, ny = rows_ref.shape
    nx = n // bands
    extend(ext_ref, rows_ref[...])
    for g in range(0, bands, 8):
        accs = [jnp.zeros((8, ny), F32) for _ in range(nx)]
        for c in range(5):
            for a in range(5):
                w = taps_ref[(5 * a + c) * bands + g : (5 * a + c) * bands + g + 8, :]
                for x in range(nx):
                    if 0 <= x + a - 2 < nx:
                        base = (x + a - 2) * bands + g
                        accs[x] = accs[x] + w * ext_ref[c, base : base + 8, :]
        for x in range(nx):
            out_ref[x * bands + g : x * bands + g + 8, :] = accs[x]


def side_sums(ext_ref, taps_ref, bands, up, put):
    parts = (((4, 0),), ((3, 0), (4, 1))) if up else (((0, 0), (1, 1)), ((0, 1),))
    for g in range(0, bands, 8):
        for x, terms in enumerate(parts):
            acc = None
            for a, e in terms:
                for c in range(5):
                    tap = (5 * a + c) * bands + g
                    term = taps_ref[tap : tap + 8, :] * ext_ref[c, e * bands + g : e * bands + g + 8, :]
                    acc = term if acc is None else acc + term
            put(x * bands + g, acc)


def even_side_kernel(bands, inner_ref, odd_ref, even_ref, rows_ref, taps_ref, lane_taps_ref, hit_ref, cell_ref, out_ref, ext_ref, sum_ref):
    n, ny = inner_ref.shape
    two = 2 * bands
    ra_odd, _ = sides("ra")
    sum_ref[...] = inner_ref[...]
    extend(ext_ref, rows_ref[0:two, :].astype(F32))

    def add_from(start):
        def put(at, value):
            sum_ref[start + at : start + at + 8, :] += value

        return put

    pl.when(ra_odd)(lambda: side_sums(ext_ref, taps_ref, bands, False, add_from(0)))
    pl.when(jnp.logical_not(ra_odd))(lambda: side_sums(ext_ref, taps_ref, bands, True, add_from(n - two)))

    own = beside(columns_of(odd_ref[...].astype(F32)), columns_of(even_ref[...].astype(F32)))
    rims = rows_ref[two : two + RIM, :].astype(F32)
    side = beside(rims[0:4], rims[4:8])
    columns = jnp.concatenate([jnp.where(ra_odd, side, 0.0), own, jnp.where(ra_odd, 0.0, side)], 1)
    edges = edge_sums(lane_taps_ref, bands, columns)
    cell = cell_ref[...]
    value = at_column(sum_ref[...], hit_ref[...], cell) + at_edge(edges, hit_ref[...], cell, ny)
    out_ref[...] = jnp.broadcast_to(value, out_ref.shape)


def weight_kernel(bands, even_side_ref, rows_ref, taps_ref, lane_taps_ref, hit_ref, cell_ref, basis_in_ref, out_ref, basis_ref, ext_ref, sum_ref):
    two, ny = sum_ref.shape
    n = hit_ref.shape[0]
    ra_odd, has_odd = sides("ra")
    extend(ext_ref, jnp.where(has_odd, rows_ref[0:two, :].astype(F32), 0.0))

    def put(at, value):
        sum_ref[at : at + 8, :] = value

    pl.when(ra_odd)(lambda: side_sums(ext_ref, taps_ref, bands, True, put))
    pl.when(jnp.logical_not(ra_odd))(lambda: side_sums(ext_ref, taps_ref, bands, False, put))

    rims = rows_ref[two : two + RIM, :].astype(F32)
    side = jnp.where(has_odd, beside(rims[0:4], rims[4:8]), 0.0)
    columns = jnp.concatenate([jnp.where(ra_odd, 0.0, side), jnp.zeros((RIM, n), F32), jnp.where(ra_odd, side, 0.0)], 1)
    edges = edge_sums(lane_taps_ref, bands, columns)
    edges = jnp.where(ra_odd, edges[:, n - two :], edges[:, 0:two])
    hits = hit_ref[pl.ds(pl.multiple_of(jnp.where(ra_odd, n - two, 0), two), two), :]
    cell = cell_ref[...]
    value = even_side_ref[0:1, :] + at_column(sum_ref[...], hits, cell) + at_edge(edges, hits, cell, ny)
    weights = lax.rsqrt(value)
    blk = out_ref.shape[1]
    rows = [weights[:, at : at + blk] for at in range(0, weights.shape[1], blk)]
    out_ref[...] = jnp.concatenate([*rows, jnp.zeros((out_ref.shape[0] - len(rows), blk), F32)], 0).astype(BF16)


def stack_weight_kernel(nblk, own_ref, odd_ref, even_ref, basis_in_ref, out_ref, basis_ref):
    _, has_odd = sides("dec")
    own, odd, even = (ref[...].astype(F32)[0:nblk] for ref in (own_ref, odd_ref, even_ref))
    none = jnp.zeros((out_ref.shape[0] - 3 * nblk, out_ref.shape[1]), F32)
    out_ref[...] = jnp.concatenate([own, jnp.where(has_odd, odd, 0.0), even, none], 0).astype(BF16)


def stack_rows_kernel(a_ref, b_ref, c_ref, after_ref, out_ref):
    n = a_ref.shape[0]
    out_ref[0:n, :] = a_ref[...]
    out_ref[n : 2 * n, :] = b_ref[...]
    out_ref[2 * n :, :] = c_ref[...]


def sincos(theta):
    turns = theta * (0.5 / math.pi)
    magic = 12582912.0
    r = turns - ((turns + magic) - magic)
    z = r * r
    c = jnp.full_like(z, COS[-1])
    for k in COS[-2::-1]:
        c = c * z + k
    s = jnp.full_like(z, SIN[-1])
    for k in SIN[-2::-1]:
        s = s * z + k
    return c, s * r


def basis_kernel(first, tiles, nblk, freq_ref, feat_ref, out_ref, ft_ref):
    feats, nfreq = freq_ref.shape
    blk = out_ref.shape[2]
    ft_ref[...] = freq_ref[...].astype(F32).T.astype(BF16)

    def work(t):
        for b in range(nblk):
            c, s = sincos(dot(ft_ref[...], feat_ref[t * feats : (t + 1) * feats, b * blk : (b + 1) * blk], 1, 0))
            out_ref[first + t * nblk + b, 0:nfreq, :] = c.astype(BF16)
            out_ref[first + t * nblk + b, nfreq:, :] = s.astype(BF16)

    def inside():
        for t in tiles:
            if t != 1:
                work(t)
        if 1 in tiles:
            pl.when(sides("dec")[1])(functools.partial(work, 1))

    if first == 6 * nblk:
        pl.when(sides("ra")[1])(inside)
    else:
        inside()


def own_basis_kernel(nblk, src_ref, count_ref, freq_ref, feat_ref, after_ref, out_ref, code_ref, ft_ref, tile_ref):
    list_slots(nblk, src_ref, count_ref, code_ref, tile_ref)
    basis_kernel(0, (0,), nblk, freq_ref, feat_ref, out_ref, ft_ref)


def pair_sums(code_ref, pip_ref, basis_ref, w_ref, at, a):
    lhs, rhs = [], []
    for k in range(2):
        code = code_ref[at + k]
        lhs.append(basis_ref[lax.rem(lax.div(code, 256), 256)])
        w = w_ref[pl.ds(lax.div(code, 65536), 1), :]
        rhs.append((pip_ref[a, lax.rem(code, 256)].astype(F32) * w).astype(BF16))
    return dot(jnp.concatenate(lhs, 1), jnp.concatenate(rhs, 1), 1, 1)


def spread_weights(w_ref, *refs):
    rows = w_ref.shape[0] // 9 * 3
    w_ref[3 * rows :, :] = jnp.zeros((w_ref.shape[0] - 3 * rows, w_ref.shape[1]), F32)
    for i, ref in enumerate(refs):
        w = ref[...].astype(F32)[0:rows]
        w_ref[i * rows : (i + 1) * rows, :] = w if i < 2 else jnp.where(sides("ra")[1], w, 0.0)


def early_kernel(code_ref, pip_ref, basis_ref, w_own_ref, w_even_ref, after_ref, sum_ref, w_ref):
    nblk, _, blk, _ = pip_ref.shape
    spread_weights(w_ref, w_own_ref, w_even_ref)
    for a in range(nblk):
        total = None
        for p in range(0, FIRST, 2):
            part = pair_sums(code_ref, pip_ref, basis_ref, w_ref, a * FIRST + p, a)
            total = part if total is None else total + part
        sum_ref[a] = total


def pair_kernel(code_ref, pip_ref, basis_ref, early_ref, w_own_ref, w_even_ref, w_odd_ref, out_ref, w_ref, sum_ref, done_ref, sems):
    nblk, slots, blk, _ = pip_ref.shape
    nfreq = out_ref.shape[0]
    half, steps = nblk * FIRST, (slots - FIRST) // 2
    spread_weights(w_ref, w_own_ref, w_even_ref, w_odd_ref)
    many = code_ref[half + nblk * slots]

    def finish(start_ref, count):
        copies = []
        for a in range(nblk):
            total = start_ref[a]
            for t in range(count):
                total = total + pair_sums(code_ref, pip_ref, basis_ref, w_ref, half + a * slots + 2 * t, a)
            own = basis_ref[a].astype(F32)
            folded = own[:nfreq] * total[:nfreq] + own[nfreq:] * total[nfreq:]
            done_ref[a] = (folded * w_ref[a : a + 1, :]).astype(BF16)
            copies.append(pltpu.make_async_copy(done_ref.at[a], out_ref.at[:, a * blk : (a + 1) * blk], sems.at[a]))
            copies[-1].start()
        for copy in copies:
            copy.wait()

    @pl.when(many > steps)
    def _():
        sum_ref[...] = early_ref[...]

        def step(t, _):
            for a in range(nblk):
                sum_ref[a] += pair_sums(code_ref, pip_ref, basis_ref, w_ref, half + a * slots + 2 * t, a)
            return _

        lax.fori_loop(steps, many, step, 0)
        finish(sum_ref, steps)

    pl.when(many == steps)(lambda: finish(early_ref, steps))
    pl.when(jnp.logical_and(many > 0, many < steps))(lambda: finish(early_ref, steps - 1))
    pl.when(many == 0)(lambda: finish(early_ref, 0))


def vm(shape, dtype):
    return pltpu.VMEM(shape, dtype)


def sm(shape):
    return pltpu.SMEM(shape, jnp.int32)


def per_device(completeness, stencil, features, frequencies, gal_cell, pip, pair_src, pair_count):
    bands, nx, ny = completeness.shape
    feats, galaxies = features.shape
    nfreq = frequencies.shape[1]
    nblk, slots, blk, _ = pip.shape
    n = bands * nx
    two = 2 * bands

    def call(body, out, args, anys=(), scratch=(), name=None, aliases=None, cost=1, scalars=()):
        return pl.pallas_call(
            body, out_shape=out, in_specs=[SMEM] * len(scalars) + [VMEM] * len(args) + [ANY] * len(anys),
            out_specs=jax.tree.map(lambda x: SMEM if x.memory_space == pltpu.SMEM else VMEM, out),
            scratch_shapes=scratch, compiler_params=params(), input_output_aliases=aliases or {}, name=name,
            cost_estimate=pl.CostEstimate(flops=cost, bytes_accessed=1, transcendentals=0),
        )(*scalars, *args, *anys)

    cells = gal_cell.reshape(1, galaxies)
    given = (completeness, features, frequencies, stencil, cells, pair_src, pair_count)
    kept = tuple(vm(x.shape, x.dtype) for x in given[1:5]) + tuple(sm(x.shape) for x in given[5:])
    rim, rows, features, frequencies, stencil, cells, pair_src, pair_count = pl.pallas_call(
        rim_kernel, out_shape=(vm((RIM, 128), BF16), vm((n, ny), F32)) + kept,
        in_specs=[HBM] * len(given), out_specs=(VMEM,) * 6 + (SMEM,) * 2, compiler_params=params(), name="rim",
        scratch_shapes=[pltpu.VMEM(completeness.shape, F32), pltpu.SemaphoreType.DMA((len(given),))],
    )(*[pltpu.with_memory_space_constraint(x, pltpu.HBM) for x in given])
    tables = (vm((stencil.shape[0] * bands, ny), F32), vm((5 * RIM, n), F32), vm((n, galaxies), BF16))
    rim, taps, lane_taps, hit = call(
        functools.partial(ahead_kernel, bands, nx, ny), (vm((RIM, 128), BF16), *tables), (rim, stencil, cells), (),
        [pltpu.VMEM((32, 128), F32)], "ahead",
    )
    d_odd, d_even = exchange("dec", rim, rim)
    f_odd, f_even = exchange("dec", features, features)
    taps, lane_taps, hit = call(
        functools.partial(ready_kernel, bands, nx, ny), tables, (stencil, cells), (rim, taps, lane_taps, hit),
        [pltpu.VMEM((32, 128), F32)], "ready", {3: 0, 4: 1, 5: 2},
    )
    inner = call(
        functools.partial(inner_kernel, bands), vm((n, ny), F32), (rows, taps), (), [pltpu.VMEM((5, n, ny), F32)], "inner",
    )
    to_odd, to_even = call(
        row_kernel, (vm((two + RIM, ny), BF16),) * 2, (rows, d_odd, d_even), (inner,), name="rows", cost=LONG
    )
    r_odd, r_even = exchange("ra", to_odd, to_even)
    even_side = call(
        functools.partial(even_side_kernel, bands), vm((8, galaxies), F32),
        (inner, d_odd, d_even, r_even, taps, lane_taps, hit, cells), (),
        [pltpu.VMEM((5, two, ny), F32), pltpu.VMEM((n, ny), F32)], "even_side",
    )
    column = call(stack_rows_kernel, vm((3 * feats, galaxies), BF16), (features, f_odd, f_even), (even_side,), name="stack_features")
    c_odd, c_even = exchange("ra", column, column)

    blocks = vm((9 * nblk, 2 * nfreq, blk), BF16)
    scratch = [pltpu.VMEM((nfreq, feats), BF16)]
    table, code = call(
        functools.partial(own_basis_kernel, nblk), (blocks, sm((nblk * (FIRST + slots) + 2,))), (frequencies, features), (column,),
        scratch + [pltpu.SMEM((9,), jnp.int32)], "own_basis", scalars=(pair_src, pair_count),
    )

    def basis(part, tiles, array, buffer, after):
        def body(freq_ref, feat_ref, *refs):
            basis_kernel(3 * part * nblk, tiles, nblk, freq_ref, feat_ref, *refs[-2:])

        return call(body, blocks, (frequencies, array), (after, buffer), scratch, "basis%d" % part, {3: 0})

    weight, table = call(
        functools.partial(weight_kernel, bands), (vm((3 * nblk + 15 & -16, blk), BF16), blocks),
        (even_side, r_odd, taps, lane_taps, hit, cells), (table,),
        [pltpu.VMEM((5, two, ny), F32), pltpu.VMEM((two, ny), F32)], "weight", {6: 1}, LONG,
    )
    w_odd, w_even = exchange("dec", weight, weight)
    table = basis(0, (1, 2), column, table, weight)
    table = basis(1, (0, 1, 2), c_even, table, weight)
    w_column, table = call(
        functools.partial(stack_weight_kernel, nblk), (vm(weight.shape, BF16), blocks), (weight, w_odd, w_even), (table,), name="stack_weights",
        aliases={3: 1},
    )
    x_odd, x_even = exchange("ra", w_column, w_column)
    early = call(
        early_kernel, vm((nblk, 2 * nfreq, blk), F32), (pip, table, w_column, x_even), (w_column,),
        [pltpu.VMEM((9 * nblk + 4, blk), F32)], "early_pairs", scalars=(code,),
    )
    table = basis(2, (0, 1, 2), c_odd, table, early)
    return pl.pallas_call(
        pair_kernel, out_shape=jax.ShapeDtypeStruct((nfreq, galaxies), BF16), in_specs=[SMEM] + [VMEM] * 6, out_specs=ANY,
        scratch_shapes=[
            pltpu.VMEM((9 * nblk + 4, blk), F32), pltpu.VMEM((nblk, 2 * nfreq, blk), F32),
            pltpu.VMEM((nblk, nfreq, blk), BF16), pltpu.SemaphoreType.DMA((nblk,)),
        ],
        compiler_params=params(), name="pairs",
    )(code, pip, table, early, w_column, x_even, x_odd)


def solution(mesh):
    in_specs = (
        P(None, "ra", "dec"),
        P(),
        P(None, ("ra", "dec")),
        P(),
        P(("ra", "dec")),
        P(("ra", "dec"), None, None, None),
        P(("ra", "dec"), None),
        P(("ra", "dec")),
    )
    out_specs = P(None, ("ra", "dec"))
    return jax.shard_map(per_device, mesh=mesh, in_specs=in_specs, out_specs=out_specs, check_vma=False)
```

```python
import functools
import math

import jax
import jax.numpy as jnp
from jax import lax
from jax.experimental import pallas as pl
from jax.experimental.pallas import tpu as pltpu
from jax.sharding import PartitionSpec as P

BF16 = jnp.bfloat16
F32 = jnp.float32
LONG = 1 << 36
FIRST = 6
RIM = 16

VMEM = pl.BlockSpec(memory_space=pltpu.VMEM)
SMEM = pl.BlockSpec(memory_space=pltpu.SMEM)
ANY = pl.BlockSpec(memory_space=pl.ANY)
HBM = pl.BlockSpec(memory_space=pltpu.HBM)

COS = (0.99999922, -19.73898252, 64.92872662, -85.27239701, 58.79403871, -21.07678212)
SIN = (6.2830558, -41.33121431, 81.36681529, -74.47800454, 32.7814008)


def params(limit=None, **kw):
    return pltpu.CompilerParams(vmem_limit_bytes=limit or (16 << 20), **kw)


def swap(axis, odd, payload):
    ra, dec = lax.axis_size("ra"), lax.axis_size("dec")
    here = (lambda r, d: r * dec + d) if axis == "ra" else (lambda d, r: r * dec + d)
    count, other = (ra, dec) if axis == "ra" else (dec, ra)
    pairs = [(here(i, k), here(i + 1, k)) for i in range(odd, count - 1, 2) for k in range(other)]
    busy = {i for pair in pairs for i in pair}
    for i in (0, count - 1):
        ends = [(here(i, k), here(i, k + 1)) for k in range(0, other - 1, 2)]
        pairs += [pair for pair in ends if not busy & set(pair)]
    return lax.ppermute(payload, ("ra", "dec"), sorted(pairs + [(b, a) for a, b in pairs]))


def exchange(axis, odd_payload, even_payload):
    if axis == "ra":
        even = swap(axis, 0, even_payload)
        return swap(axis, 1, odd_payload), even
    odd = swap(axis, 1, odd_payload)
    return odd, swap(axis, 0, even_payload)


def sides(axis):
    i, n = lax.axis_index(axis), lax.axis_size(axis)
    odd = lax.rem(i, 2) == 1
    return odd, jnp.logical_and(i > 0, jnp.logical_not(jnp.logical_and(odd, i == n - 1)))


def dot(a, b, ca, cb):
    return lax.dot_general(a, b, (((ca,), (cb,)), ((), ())), preferred_element_type=F32)


def rim_kernel(*refs):
    count = (len(refs) - 4) // 2
    given, (rim_ref, rows_ref, hit_ref), kept = refs[:count], refs[count : count + 3], refs[count + 3 : -2]
    comp_ref, sems = refs[-2:]
    bands, nx, ny = comp_ref.shape
    parts = [pl.ds(at, bands // 4) for at in range(0, bands, bands // 4)]
    others = list(zip(given[1:], kept, strict=True))
    pairs = others[:1] + [(given[0].at[part], comp_ref.at[part]) for part in parts] + others[1:]
    copies = [pltpu.make_async_copy(a, b, sems.at[i]) for i, (a, b) in enumerate(pairs)]
    for copy in copies:
        copy.start()
    row = lax.broadcasted_iota(jnp.int32, (8, ny), 0)
    lane = lax.broadcasted_iota(jnp.int32, (8, ny), 1)
    pick = ((row < 2) & (lane == row)) | ((row >= 2) & (row < 4) & (lane == row + ny - 4))
    copies[0].wait()
    cell = kept[0][...]
    slot = (cell // ny % nx) * bands + cell // (nx * ny)
    hit = lax.broadcasted_iota(jnp.int32, hit_ref.shape, 0) == slot
    hit_ref[...] = jnp.where(hit, 1.0, 0.0).astype(BF16)
    for copy, part in zip(copies[1:], parts):
        copy.wait()
        for x in range(nx):
            at = x * bands + part.start
            rows_ref[at : at + part.size, :] = comp_ref[part.start : part.start + part.size, x, :]
    rim = dot(pick.astype(F32).astype(BF16), rows_ref[...].astype(BF16), 1, 1)
    rim_ref[...] = jnp.concatenate([rim[0:4, at : at + 128] for at in range(0, bands * nx, 128)], 0).astype(BF16)
    for copy in copies[len(parts) + 1 :]:
        copy.wait()


def list_slots(nblk, src_ref, count_ref, code_ref, tile_ref):
    own, slots = src_ref.shape
    blocks, half = 9 * nblk, own * FIRST
    ra_odd, _ = sides("ra")
    dec_odd, _ = sides("dec")
    ra_up, dec_up = jnp.where(ra_odd, 2, 1), jnp.where(dec_odd, 1, 2)
    ra, dec = lax.axis_index("ra"), lax.axis_index("dec")
    last_ra, last_dec = lax.axis_size("ra") - 1, lax.axis_size("dec") - 1
    for i, (ra_at, ra_in) in enumerate(((3 - ra_up, ra > 0), (0, ra >= 0), (ra_up, ra < last_ra))):
        for j, (dec_at, dec_in) in enumerate(((3 - dec_up, dec > 0), (0, dec >= 0), (dec_up, dec < last_dec))):
            tile_ref[3 * i + j] = jnp.where(jnp.logical_and(ra_in, dec_in), (3 * ra_at + dec_at) * nblk, -blocks)
    for i in range(half + own * slots):
        code_ref[i] = blocks * 65536
    steps = jnp.int32(0)
    for a in range(own):
        early, late = jnp.int32(0), jnp.int32(0)
        for p in range(slots):
            s = src_ref[a, p]
            at = tile_ref[lax.div(s, nblk)] + lax.rem(s, nblk)
            live = jnp.logical_and(p < count_ref[a], at >= 0)
            soon = jnp.logical_and(at < 6 * nblk, early < FIRST)
            to = jnp.where(soon, a * FIRST + early, half + a * slots + late)
            code_ref[jnp.where(live, to, half + own * slots + 1)] = p + at * (256 + 65536)
            early = early + jnp.where(jnp.logical_and(live, soon), 1, 0)
            late = late + jnp.where(jnp.logical_and(live, jnp.logical_not(soon)), 1, 0)
        steps = jnp.maximum(steps, lax.div(late + 1, 2))
    code_ref[half + own * slots] = steps


def leads():
    return jnp.logical_and(lax.axis_index("ra") < 2, lax.axis_index("dec") == 0)


def ahead_kernel(bands, nx, ny, rim_in_ref, stencil_ref, rim_ref, taps_ref, lane_taps_ref, st_ref):
    rim_ref[...] = rim_in_ref[...]
    pl.when(leads())(lambda: ready(bands, nx, ny, stencil_ref, taps_ref, lane_taps_ref, st_ref))


def ready_kernel(bands, nx, ny, stencil_ref, rim_ref, taps_in_ref, lane_taps_in_ref, taps_ref, lane_taps_ref, st_ref):
    late = jnp.logical_not(leads())
    pl.when(late)(lambda: ready(bands, nx, ny, stencil_ref, taps_ref, lane_taps_ref, st_ref))


def ready(bands, nx, ny, stencil_ref, taps_ref, lane_taps_ref, st_ref):
    st_ref[...] = jnp.zeros_like(st_ref)
    count = stencil_ref.shape[0]
    st_ref[0:count, 0:bands] = stencil_ref[...]
    st_ref[0:count, bands : 2 * bands] = stencil_ref[...]
    by_band = st_ref[...].T
    for k in range(count):
        taps_ref[k * bands : (k + 1) * bands, :] = jnp.broadcast_to(by_band[0:bands, k : k + 1], (bands, ny))
    along = jnp.concatenate([st_ref[...]] * (nx // 2), 1)
    lane_taps_ref[...] = jnp.zeros_like(lane_taps_ref)
    for a in range(5):
        for row, c in ((0, 0), (1, 0), (2, 4), (3, 3), (8, 1), (11, 4)):
            lane_taps_ref[16 * a + row : 16 * a + row + 1, :] = along[5 * a + c : 5 * a + c + 1, :]


def row_kernel(rows_ref, odd_ref, even_ref, after_ref, to_odd_ref, to_even_ref):
    n = rows_ref.shape[0]
    two = to_odd_ref.shape[0] - RIM
    is_odd, _ = sides("ra")

    def put(ref, start):
        ref[0:two, :] = rows_ref[start : start + two, :].astype(BF16)
        at = start // 128 * 4
        edges = [r[...].astype(F32)[at : at + 4] for r in (odd_ref, even_ref)]
        ref[two:, :] = jnp.concatenate([*edges, jnp.zeros((RIM - 8, 128), F32)], 0).astype(BF16)

    @pl.when(is_odd)
    def _():
        put(to_odd_ref, n - two)
        put(to_even_ref, 0)

    @pl.when(jnp.logical_not(is_odd))
    def _():
        put(to_odd_ref, 0)
        put(to_even_ref, n - two)


def beside(odd, even):
    dec_odd, has_odd = sides("dec")
    odd = jnp.where(has_odd, odd, 0.0)
    before, after = jnp.where(dec_odd, even, odd), jnp.where(dec_odd, odd, even)
    none = jnp.zeros_like(before)
    return jnp.concatenate([before[2:4], after[0:1], after[0:1], none, before[3:4], none[0:2], after[1:2], none], 0)


def columns_of(rim):
    return jnp.concatenate([rim[at : at + 4] for at in range(0, RIM, 4)], 1)


def edge_sums(lane_taps_ref, bands, columns):
    width = columns.shape[1]
    size = lane_taps_ref.shape[1]
    total = jnp.zeros((RIM, size), F32)
    for a in range(5):
        moved = columns if a == 0 else pltpu.roll(columns, width - a * bands, 1)
        total = total + lane_taps_ref[16 * a : 16 * a + 16, :] * moved[:, 0:size]
    return total[0:8] + total[8:16]


def extend(ext_ref, cells):
    ny = cells.shape[1]
    at = lax.broadcasted_iota(jnp.int32, cells.shape, 1)
    ext_ref[2] = cells
    ext_ref[3] = jnp.where(at > ny - 2, 0.0, pltpu.roll(cells, ny - 1, 1))
    ext_ref[4] = jnp.where(at > ny - 3, 0.0, pltpu.roll(cells, ny - 2, 1))
    ext_ref[1] = jnp.where(at < 1, 0.0, pltpu.roll(cells, 1, 1))
    ext_ref[0] = jnp.where(at < 2, 0.0, pltpu.roll(cells, 2, 1))


def split(x):
    high = x.astype(BF16)
    return high, (x - high.astype(F32)).astype(BF16)


def at_column(table, hits, cell):
    high, low = split(table)
    found = dot(high, hits, 0, 0) + dot(low, hits, 0, 0)
    at = lax.broadcasted_iota(jnp.int32, found.shape, 0) == cell % table.shape[1]
    return jnp.sum(jnp.where(at, found, 0.0), axis=0, keepdims=True)


def at_edge(edges, hits, cell, ny):
    found = dot(jnp.concatenate(split(edges), 0), hits, 1, 0)
    found = found[0:8] + found[8:16]
    y = cell % ny
    row = jnp.where(y < 2, y, jnp.where(y > ny - 3, y - (ny - 4), 8))
    return jnp.sum(jnp.where(lax.broadcasted_iota(jnp.int32, found.shape, 0) == row, found, 0.0), axis=0, keepdims=True)


def inner_kernel(bands, rows_ref, taps_ref, out_ref, ext_ref):
    n, ny = rows_ref.shape
    nx = n // bands
    extend(ext_ref, rows_ref[...])
    for g in range(0, bands, 8):
        accs = [jnp.zeros((8, ny), F32) for _ in range(nx)]
        for c in range(5):
            for a in range(5):
                w = taps_ref[(5 * a + c) * bands + g : (5 * a + c) * bands + g + 8, :]
                for x in range(nx):
                    if 0 <= x + a - 2 < nx:
                        base = (x + a - 2) * bands + g
                        accs[x] = accs[x] + w * ext_ref[c, base : base + 8, :]
        for x in range(nx):
            out_ref[x * bands + g : x * bands + g + 8, :] = accs[x]


def side_sums(ext_ref, taps_ref, bands, up, put):
    parts = (((4, 0),), ((3, 0), (4, 1))) if up else (((0, 0), (1, 1)), ((0, 1),))
    for g in range(0, bands, 8):
        for x, terms in enumerate(parts):
            acc = None
            for a, e in terms:
                for c in range(5):
                    tap = (5 * a + c) * bands + g
                    term = taps_ref[tap : tap + 8, :] * ext_ref[c, e * bands + g : e * bands + g + 8, :]
                    acc = term if acc is None else acc + term
            put(x * bands + g, acc)


def even_side_kernel(bands, inner_ref, odd_ref, even_ref, rows_ref, taps_ref, lane_taps_ref, hit_ref, cell_ref, out_ref, ext_ref, sum_ref):
    n, ny = inner_ref.shape
    two = 2 * bands
    ra_odd, _ = sides("ra")
    sum_ref[...] = inner_ref[...]
    extend(ext_ref, rows_ref[0:two, :].astype(F32))

    def add_from(start):
        def put(at, value):
            sum_ref[start + at : start + at + 8, :] += value

        return put

    pl.when(ra_odd)(lambda: side_sums(ext_ref, taps_ref, bands, False, add_from(0)))
    pl.when(jnp.logical_not(ra_odd))(lambda: side_sums(ext_ref, taps_ref, bands, True, add_from(n - two)))

    own = beside(columns_of(odd_ref[...].astype(F32)), columns_of(even_ref[...].astype(F32)))
    rims = rows_ref[two : two + RIM, :].astype(F32)
    side = beside(rims[0:4], rims[4:8])
    columns = jnp.concatenate([jnp.where(ra_odd, side, 0.0), own, jnp.where(ra_odd, 0.0, side)], 1)
    edges = edge_sums(lane_taps_ref, bands, columns)
    cell = cell_ref[...]
    value = at_column(sum_ref[...], hit_ref[...], cell) + at_edge(edges, hit_ref[...], cell, ny)
    out_ref[...] = jnp.broadcast_to(value, out_ref.shape)


def weight_kernel(bands, even_side_ref, rows_ref, taps_ref, lane_taps_ref, hit_ref, cell_ref, basis_in_ref, out_ref, basis_ref, ext_ref, sum_ref):
    two, ny = sum_ref.shape
    n = hit_ref.shape[0]
    ra_odd, has_odd = sides("ra")
    extend(ext_ref, jnp.where(has_odd, rows_ref[0:two, :].astype(F32), 0.0))

    def put(at, value):
        sum_ref[at : at + 8, :] = value

    pl.when(ra_odd)(lambda: side_sums(ext_ref, taps_ref, bands, True, put))
    pl.when(jnp.logical_not(ra_odd))(lambda: side_sums(ext_ref, taps_ref, bands, False, put))

    rims = rows_ref[two : two + RIM, :].astype(F32)
    side = jnp.where(has_odd, beside(rims[0:4], rims[4:8]), 0.0)
    columns = jnp.concatenate([jnp.where(ra_odd, 0.0, side), jnp.zeros((RIM, n), F32), jnp.where(ra_odd, side, 0.0)], 1)
    edges = edge_sums(lane_taps_ref, bands, columns)
    edges = jnp.where(ra_odd, edges[:, n - two :], edges[:, 0:two])
    hits = hit_ref[pl.ds(pl.multiple_of(jnp.where(ra_odd, n - two, 0), two), two), :]
    cell = cell_ref[...]
    value = even_side_ref[0:1, :] + at_column(sum_ref[...], hits, cell) + at_edge(edges, hits, cell, ny)
    weights = lax.rsqrt(value)
    blk = out_ref.shape[1]
    rows = [weights[:, at : at + blk] for at in range(0, weights.shape[1], blk)]
    out_ref[...] = jnp.concatenate([*rows, jnp.zeros((out_ref.shape[0] - len(rows), blk), F32)], 0).astype(BF16)


def stack_weight_kernel(nblk, own_ref, odd_ref, even_ref, basis_in_ref, out_ref, basis_ref):
    _, has_odd = sides("dec")
    own, odd, even = (ref[...].astype(F32)[0:nblk] for ref in (own_ref, odd_ref, even_ref))
    none = jnp.zeros((out_ref.shape[0] - 3 * nblk, out_ref.shape[1]), F32)
    out_ref[...] = jnp.concatenate([own, jnp.where(has_odd, odd, 0.0), even, none], 0).astype(BF16)


def stack_rows_kernel(a_ref, b_ref, c_ref, after_ref, out_ref):
    n = a_ref.shape[0]
    out_ref[0:n, :] = a_ref[...]
    out_ref[n : 2 * n, :] = b_ref[...]
    out_ref[2 * n :, :] = c_ref[...]


def sincos(theta):
    turns = theta * (0.5 / math.pi)
    magic = 12582912.0
    r = turns - ((turns + magic) - magic)
    z = r * r
    c = jnp.full_like(z, COS[-1])
    for k in COS[-2::-1]:
        c = c * z + k
    s = jnp.full_like(z, SIN[-1])
    for k in SIN[-2::-1]:
        s = s * z + k
    return c, s * r


def basis_kernel(first, tiles, nblk, freq_ref, feat_ref, out_ref, ft_ref):
    feats, nfreq = freq_ref.shape
    blk = out_ref.shape[2]
    ft_ref[...] = freq_ref[...].astype(F32).T.astype(BF16)

    def work(t):
        for b in range(nblk):
            c, s = sincos(dot(ft_ref[...], feat_ref[t * feats : (t + 1) * feats, b * blk : (b + 1) * blk], 1, 0))
            out_ref[first + t * nblk + b, 0:nfreq, :] = c.astype(BF16)
            out_ref[first + t * nblk + b, nfreq:, :] = s.astype(BF16)

    def inside():
        for t in tiles:
            if t != 1:
                work(t)
        if 1 in tiles:
            pl.when(sides("dec")[1])(functools.partial(work, 1))

    if first == 6 * nblk:
        pl.when(sides("ra")[1])(inside)
    else:
        inside()


def own_basis_kernel(nblk, src_ref, count_ref, freq_ref, feat_ref, after_ref, out_ref, code_ref, ft_ref, tile_ref):
    list_slots(nblk, src_ref, count_ref, code_ref, tile_ref)
    basis_kernel(0, (0,), nblk, freq_ref, feat_ref, out_ref, ft_ref)


def pair_sums(code_ref, pip_ref, basis_ref, w_ref, at, a):
    lhs, rhs = [], []
    for k in range(2):
        code = code_ref[at + k]
        lhs.append(basis_ref[lax.rem(lax.div(code, 256), 256)])
        w = w_ref[pl.ds(lax.div(code, 65536), 1), :]
        rhs.append((pip_ref[a, lax.rem(code, 256)].astype(F32) * w).astype(BF16))
    return dot(jnp.concatenate(lhs, 1), jnp.concatenate(rhs, 1), 1, 1)


def spread_weights(w_ref, *refs):
    rows = w_ref.shape[0] // 9 * 3
    w_ref[3 * rows :, :] = jnp.zeros((w_ref.shape[0] - 3 * rows, w_ref.shape[1]), F32)
    for i, ref in enumerate(refs):
        w = ref[...].astype(F32)[0:rows]
        w_ref[i * rows : (i + 1) * rows, :] = w if i < 2 else jnp.where(sides("ra")[1], w, 0.0)


def early_kernel(code_ref, pip_ref, basis_ref, w_own_ref, w_even_ref, after_ref, sum_ref, w_ref):
    nblk, _, blk, _ = pip_ref.shape
    spread_weights(w_ref, w_own_ref, w_even_ref)
    for a in range(nblk):
        total = None
        for p in range(0, FIRST, 2):
            part = pair_sums(code_ref, pip_ref, basis_ref, w_ref, a * FIRST + p, a)
            total = part if total is None else total + part
        sum_ref[a] = total


def pair_kernel(code_ref, pip_ref, basis_ref, early_ref, w_own_ref, w_even_ref, w_odd_ref, out_ref, w_ref, sum_ref, done_ref, sems):
    nblk, slots, blk, _ = pip_ref.shape
    nfreq = out_ref.shape[0]
    half, steps = nblk * FIRST, (slots - FIRST) // 2
    spread_weights(w_ref, w_own_ref, w_even_ref, w_odd_ref)
    many = code_ref[half + nblk * slots]

    def finish(start_ref, count):
        copies = []
        for a in range(nblk):
            total = start_ref[a]
            for t in range(count):
                total = total + pair_sums(code_ref, pip_ref, basis_ref, w_ref, half + a * slots + 2 * t, a)
            own = basis_ref[a].astype(F32)
            folded = own[:nfreq] * total[:nfreq] + own[nfreq:] * total[nfreq:]
            done_ref[a] = (folded * w_ref[a : a + 1, :]).astype(BF16)
            copies.append(pltpu.make_async_copy(done_ref.at[a], out_ref.at[:, a * blk : (a + 1) * blk], sems.at[a]))
            copies[-1].start()
        for copy in copies:
            copy.wait()

    @pl.when(many > steps)
    def _():
        sum_ref[...] = early_ref[...]

        def step(t, _):
            for a in range(nblk):
                sum_ref[a] += pair_sums(code_ref, pip_ref, basis_ref, w_ref, half + a * slots + 2 * t, a)
            return _

        lax.fori_loop(steps, many, step, 0)
        finish(sum_ref, steps)

    pl.when(many == steps)(lambda: finish(early_ref, steps))
    pl.when(jnp.logical_and(many > 0, many < steps))(lambda: finish(early_ref, steps - 1))
    pl.when(many == 0)(lambda: finish(early_ref, 0))


def vm(shape, dtype):
    return pltpu.VMEM(shape, dtype)


def sm(shape):
    return pltpu.SMEM(shape, jnp.int32)


def per_device(completeness, stencil, features, frequencies, gal_cell, pip, pair_src, pair_count):
    bands, nx, ny = completeness.shape
    feats, galaxies = features.shape
    nfreq = frequencies.shape[1]
    nblk, slots, blk, _ = pip.shape
    n = bands * nx
    two = 2 * bands

    def call(body, out, args, anys=(), scratch=(), name=None, aliases=None, cost=1, scalars=()):
        return pl.pallas_call(
            body, out_shape=out, in_specs=[SMEM] * len(scalars) + [VMEM] * len(args) + [ANY] * len(anys),
            out_specs=jax.tree.map(lambda x: SMEM if x.memory_space == pltpu.SMEM else VMEM, out),
            scratch_shapes=scratch, compiler_params=params(), input_output_aliases=aliases or {}, name=name,
            cost_estimate=pl.CostEstimate(flops=cost, bytes_accessed=1, transcendentals=0),
        )(*scalars, *args, *anys)

    cells = gal_cell.reshape(1, galaxies)
    given = (completeness, cells, stencil, features, frequencies, pair_src, pair_count)
    kept = tuple(vm(x.shape, x.dtype) for x in given[1:5]) + tuple(sm(x.shape) for x in given[5:])
    rim, rows, hit, cells, stencil, features, frequencies, pair_src, pair_count = pl.pallas_call(
        rim_kernel, out_shape=(vm((RIM, 128), BF16), vm((n, ny), F32), vm((n, galaxies), BF16)) + kept,
        in_specs=[HBM] * len(given), out_specs=(VMEM,) * 7 + (SMEM,) * 2, compiler_params=params(), name="rim",
        scratch_shapes=[pltpu.VMEM(completeness.shape, F32), pltpu.SemaphoreType.DMA((len(given) + 3,))],
    )(*[pltpu.with_memory_space_constraint(x, pltpu.HBM) for x in given])
    tables = (vm((stencil.shape[0] * bands, ny), F32), vm((5 * RIM, n), F32))
    rim, taps, lane_taps = call(
        functools.partial(ahead_kernel, bands, nx, ny), (vm((RIM, 128), BF16), *tables), (rim, stencil), (),
        [pltpu.VMEM((32, 128), F32)], "ahead",
    )
    d_odd, d_even = exchange("dec", rim, rim)
    f_odd, f_even = exchange("dec", features, features)
    taps, lane_taps = call(
        functools.partial(ready_kernel, bands, nx, ny), tables, (stencil,), (rim, taps, lane_taps),
        [pltpu.VMEM((32, 128), F32)], "ready", {2: 0, 3: 1},
    )
    inner = call(
        functools.partial(inner_kernel, bands), vm((n, ny), F32), (rows, taps), (), [pltpu.VMEM((5, n, ny), F32)], "inner",
    )
    to_odd, to_even = call(
        row_kernel, (vm((two + RIM, ny), BF16),) * 2, (rows, d_odd, d_even), (inner,), name="rows", cost=LONG
    )
    r_odd, r_even = exchange("ra", to_odd, to_even)
    even_side = call(
        functools.partial(even_side_kernel, bands), vm((8, galaxies), F32),
        (inner, d_odd, d_even, r_even, taps, lane_taps, hit, cells), (),
        [pltpu.VMEM((5, two, ny), F32), pltpu.VMEM((n, ny), F32)], "even_side",
    )
    column = call(stack_rows_kernel, vm((3 * feats, galaxies), BF16), (features, f_odd, f_even), (even_side,), name="stack_features")
    c_odd, c_even = exchange("ra", column, column)

    blocks = vm((9 * nblk, 2 * nfreq, blk), BF16)
    scratch = [pltpu.VMEM((nfreq, feats), BF16)]
    table, code = call(
        functools.partial(own_basis_kernel, nblk), (blocks, sm((nblk * (FIRST + slots) + 2,))), (frequencies, features), (column,),
        scratch + [pltpu.SMEM((9,), jnp.int32)], "own_basis", scalars=(pair_src, pair_count),
    )

    def basis(part, tiles, array, buffer, after):
        def body(freq_ref, feat_ref, *refs):
            basis_kernel(3 * part * nblk, tiles, nblk, freq_ref, feat_ref, *refs[-2:])

        return call(body, blocks, (frequencies, array), (after, buffer), scratch, "basis%d" % part, {3: 0})

    weight, table = call(
        functools.partial(weight_kernel, bands), (vm((3 * nblk + 15 & -16, blk), BF16), blocks),
        (even_side, r_odd, taps, lane_taps, hit, cells), (table,),
        [pltpu.VMEM((5, two, ny), F32), pltpu.VMEM((two, ny), F32)], "weight", {6: 1}, LONG,
    )
    w_odd, w_even = exchange("dec", weight, weight)
    table = basis(0, (1, 2), column, table, weight)
    table = basis(1, (0, 1, 2), c_even, table, weight)
    w_column, table = call(
        functools.partial(stack_weight_kernel, nblk), (vm(weight.shape, BF16), blocks), (weight, w_odd, w_even), (table,), name="stack_weights",
        aliases={3: 1},
    )
    x_odd, x_even = exchange("ra", w_column, w_column)
    early = call(
        early_kernel, vm((nblk, 2 * nfreq, blk), F32), (pip, table, w_column, x_even), (w_column,),
        [pltpu.VMEM((9 * nblk + 4, blk), F32)], "early_pairs", scalars=(code,),
    )
    table = basis(2, (0, 1, 2), c_odd, table, early)
    return pl.pallas_call(
        pair_kernel, out_shape=jax.ShapeDtypeStruct((nfreq, galaxies), BF16), in_specs=[SMEM] + [VMEM] * 6, out_specs=ANY,
        scratch_shapes=[
            pltpu.VMEM((9 * nblk + 4, blk), F32), pltpu.VMEM((nblk, 2 * nfreq, blk), F32),
            pltpu.VMEM((nblk, nfreq, blk), BF16), pltpu.SemaphoreType.DMA((nblk,)),
        ],
        compiler_params=params(), name="pairs",
    )(code, pip, table, early, w_column, x_even, x_odd)


def solution(mesh):
    in_specs = (
        P(None, "ra", "dec"),
        P(),
        P(None, ("ra", "dec")),
        P(),
        P(("ra", "dec")),
        P(("ra", "dec"), None, None, None),
        P(("ra", "dec"), None),
        P(("ra", "dec")),
    )
    out_specs = P(None, ("ra", "dec"))
    return jax.shard_map(per_device, mesh=mesh, in_specs=in_specs, out_specs=out_specs, check_vma=False)
```

```python
import functools
import math

import jax
import jax.numpy as jnp
from jax import lax
from jax.experimental import pallas as pl
from jax.experimental.pallas import tpu as pltpu
from jax.sharding import PartitionSpec as P

BF16 = jnp.bfloat16
F32 = jnp.float32
LONG = 1 << 36
FIRST = 6
RIM = 16

VMEM = pl.BlockSpec(memory_space=pltpu.VMEM)
SMEM = pl.BlockSpec(memory_space=pltpu.SMEM)
ANY = pl.BlockSpec(memory_space=pl.ANY)
HBM = pl.BlockSpec(memory_space=pltpu.HBM)

COS = (0.99999922, -19.73898252, 64.92872662, -85.27239701, 58.79403871, -21.07678212)
SIN = (6.2830558, -41.33121431, 81.36681529, -74.47800454, 32.7814008)


def params(limit=None, **kw):
    return pltpu.CompilerParams(vmem_limit_bytes=limit or (16 << 20), **kw)


def swap(axis, odd, payload):
    ra, dec = lax.axis_size("ra"), lax.axis_size("dec")
    here = (lambda r, d: r * dec + d) if axis == "ra" else (lambda d, r: r * dec + d)
    count, other = (ra, dec) if axis == "ra" else (dec, ra)
    pairs = [(here(i, k), here(i + 1, k)) for i in range(odd, count - 1, 2) for k in range(other)]
    busy = {i for pair in pairs for i in pair}
    for i in (0, count - 1):
        ends = [(here(i, k), here(i, k + 1)) for k in range(0, other - 1, 2)]
        pairs += [pair for pair in ends if not busy & set(pair)]
    return lax.ppermute(payload, ("ra", "dec"), sorted(pairs + [(b, a) for a, b in pairs]))


def exchange(axis, odd_payload, even_payload):
    if axis == "ra":
        even = swap(axis, 0, even_payload)
        return swap(axis, 1, odd_payload), even
    odd = swap(axis, 1, odd_payload)
    return odd, swap(axis, 0, even_payload)


def sides(axis):
    i, n = lax.axis_index(axis), lax.axis_size(axis)
    odd = lax.rem(i, 2) == 1
    return odd, jnp.logical_and(i > 0, jnp.logical_not(jnp.logical_and(odd, i == n - 1)))


def dot(a, b, ca, cb):
    return lax.dot_general(a, b, (((ca,), (cb,)), ((), ())), preferred_element_type=F32)


def rim_kernel(*refs):
    count = (len(refs) - 4) // 2
    given, (rim_ref, rows_ref, hit_ref), kept = refs[:count], refs[count : count + 3], refs[count + 3 : -2]
    comp_ref, sems = refs[-2:]
    bands, nx, ny = comp_ref.shape
    parts = [pl.ds(at, bands // 4) for at in range(0, bands, bands // 4)]
    others = list(zip(given[1:], kept, strict=True))
    pairs = others[:1] + [(given[0].at[part], comp_ref.at[part]) for part in parts] + others[1:]
    copies = [pltpu.make_async_copy(a, b, sems.at[i]) for i, (a, b) in enumerate(pairs)]
    for copy in copies:
        copy.start()
    row = lax.broadcasted_iota(jnp.int32, (8, ny), 0)
    lane = lax.broadcasted_iota(jnp.int32, (8, ny), 1)
    pick = ((row < 2) & (lane == row)) | ((row >= 2) & (row < 4) & (lane == row + ny - 4))
    copies[0].wait()
    cell = kept[0][...]
    slot = (cell // ny % nx) * bands + cell // (nx * ny)
    hit = lax.broadcasted_iota(jnp.int32, hit_ref.shape, 0) == slot
    hit_ref[...] = jnp.where(hit, 1.0, 0.0).astype(BF16)
    for copy, part in zip(copies[1:], parts):
        copy.wait()
        for x in range(nx):
            at = x * bands + part.start
            rows_ref[at : at + part.size, :] = comp_ref[part.start : part.start + part.size, x, :]
    rim = dot(pick.astype(F32).astype(BF16), rows_ref[...].astype(BF16), 1, 1)
    rim_ref[...] = jnp.concatenate([rim[0:4, at : at + 128] for at in range(0, bands * nx, 128)], 0).astype(BF16)
    for copy in copies[len(parts) + 1 :]:
        copy.wait()


def list_slots(nblk, src_ref, count_ref, code_ref, tile_ref):
    own, slots = src_ref.shape
    blocks, half = 9 * nblk, own * FIRST
    ra_odd, _ = sides("ra")
    dec_odd, _ = sides("dec")
    ra_up, dec_up = jnp.where(ra_odd, 2, 1), jnp.where(dec_odd, 1, 2)
    ra, dec = lax.axis_index("ra"), lax.axis_index("dec")
    last_ra, last_dec = lax.axis_size("ra") - 1, lax.axis_size("dec") - 1
    for i, (ra_at, ra_in) in enumerate(((3 - ra_up, ra > 0), (0, ra >= 0), (ra_up, ra < last_ra))):
        for j, (dec_at, dec_in) in enumerate(((3 - dec_up, dec > 0), (0, dec >= 0), (dec_up, dec < last_dec))):
            tile_ref[3 * i + j] = jnp.where(jnp.logical_and(ra_in, dec_in), (3 * ra_at + dec_at) * nblk, -blocks)
    for i in range(half + own * slots):
        code_ref[i] = blocks * 65536
    steps = jnp.int32(0)
    for a in range(own):
        early, late = jnp.int32(0), jnp.int32(0)
        for p in range(slots):
            s = src_ref[a, p]
            at = tile_ref[lax.div(s, nblk)] + lax.rem(s, nblk)
            live = jnp.logical_and(p < count_ref[a], at >= 0)
            soon = jnp.logical_and(at < 6 * nblk, early < FIRST)
            to = jnp.where(soon, a * FIRST + early, half + a * slots + late)
            code_ref[jnp.where(live, to, half + own * slots + 1)] = p + at * (256 + 65536)
            early = early + jnp.where(jnp.logical_and(live, soon), 1, 0)
            late = late + jnp.where(jnp.logical_and(live, jnp.logical_not(soon)), 1, 0)
        steps = jnp.maximum(steps, lax.div(late + 1, 2))
    code_ref[half + own * slots] = steps


def leads():
    return jnp.logical_and(lax.axis_index("ra") < 2, lax.axis_index("dec") == 0)


def ahead_kernel(bands, nx, ny, rim_in_ref, stencil_ref, rim_ref, taps_ref, lane_taps_ref, st_ref):
    rim_ref[...] = rim_in_ref[...]
    pl.when(leads())(lambda: ready(bands, nx, ny, stencil_ref, taps_ref, lane_taps_ref, st_ref))


def ready_kernel(bands, nx, ny, stencil_ref, rim_ref, taps_in_ref, lane_taps_in_ref, taps_ref, lane_taps_ref, st_ref):
    late = jnp.logical_not(leads())
    pl.when(late)(lambda: ready(bands, nx, ny, stencil_ref, taps_ref, lane_taps_ref, st_ref))


def ready(bands, nx, ny, stencil_ref, taps_ref, lane_taps_ref, st_ref):
    st_ref[...] = jnp.zeros_like(st_ref)
    count = stencil_ref.shape[0]
    st_ref[0:count, 0:bands] = stencil_ref[...]
    st_ref[0:count, bands : 2 * bands] = stencil_ref[...]
    by_band = st_ref[...].T
    for k in range(count):
        taps_ref[k * bands : (k + 1) * bands, :] = jnp.broadcast_to(by_band[0:bands, k : k + 1], (bands, ny))
    along = jnp.concatenate([st_ref[...]] * (nx // 2), 1)
    lane_taps_ref[...] = jnp.zeros_like(lane_taps_ref)
    for a in range(5):
        for row, c in ((0, 0), (1, 0), (2, 4), (3, 3), (8, 1), (11, 4)):
            lane_taps_ref[16 * a + row : 16 * a + row + 1, :] = along[5 * a + c : 5 * a + c + 1, :]


def row_kernel(rows_ref, odd_ref, even_ref, after_ref, to_odd_ref, to_even_ref):
    n = rows_ref.shape[0]
    two = to_odd_ref.shape[0] - RIM
    is_odd, _ = sides("ra")

    def put(ref, start):
        ref[0:two, :] = rows_ref[start : start + two, :].astype(BF16)
        at = start // 128 * 4
        edges = [r[...].astype(F32)[at : at + 4] for r in (odd_ref, even_ref)]
        ref[two:, :] = jnp.concatenate([*edges, jnp.zeros((RIM - 8, 128), F32)], 0).astype(BF16)

    @pl.when(is_odd)
    def _():
        put(to_odd_ref, n - two)
        put(to_even_ref, 0)

    @pl.when(jnp.logical_not(is_odd))
    def _():
        put(to_odd_ref, 0)
        put(to_even_ref, n - two)


def beside(odd, even):
    dec_odd, has_odd = sides("dec")
    odd = jnp.where(has_odd, odd, 0.0)
    before, after = jnp.where(dec_odd, even, odd), jnp.where(dec_odd, odd, even)
    none = jnp.zeros_like(before)
    return jnp.concatenate([before[2:4], after[0:1], after[0:1], none, before[3:4], none[0:2], after[1:2], none], 0)


def columns_of(rim):
    return jnp.concatenate([rim[at : at + 4] for at in range(0, RIM, 4)], 1)


def edge_sums(lane_taps_ref, bands, columns):
    width = columns.shape[1]
    size = lane_taps_ref.shape[1]
    total = jnp.zeros((RIM, size), F32)
    for a in range(5):
        moved = columns if a == 0 else pltpu.roll(columns, width - a * bands, 1)
        total = total + lane_taps_ref[16 * a : 16 * a + 16, :] * moved[:, 0:size]
    return total[0:8] + total[8:16]


def shifts(cells):
    ny = cells.shape[1]
    at = lax.broadcasted_iota(jnp.int32, cells.shape, 1)
    return (
        jnp.where(at < 2, 0.0, pltpu.roll(cells, 2, 1)),
        jnp.where(at < 1, 0.0, pltpu.roll(cells, 1, 1)),
        cells,
        jnp.where(at > ny - 2, 0.0, pltpu.roll(cells, ny - 1, 1)),
        jnp.where(at > ny - 3, 0.0, pltpu.roll(cells, ny - 2, 1)),
    )


def split(x):
    high = x.astype(BF16)
    return high, (x - high.astype(F32)).astype(BF16)


def at_column(table, hits, cell):
    high, low = split(table)
    found = dot(high, hits, 0, 0) + dot(low, hits, 0, 0)
    at = lax.broadcasted_iota(jnp.int32, found.shape, 0) == cell % table.shape[1]
    return jnp.sum(jnp.where(at, found, 0.0), axis=0, keepdims=True)


def at_edge(edges, hits, cell, ny):
    found = dot(jnp.concatenate(split(edges), 0), hits, 1, 0)
    found = found[0:8] + found[8:16]
    y = cell % ny
    row = jnp.where(y < 2, y, jnp.where(y > ny - 3, y - (ny - 4), 8))
    return jnp.sum(jnp.where(lax.broadcasted_iota(jnp.int32, found.shape, 0) == row, found, 0.0), axis=0, keepdims=True)


def inner_kernel(bands, rows_ref, taps_ref, out_ref):
    n, ny = rows_ref.shape
    nx = n // bands
    for g in range(0, bands, 8):
        cells = [shifts(rows_ref[x * bands + g : x * bands + g + 8, :]) for x in range(nx)]
        accs = [jnp.zeros((8, ny), F32) for _ in range(nx)]
        for c in range(5):
            for a in range(5):
                w = taps_ref[(5 * a + c) * bands + g : (5 * a + c) * bands + g + 8, :]
                for x in range(nx):
                    if 0 <= x + a - 2 < nx:
                        accs[x] = accs[x] + w * cells[x + a - 2][c]
        for x in range(nx):
            out_ref[x * bands + g : x * bands + g + 8, :] = accs[x]


def side_sums(rows_ref, taps_ref, bands, up, there, put):
    parts = (((4, 0),), ((3, 0), (4, 1))) if up else (((0, 0), (1, 1)), ((0, 1),))
    for g in range(0, bands, 16):
        pairs = [rows_ref[e * bands + g : e * bands + g + 16, :].astype(F32) for e in range(2)]
        for h in (0, 8):
            cells = [shifts(jnp.where(there, pair[h : h + 8], 0.0)) for pair in pairs]
            for x, terms in enumerate(parts):
                acc = None
                for a, e in terms:
                    for c in range(5):
                        tap = (5 * a + c) * bands + g + h
                        term = taps_ref[tap : tap + 8, :] * cells[e][c]
                        acc = term if acc is None else acc + term
                put(x * bands + g + h, acc)


def even_side_kernel(bands, inner_ref, odd_ref, even_ref, rows_ref, taps_ref, lane_taps_ref, hit_ref, cell_ref, out_ref, sum_ref):
    n, ny = inner_ref.shape
    two = 2 * bands
    ra_odd, _ = sides("ra")
    sum_ref[...] = inner_ref[...]

    def add_from(start):
        def put(at, value):
            sum_ref[start + at : start + at + 8, :] += value

        return put

    pl.when(ra_odd)(lambda: side_sums(rows_ref, taps_ref, bands, False, True, add_from(0)))
    pl.when(jnp.logical_not(ra_odd))(lambda: side_sums(rows_ref, taps_ref, bands, True, True, add_from(n - two)))

    own = beside(columns_of(odd_ref[...].astype(F32)), columns_of(even_ref[...].astype(F32)))
    rims = rows_ref[two : two + RIM, :].astype(F32)
    side = beside(rims[0:4], rims[4:8])
    columns = jnp.concatenate([jnp.where(ra_odd, side, 0.0), own, jnp.where(ra_odd, 0.0, side)], 1)
    edges = edge_sums(lane_taps_ref, bands, columns)
    cell = cell_ref[...]
    value = at_column(sum_ref[...], hit_ref[...], cell) + at_edge(edges, hit_ref[...], cell, ny)
    out_ref[...] = jnp.broadcast_to(value, out_ref.shape)


def weight_kernel(bands, even_side_ref, rows_ref, taps_ref, lane_taps_ref, hit_ref, cell_ref, basis_in_ref, out_ref, basis_ref, sum_ref):
    two, ny = sum_ref.shape
    n = hit_ref.shape[0]
    ra_odd, has_odd = sides("ra")

    def put(at, value):
        sum_ref[at : at + 8, :] = value

    pl.when(ra_odd)(lambda: side_sums(rows_ref, taps_ref, bands, True, has_odd, put))
    pl.when(jnp.logical_not(ra_odd))(lambda: side_sums(rows_ref, taps_ref, bands, False, has_odd, put))

    rims = rows_ref[two : two + RIM, :].astype(F32)
    side = jnp.where(has_odd, beside(rims[0:4], rims[4:8]), 0.0)
    columns = jnp.concatenate([jnp.where(ra_odd, 0.0, side), jnp.zeros((RIM, n), F32), jnp.where(ra_odd, side, 0.0)], 1)
    edges = edge_sums(lane_taps_ref, bands, columns)
    edges = jnp.where(ra_odd, edges[:, n - two :], edges[:, 0:two])
    hits = hit_ref[pl.ds(pl.multiple_of(jnp.where(ra_odd, n - two, 0), two), two), :]
    cell = cell_ref[...]
    value = even_side_ref[0:1, :] + at_column(sum_ref[...], hits, cell) + at_edge(edges, hits, cell, ny)
    weights = lax.rsqrt(value)
    blk = out_ref.shape[1]
    rows = [weights[:, at : at + blk] for at in range(0, weights.shape[1], blk)]
    out_ref[...] = jnp.concatenate([*rows, jnp.zeros((out_ref.shape[0] - len(rows), blk), F32)], 0).astype(BF16)


def stack_weight_kernel(nblk, own_ref, odd_ref, even_ref, basis_in_ref, out_ref, basis_ref):
    _, has_odd = sides("dec")
    own, odd, even = (ref[...].astype(F32)[0:nblk] for ref in (own_ref, odd_ref, even_ref))
    none = jnp.zeros((out_ref.shape[0] - 3 * nblk, out_ref.shape[1]), F32)
    out_ref[...] = jnp.concatenate([own, jnp.where(has_odd, odd, 0.0), even, none], 0).astype(BF16)


def stack_rows_kernel(a_ref, b_ref, c_ref, after_ref, out_ref):
    n = a_ref.shape[0]
    out_ref[0:n, :] = a_ref[...]
    out_ref[n : 2 * n, :] = b_ref[...]
    out_ref[2 * n :, :] = c_ref[...]


def sincos(theta):
    turns = theta * (0.5 / math.pi)
    magic = 12582912.0
    r = turns - ((turns + magic) - magic)
    z = r * r
    c = jnp.full_like(z, COS[-1])
    for k in COS[-2::-1]:
        c = c * z + k
    s = jnp.full_like(z, SIN[-1])
    for k in SIN[-2::-1]:
        s = s * z + k
    return c, s * r


def basis_kernel(first, tiles, nblk, freq_ref, feat_ref, out_ref, ft_ref, wide_ref=None):
    feats, nfreq = freq_ref.shape
    blk = out_ref.shape[2]
    ft_ref[...] = freq_ref[...].astype(F32).T.astype(BF16)

    def work(t):
        for b in range(nblk):
            c, s = sincos(dot(ft_ref[...], feat_ref[t * feats : (t + 1) * feats, b * blk : (b + 1) * blk], 1, 0))
            if wide_ref is not None:
                wide_ref[b, 0:nfreq, :] = c
                wide_ref[b, nfreq:, :] = s
            out_ref[first + t * nblk + b, 0:nfreq, :] = c.astype(BF16)
            out_ref[first + t * nblk + b, nfreq:, :] = s.astype(BF16)

    def inside():
        for t in tiles:
            if t != 1:
                work(t)
        if 1 in tiles:
            pl.when(sides("dec")[1])(functools.partial(work, 1))

    if first == 6 * nblk:
        pl.when(sides("ra")[1])(inside)
    else:
        inside()


def own_basis_kernel(nblk, src_ref, count_ref, freq_ref, feat_ref, after_ref, out_ref, wide_ref, code_ref, ft_ref, tile_ref):
    list_slots(nblk, src_ref, count_ref, code_ref, tile_ref)
    basis_kernel(0, (0,), nblk, freq_ref, feat_ref, out_ref, ft_ref, wide_ref)


def pair_sums(code_ref, pip_ref, basis_ref, w_ref, at, a):
    lhs, rhs = [], []
    for k in range(2):
        code = code_ref[at + k]
        lhs.append(basis_ref[lax.rem(lax.div(code, 256), 256)])
        w = w_ref[pl.ds(lax.div(code, 65536), 1), :]
        rhs.append((pip_ref[a, lax.rem(code, 256)].astype(F32) * w).astype(BF16))
    return dot(jnp.concatenate(lhs, 1), jnp.concatenate(rhs, 1), 1, 1)


def spread_weights(w_ref, *refs):
    rows = w_ref.shape[0] // 9 * 3
    w_ref[3 * rows :, :] = jnp.zeros((w_ref.shape[0] - 3 * rows, w_ref.shape[1]), F32)
    for i, ref in enumerate(refs):
        w = ref[...].astype(F32)[0:rows]
        w_ref[i * rows : (i + 1) * rows, :] = w if i < 2 else jnp.where(sides("ra")[1], w, 0.0)


def early_kernel(code_ref, pip_ref, basis_ref, w_own_ref, w_even_ref, after_ref, sum_ref, w_ref):
    nblk, _, blk, _ = pip_ref.shape
    spread_weights(w_ref, w_own_ref, w_even_ref)
    for a in range(nblk):
        total = None
        for p in range(0, FIRST, 2):
            part = pair_sums(code_ref, pip_ref, basis_ref, w_ref, a * FIRST + p, a)
            total = part if total is None else total + part
        sum_ref[a] = total


def pair_kernel(code_ref, pip_ref, basis_ref, own_ref, early_ref, w_own_ref, w_even_ref, w_odd_ref, out_ref, w_ref, sum_ref, done_ref, sems):
    nblk, slots, blk, _ = pip_ref.shape
    nfreq = out_ref.shape[0]
    half, steps = nblk * FIRST, (slots - FIRST) // 2
    spread_weights(w_ref, w_own_ref, w_even_ref, w_odd_ref)
    many = code_ref[half + nblk * slots]

    def finish(start_ref, count):
        copies = []
        for a in range(nblk):
            total = start_ref[a]
            for t in range(count):
                total = total + pair_sums(code_ref, pip_ref, basis_ref, w_ref, half + a * slots + 2 * t, a)
            folded = own_ref[a, 0:nfreq] * total[:nfreq] + own_ref[a, nfreq:] * total[nfreq:]
            done_ref[a] = (folded * w_ref[a : a + 1, :]).astype(BF16)
            copies.append(pltpu.make_async_copy(done_ref.at[a], out_ref.at[:, a * blk : (a + 1) * blk], sems.at[a]))
            copies[-1].start()
        for copy in copies:
            copy.wait()

    @pl.when(many > steps)
    def _():
        sum_ref[...] = early_ref[...]

        def step(t, _):
            for a in range(nblk):
                sum_ref[a] += pair_sums(code_ref, pip_ref, basis_ref, w_ref, half + a * slots + 2 * t, a)
            return _

        lax.fori_loop(steps, many, step, 0)
        finish(sum_ref, steps)

    pl.when(many == steps)(lambda: finish(early_ref, steps))
    pl.when(jnp.logical_and(many > 0, many < steps))(lambda: finish(early_ref, steps - 1))
    pl.when(many == 0)(lambda: finish(early_ref, 0))


def vm(shape, dtype):
    return pltpu.VMEM(shape, dtype)


def sm(shape):
    return pltpu.SMEM(shape, jnp.int32)


def per_device(completeness, stencil, features, frequencies, gal_cell, pip, pair_src, pair_count):
    bands, nx, ny = completeness.shape
    feats, galaxies = features.shape
    nfreq = frequencies.shape[1]
    nblk, slots, blk, _ = pip.shape
    n = bands * nx
    two = 2 * bands

    def call(body, out, args, anys=(), scratch=(), name=None, aliases=None, cost=1, scalars=()):
        return pl.pallas_call(
            body, out_shape=out, in_specs=[SMEM] * len(scalars) + [VMEM] * len(args) + [ANY] * len(anys),
            out_specs=jax.tree.map(lambda x: SMEM if x.memory_space == pltpu.SMEM else VMEM, out),
            scratch_shapes=scratch, compiler_params=params(), input_output_aliases=aliases or {}, name=name,
            cost_estimate=pl.CostEstimate(flops=cost, bytes_accessed=1, transcendentals=0),
        )(*scalars, *args, *anys)

    cells = gal_cell.reshape(1, galaxies)
    given = (completeness, cells, stencil, features, frequencies, pair_src, pair_count)
    kept = tuple(vm(x.shape, x.dtype) for x in given[1:5]) + tuple(sm(x.shape) for x in given[5:])
    rim, rows, hit, cells, stencil, features, frequencies, pair_src, pair_count = pl.pallas_call(
        rim_kernel, out_shape=(vm((RIM, 128), BF16), vm((n, ny), F32), vm((n, galaxies), BF16)) + kept,
        in_specs=[HBM] * len(given), out_specs=(VMEM,) * 7 + (SMEM,) * 2, compiler_params=params(), name="rim",
        scratch_shapes=[pltpu.VMEM(completeness.shape, F32), pltpu.SemaphoreType.DMA((len(given) + 3,))],
    )(*[pltpu.with_memory_space_constraint(x, pltpu.HBM) for x in given])
    tables = (vm((stencil.shape[0] * bands, ny), F32), vm((5 * RIM, n), F32))
    rim, taps, lane_taps = call(
        functools.partial(ahead_kernel, bands, nx, ny), (vm((RIM, 128), BF16), *tables), (rim, stencil), (),
        [pltpu.VMEM((32, 128), F32)], "ahead",
    )
    d_odd, d_even = exchange("dec", rim, rim)
    f_odd, f_even = exchange("dec", features, features)
    taps, lane_taps = call(
        functools.partial(ready_kernel, bands, nx, ny), tables, (stencil,), (rim, taps, lane_taps),
        [pltpu.VMEM((32, 128), F32)], "ready", {2: 0, 3: 1},
    )
    inner = call(
        functools.partial(inner_kernel, bands), vm((n, ny), F32), (rows, taps), (), (), "inner",
    )
    to_odd, to_even = call(
        row_kernel, (vm((two + RIM, ny), BF16),) * 2, (rows, d_odd, d_even), (inner,), name="rows", cost=LONG
    )
    r_odd, r_even = exchange("ra", to_odd, to_even)
    even_side = call(
        functools.partial(even_side_kernel, bands), vm((8, galaxies), F32),
        (inner, d_odd, d_even, r_even, taps, lane_taps, hit, cells), (),
        [pltpu.VMEM((n, ny), F32)], "even_side",
    )
    column = call(stack_rows_kernel, vm((3 * feats, galaxies), BF16), (features, f_odd, f_even), (even_side,), name="stack_features")
    c_odd, c_even = exchange("ra", column, column)

    blocks = vm((9 * nblk, 2 * nfreq, blk), BF16)
    scratch = [pltpu.VMEM((nfreq, feats), BF16)]
    table, own_wide, code = call(
        functools.partial(own_basis_kernel, nblk), (blocks, vm((nblk, 2 * nfreq, blk), F32), sm((nblk * (FIRST + slots) + 2,))), (frequencies, features), (column,),
        scratch + [pltpu.SMEM((9,), jnp.int32)], "own_basis", scalars=(pair_src, pair_count),
    )

    def basis(part, tiles, array, buffer, after):
        def body(freq_ref, feat_ref, *refs):
            basis_kernel(3 * part * nblk, tiles, nblk, freq_ref, feat_ref, *refs[-2:])

        return call(body, blocks, (frequencies, array), (after, buffer), scratch, "basis%d" % part, {3: 0})

    weight, table = call(
        functools.partial(weight_kernel, bands), (vm((3 * nblk + 15 & -16, blk), BF16), blocks),
        (even_side, r_odd, taps, lane_taps, hit, cells), (table,),
        [pltpu.VMEM((two, ny), F32)], "weight", {6: 1}, LONG,
    )
    w_odd, w_even = exchange("dec", weight, weight)
    table = basis(0, (1, 2), column, table, weight)
    table = basis(1, (0, 1, 2), c_even, table, weight)
    w_column, table = call(
        functools.partial(stack_weight_kernel, nblk), (vm(weight.shape, BF16), blocks), (weight, w_odd, w_even), (table,), name="stack_weights",
        aliases={3: 1},
    )
    x_odd, x_even = exchange("ra", w_column, w_column)
    early = call(
        early_kernel, vm((nblk, 2 * nfreq, blk), F32), (pip, table, w_column, x_even), (w_column,),
        [pltpu.VMEM((9 * nblk + 4, blk), F32)], "early_pairs", scalars=(code,),
    )
    table = basis(2, (0, 1, 2), c_odd, table, early)
    return pl.pallas_call(
        pair_kernel, out_shape=jax.ShapeDtypeStruct((nfreq, galaxies), BF16), in_specs=[SMEM] + [VMEM] * 7, out_specs=ANY,
        scratch_shapes=[
            pltpu.VMEM((9 * nblk + 4, blk), F32), pltpu.VMEM((nblk, 2 * nfreq, blk), F32),
            pltpu.VMEM((nblk, nfreq, blk), BF16), pltpu.SemaphoreType.DMA((nblk,)),
        ],
        compiler_params=params(), name="pairs",
    )(code, pip, table, own_wide, early, w_column, x_even, x_odd)


def solution(mesh):
    in_specs = (
        P(None, "ra", "dec"),
        P(),
        P(None, ("ra", "dec")),
        P(),
        P(("ra", "dec")),
        P(("ra", "dec"), None, None, None),
        P(("ra", "dec"), None),
        P(("ra", "dec")),
    )
    out_specs = P(None, ("ra", "dec"))
    return jax.shard_map(per_device, mesh=mesh, in_specs=in_specs, out_specs=out_specs, check_vma=False)
```

```python
import functools
import math

import jax
import jax.numpy as jnp
from jax import lax
from jax.experimental import pallas as pl
from jax.experimental.pallas import tpu as pltpu
from jax.sharding import PartitionSpec as P

BF16 = jnp.bfloat16
F32 = jnp.float32
LONG = 1 << 36
FIRST = 6
RIM = 16

VMEM = pl.BlockSpec(memory_space=pltpu.VMEM)
SMEM = pl.BlockSpec(memory_space=pltpu.SMEM)
ANY = pl.BlockSpec(memory_space=pl.ANY)
HBM = pl.BlockSpec(memory_space=pltpu.HBM)

COS = (0.99995979, -19.73104169, 64.67343113, -82.40355036, 45.64655658)
SIN = (6.2830558, -41.33121431, 81.36681529, -74.47800454, 32.7814008)


def params(limit=None, **kw):
    return pltpu.CompilerParams(vmem_limit_bytes=limit or (16 << 20), **kw)


def swap(axis, odd, payload):
    ra, dec = lax.axis_size("ra"), lax.axis_size("dec")
    here = (lambda r, d: r * dec + d) if axis == "ra" else (lambda d, r: r * dec + d)
    count, other = (ra, dec) if axis == "ra" else (dec, ra)
    pairs = [(here(i, k), here(i + 1, k)) for i in range(odd, count - 1, 2) for k in range(other)]
    busy = {i for pair in pairs for i in pair}
    for i in (0, count - 1):
        ends = [(here(i, k), here(i, k + 1)) for k in range(0, other - 1, 2)]
        pairs += [pair for pair in ends if not busy & set(pair)]
    return lax.ppermute(payload, ("ra", "dec"), sorted(pairs + [(b, a) for a, b in pairs]))


def exchange(axis, odd_payload, even_payload):
    if axis == "ra":
        even = swap(axis, 0, even_payload)
        return swap(axis, 1, odd_payload), even
    odd = swap(axis, 1, odd_payload)
    return odd, swap(axis, 0, even_payload)


def sides(axis):
    i, n = lax.axis_index(axis), lax.axis_size(axis)
    odd = lax.rem(i, 2) == 1
    return odd, jnp.logical_and(i > 0, jnp.logical_not(jnp.logical_and(odd, i == n - 1)))


def dot(a, b, ca, cb):
    return lax.dot_general(a, b, (((ca,), (cb,)), ((), ())), preferred_element_type=F32)


def rim_kernel(*refs):
    count = (len(refs) - 4) // 2
    given, (rim_ref, rows_ref, hit_ref), kept = refs[:count], refs[count : count + 3], refs[count + 3 : -2]
    comp_ref, sems = refs[-2:]
    bands, nx, ny = comp_ref.shape
    parts = [pl.ds(at, bands // 4) for at in range(0, bands, bands // 4)]
    others = list(zip(given[1:], kept, strict=True))
    pairs = others[:1] + [(given[0].at[part], comp_ref.at[part]) for part in parts] + others[1:]
    copies = [pltpu.make_async_copy(a, b, sems.at[i]) for i, (a, b) in enumerate(pairs)]
    for copy in copies:
        copy.start()
    row = lax.broadcasted_iota(jnp.int32, (8, ny), 0)
    lane = lax.broadcasted_iota(jnp.int32, (8, ny), 1)
    pick = ((row < 2) & (lane == row)) | ((row >= 2) & (row < 4) & (lane == row + ny - 4))
    copies[0].wait()
    cell = kept[0][...]
    slot = (cell // ny % nx) * bands + cell // (nx * ny)
    hit = lax.broadcasted_iota(jnp.int32, hit_ref.shape, 0) == slot
    hit_ref[...] = jnp.where(hit, 1.0, 0.0).astype(BF16)
    for copy, part in zip(copies[1:], parts):
        copy.wait()
        for x in range(nx):
            at = x * bands + part.start
            rows_ref[at : at + part.size, :] = comp_ref[part.start : part.start + part.size, x, :]
    rim = dot(pick.astype(F32).astype(BF16), rows_ref[...].astype(BF16), 1, 1)
    rim_ref[...] = jnp.concatenate([rim[0:4, at : at + 128] for at in range(0, bands * nx, 128)], 0).astype(BF16)
    for copy in copies[len(parts) + 1 :]:
        copy.wait()


def list_slots(nblk, src_ref, count_ref, code_ref, tile_ref):
    own, slots = src_ref.shape
    blocks, half = 9 * nblk, own * FIRST
    ra_odd, _ = sides("ra")
    dec_odd, _ = sides("dec")
    ra_up, dec_up = jnp.where(ra_odd, 2, 1), jnp.where(dec_odd, 1, 2)
    ra, dec = lax.axis_index("ra"), lax.axis_index("dec")
    last_ra, last_dec = lax.axis_size("ra") - 1, lax.axis_size("dec") - 1
    for i, (ra_at, ra_in) in enumerate(((3 - ra_up, ra > 0), (0, ra >= 0), (ra_up, ra < last_ra))):
        for j, (dec_at, dec_in) in enumerate(((3 - dec_up, dec > 0), (0, dec >= 0), (dec_up, dec < last_dec))):
            tile_ref[3 * i + j] = jnp.where(jnp.logical_and(ra_in, dec_in), (3 * ra_at + dec_at) * nblk, -blocks)
    for i in range(half + own * slots):
        code_ref[i] = blocks * 65536
    steps = jnp.int32(0)
    for a in range(own):
        early, late = jnp.int32(0), jnp.int32(0)
        for p in range(slots):
            s = src_ref[a, p]
            at = tile_ref[lax.div(s, nblk)] + lax.rem(s, nblk)
            live = jnp.logical_and(p < count_ref[a], at >= 0)
            soon = jnp.logical_and(at < 6 * nblk, early < FIRST)
            to = jnp.where(soon, a * FIRST + early, half + a * slots + late)
            code_ref[jnp.where(live, to, half + own * slots + 1)] = p + at * (256 + 65536)
            early = early + jnp.where(jnp.logical_and(live, soon), 1, 0)
            late = late + jnp.where(jnp.logical_and(live, jnp.logical_not(soon)), 1, 0)
        steps = jnp.maximum(steps, lax.div(late + 1, 2))
    code_ref[half + own * slots] = steps


def leads():
    return jnp.logical_and(lax.axis_index("ra") < 2, lax.axis_index("dec") == 0)


def ahead_kernel(bands, nx, ny, rim_in_ref, stencil_ref, rim_ref, taps_ref, lane_taps_ref, st_ref):
    rim_ref[...] = rim_in_ref[...]
    pl.when(leads())(lambda: ready(bands, nx, ny, stencil_ref, taps_ref, lane_taps_ref, st_ref))


def ready_kernel(bands, nx, ny, stencil_ref, rim_ref, taps_in_ref, lane_taps_in_ref, taps_ref, lane_taps_ref, st_ref):
    late = jnp.logical_not(leads())
    pl.when(late)(lambda: ready(bands, nx, ny, stencil_ref, taps_ref, lane_taps_ref, st_ref))


def ready(bands, nx, ny, stencil_ref, taps_ref, lane_taps_ref, st_ref):
    st_ref[...] = jnp.zeros_like(st_ref)
    count = stencil_ref.shape[0]
    st_ref[0:count, 0:bands] = stencil_ref[...]
    st_ref[0:count, bands : 2 * bands] = stencil_ref[...]
    by_band = st_ref[...].T
    for k in range(count):
        taps_ref[k * bands : (k + 1) * bands, :] = jnp.broadcast_to(by_band[0:bands, k : k + 1], (bands, ny))
    along = jnp.concatenate([st_ref[...]] * (nx // 2), 1)
    lane_taps_ref[...] = jnp.zeros_like(lane_taps_ref)
    for a in range(5):
        for row, c in ((0, 0), (1, 0), (2, 4), (3, 3), (8, 1), (11, 4)):
            lane_taps_ref[16 * a + row : 16 * a + row + 1, :] = along[5 * a + c : 5 * a + c + 1, :]


def row_kernel(rows_ref, odd_ref, even_ref, after_ref, to_odd_ref, to_even_ref):
    n = rows_ref.shape[0]
    two = to_odd_ref.shape[0] - RIM
    is_odd, _ = sides("ra")

    def put(ref, start):
        ref[0:two, :] = rows_ref[start : start + two, :].astype(BF16)
        at = start // 128 * 4
        edges = [r[...].astype(F32)[at : at + 4] for r in (odd_ref, even_ref)]
        ref[two:, :] = jnp.concatenate([*edges, jnp.zeros((RIM - 8, 128), F32)], 0).astype(BF16)

    @pl.when(is_odd)
    def _():
        put(to_odd_ref, n - two)
        put(to_even_ref, 0)

    @pl.when(jnp.logical_not(is_odd))
    def _():
        put(to_odd_ref, 0)
        put(to_even_ref, n - two)


def beside(odd, even):
    dec_odd, has_odd = sides("dec")
    odd = jnp.where(has_odd, odd, 0.0)
    before, after = jnp.where(dec_odd, even, odd), jnp.where(dec_odd, odd, even)
    none = jnp.zeros_like(before)
    return jnp.concatenate([before[2:4], after[0:1], after[0:1], none, before[3:4], none[0:2], after[1:2], none], 0)


def columns_of(rim):
    return jnp.concatenate([rim[at : at + 4] for at in range(0, RIM, 4)], 1)


def edge_sums(lane_taps_ref, bands, columns):
    width = columns.shape[1]
    size = lane_taps_ref.shape[1]
    total = jnp.zeros((RIM, size), F32)
    for a in range(5):
        moved = columns if a == 0 else pltpu.roll(columns, width - a * bands, 1)
        total = total + lane_taps_ref[16 * a : 16 * a + 16, :] * moved[:, 0:size]
    return total[0:8] + total[8:16]


def shifts(cells):
    ny = cells.shape[1]
    at = lax.broadcasted_iota(jnp.int32, cells.shape, 1)
    return (
        jnp.where(at < 2, 0.0, pltpu.roll(cells, 2, 1)),
        jnp.where(at < 1, 0.0, pltpu.roll(cells, 1, 1)),
        cells,
        jnp.where(at > ny - 2, 0.0, pltpu.roll(cells, ny - 1, 1)),
        jnp.where(at > ny - 3, 0.0, pltpu.roll(cells, ny - 2, 1)),
    )


def split(x):
    high = x.astype(BF16)
    return high, (x - high.astype(F32)).astype(BF16)


def at_column(table, hits, cell):
    high, low = split(table)
    found = dot(high, hits, 0, 0) + dot(low, hits, 0, 0)
    at = lax.broadcasted_iota(jnp.int32, found.shape, 0) == cell % table.shape[1]
    return jnp.sum(jnp.where(at, found, 0.0), axis=0, keepdims=True)


def at_edge(edges, hits, cell, ny):
    found = dot(jnp.concatenate(split(edges), 0), hits, 1, 0)
    found = found[0:8] + found[8:16]
    y = cell % ny
    row = jnp.where(y < 2, y, jnp.where(y > ny - 3, y - (ny - 4), 8))
    return jnp.sum(jnp.where(lax.broadcasted_iota(jnp.int32, found.shape, 0) == row, found, 0.0), axis=0, keepdims=True)


def inner_kernel(bands, rows_ref, taps_ref, out_ref):
    n, ny = rows_ref.shape
    nx = n // bands
    for g in range(0, bands, 8):
        cells = [shifts(rows_ref[x * bands + g : x * bands + g + 8, :]) for x in range(nx)]
        accs = [jnp.zeros((8, ny), F32) for _ in range(nx)]
        for c in range(5):
            for a in range(5):
                w = taps_ref[(5 * a + c) * bands + g : (5 * a + c) * bands + g + 8, :]
                for x in range(nx):
                    if 0 <= x + a - 2 < nx:
                        accs[x] = accs[x] + w * cells[x + a - 2][c]
        for x in range(nx):
            out_ref[x * bands + g : x * bands + g + 8, :] = accs[x]


def side_sums(rows_ref, taps_ref, bands, up, there, put):
    parts = (((4, 0),), ((3, 0), (4, 1))) if up else (((0, 0), (1, 1)), ((0, 1),))
    for g in range(0, bands, 16):
        pairs = [rows_ref[e * bands + g : e * bands + g + 16, :].astype(F32) for e in range(2)]
        for h in (0, 8):
            cells = [shifts(jnp.where(there, pair[h : h + 8], 0.0)) for pair in pairs]
            for x, terms in enumerate(parts):
                acc = None
                for a, e in terms:
                    for c in range(5):
                        tap = (5 * a + c) * bands + g + h
                        term = taps_ref[tap : tap + 8, :] * cells[e][c]
                        acc = term if acc is None else acc + term
                put(x * bands + g + h, acc)


def even_side_kernel(bands, inner_ref, odd_ref, even_ref, rows_ref, taps_ref, lane_taps_ref, hit_ref, cell_ref, out_ref, sum_ref):
    n, ny = inner_ref.shape
    two = 2 * bands
    ra_odd, _ = sides("ra")
    sum_ref[...] = inner_ref[...]

    def add_from(start):
        def put(at, value):
            sum_ref[start + at : start + at + 8, :] += value

        return put

    pl.when(ra_odd)(lambda: side_sums(rows_ref, taps_ref, bands, False, True, add_from(0)))
    pl.when(jnp.logical_not(ra_odd))(lambda: side_sums(rows_ref, taps_ref, bands, True, True, add_from(n - two)))

    own = beside(columns_of(odd_ref[...].astype(F32)), columns_of(even_ref[...].astype(F32)))
    rims = rows_ref[two : two + RIM, :].astype(F32)
    side = beside(rims[0:4], rims[4:8])
    columns = jnp.concatenate([jnp.where(ra_odd, side, 0.0), own, jnp.where(ra_odd, 0.0, side)], 1)
    edges = edge_sums(lane_taps_ref, bands, columns)
    cell = cell_ref[...]
    value = at_column(sum_ref[...], hit_ref[...], cell) + at_edge(edges, hit_ref[...], cell, ny)
    out_ref[...] = jnp.broadcast_to(value, out_ref.shape)


def weight_kernel(bands, even_side_ref, rows_ref, taps_ref, lane_taps_ref, hit_ref, cell_ref, basis_in_ref, out_ref, basis_ref, sum_ref):
    two, ny = sum_ref.shape
    n = hit_ref.shape[0]
    ra_odd, has_odd = sides("ra")

    def put(at, value):
        sum_ref[at : at + 8, :] = value

    pl.when(ra_odd)(lambda: side_sums(rows_ref, taps_ref, bands, True, has_odd, put))
    pl.when(jnp.logical_not(ra_odd))(lambda: side_sums(rows_ref, taps_ref, bands, False, has_odd, put))

    rims = rows_ref[two : two + RIM, :].astype(F32)
    side = jnp.where(has_odd, beside(rims[0:4], rims[4:8]), 0.0)
    columns = jnp.concatenate([jnp.where(ra_odd, 0.0, side), jnp.zeros((RIM, n), F32), jnp.where(ra_odd, side, 0.0)], 1)
    edges = edge_sums(lane_taps_ref, bands, columns)
    edges = jnp.where(ra_odd, edges[:, n - two :], edges[:, 0:two])
    hits = hit_ref[pl.ds(pl.multiple_of(jnp.where(ra_odd, n - two, 0), two), two), :]
    cell = cell_ref[...]
    value = even_side_ref[0:1, :] + at_column(sum_ref[...], hits, cell) + at_edge(edges, hits, cell, ny)
    weights = lax.rsqrt(value)
    blk = out_ref.shape[1]
    rows = [weights[:, at : at + blk] for at in range(0, weights.shape[1], blk)]
    out_ref[...] = jnp.concatenate([*rows, jnp.zeros((out_ref.shape[0] - len(rows), blk), F32)], 0).astype(BF16)


def stack_weight_kernel(nblk, own_ref, odd_ref, even_ref, basis_in_ref, out_ref, basis_ref):
    _, has_odd = sides("dec")
    own, odd, even = (ref[...].astype(F32)[0:nblk] for ref in (own_ref, odd_ref, even_ref))
    none = jnp.zeros((out_ref.shape[0] - 3 * nblk, out_ref.shape[1]), F32)
    out_ref[...] = jnp.concatenate([own, jnp.where(has_odd, odd, 0.0), even, none], 0).astype(BF16)


def stack_rows_kernel(a_ref, b_ref, c_ref, after_ref, out_ref):
    n = a_ref.shape[0]
    out_ref[0:n, :] = a_ref[...]
    out_ref[n : 2 * n, :] = b_ref[...]
    out_ref[2 * n :, :] = c_ref[...]


def sincos(theta):
    turns = theta * (0.5 / math.pi)
    magic = 12582912.0
    r = turns - ((turns + magic) - magic)
    z = r * r
    c = jnp.full_like(z, COS[-1])
    for k in COS[-2::-1]:
        c = c * z + k
    s = jnp.full_like(z, SIN[-1])
    for k in SIN[-2::-1]:
        s = s * z + k
    return c, s * r


def basis_kernel(first, tiles, nblk, freq_ref, feat_ref, out_ref, ft_ref):
    feats, nfreq = freq_ref.shape
    blk = out_ref.shape[2]
    ft_ref[...] = freq_ref[...].astype(F32).T.astype(BF16)

    def work(t):
        for b in range(nblk):
            c, s = sincos(dot(ft_ref[...], feat_ref[t * feats : (t + 1) * feats, b * blk : (b + 1) * blk], 1, 0))
            out_ref[first + t * nblk + b, 0:nfreq, :] = c.astype(BF16)
            out_ref[first + t * nblk + b, nfreq:, :] = s.astype(BF16)

    def inside():
        for t in tiles:
            if t != 1:
                work(t)
        if 1 in tiles:
            pl.when(sides("dec")[1])(functools.partial(work, 1))

    if first == 6 * nblk:
        pl.when(sides("ra")[1])(inside)
    else:
        inside()


def own_basis_kernel(nblk, src_ref, count_ref, freq_ref, feat_ref, after_ref, out_ref, code_ref, ft_ref, tile_ref):
    list_slots(nblk, src_ref, count_ref, code_ref, tile_ref)
    basis_kernel(0, (0,), nblk, freq_ref, feat_ref, out_ref, ft_ref)


def pair_sums(code_ref, pip_ref, basis_ref, w_ref, at, a):
    lhs, rhs = [], []
    for k in range(2):
        code = code_ref[at + k]
        lhs.append(basis_ref[lax.rem(lax.div(code, 256), 256)])
        w = w_ref[pl.ds(lax.div(code, 65536), 1), :]
        rhs.append((pip_ref[a, lax.rem(code, 256)].astype(F32) * w).astype(BF16))
    return dot(jnp.concatenate(lhs, 1), jnp.concatenate(rhs, 1), 1, 1)


def spread_weights(w_ref, *refs):
    rows = w_ref.shape[0] // 9 * 3
    w_ref[3 * rows :, :] = jnp.zeros((w_ref.shape[0] - 3 * rows, w_ref.shape[1]), F32)
    for i, ref in enumerate(refs):
        w = ref[...].astype(F32)[0:rows]
        w_ref[i * rows : (i + 1) * rows, :] = w if i < 2 else jnp.where(sides("ra")[1], w, 0.0)


def early_kernel(code_ref, pip_ref, basis_ref, w_own_ref, w_even_ref, after_ref, sum_ref, w_ref):
    nblk, _, blk, _ = pip_ref.shape
    spread_weights(w_ref, w_own_ref, w_even_ref)
    for a in range(nblk):
        total = None
        for p in range(0, FIRST, 2):
            part = pair_sums(code_ref, pip_ref, basis_ref, w_ref, a * FIRST + p, a)
            total = part if total is None else total + part
        sum_ref[a] = total


def pair_kernel(code_ref, pip_ref, basis_ref, early_ref, w_own_ref, w_even_ref, w_odd_ref, out_ref, w_ref, sum_ref, done_ref, sems):
    nblk, slots, blk, _ = pip_ref.shape
    nfreq = out_ref.shape[0]
    half, steps = nblk * FIRST, (slots - FIRST) // 2
    spread_weights(w_ref, w_own_ref, w_even_ref, w_odd_ref)
    many = code_ref[half + nblk * slots]

    def finish(start_ref, count):
        copies = []
        for a in range(nblk):
            total = start_ref[a]
            for t in range(count):
                total = total + pair_sums(code_ref, pip_ref, basis_ref, w_ref, half + a * slots + 2 * t, a)
            own = basis_ref[a].astype(F32)
            folded = own[:nfreq] * total[:nfreq] + own[nfreq:] * total[nfreq:]
            done_ref[a] = (folded * w_ref[a : a + 1, :]).astype(BF16)
            copies.append(pltpu.make_async_copy(done_ref.at[a], out_ref.at[:, a * blk : (a + 1) * blk], sems.at[a]))
            copies[-1].start()
        for copy in copies:
            copy.wait()

    @pl.when(many > steps + 1)
    def _():
        sum_ref[...] = early_ref[...]

        def step(t, _):
            for a in range(nblk):
                sum_ref[a] += pair_sums(code_ref, pip_ref, basis_ref, w_ref, half + a * slots + 2 * t, a)
            return _

        lax.fori_loop(steps, many, step, 0)
        finish(sum_ref, steps)

    for count in range(steps + 2):
        pl.when(many == count)(functools.partial(finish, early_ref, count))


def vm(shape, dtype):
    return pltpu.VMEM(shape, dtype)


def sm(shape):
    return pltpu.SMEM(shape, jnp.int32)


def per_device(completeness, stencil, features, frequencies, gal_cell, pip, pair_src, pair_count):
    bands, nx, ny = completeness.shape
    feats, galaxies = features.shape
    nfreq = frequencies.shape[1]
    nblk, slots, blk, _ = pip.shape
    n = bands * nx
    two = 2 * bands

    def call(body, out, args, anys=(), scratch=(), name=None, aliases=None, cost=1, scalars=()):
        return pl.pallas_call(
            body, out_shape=out, in_specs=[SMEM] * len(scalars) + [VMEM] * len(args) + [ANY] * len(anys),
            out_specs=jax.tree.map(lambda x: SMEM if x.memory_space == pltpu.SMEM else VMEM, out),
            scratch_shapes=scratch, compiler_params=params(), input_output_aliases=aliases or {}, name=name,
            cost_estimate=pl.CostEstimate(flops=cost, bytes_accessed=1, transcendentals=0),
        )(*scalars, *args, *anys)

    cells = gal_cell.reshape(1, galaxies)
    given = (completeness, cells, stencil, features, frequencies, pair_src, pair_count)
    kept = tuple(vm(x.shape, x.dtype) for x in given[1:5]) + tuple(sm(x.shape) for x in given[5:])
    rim, rows, hit, cells, stencil, features, frequencies, pair_src, pair_count = pl.pallas_call(
        rim_kernel, out_shape=(vm((RIM, 128), BF16), vm((n, ny), F32), vm((n, galaxies), BF16)) + kept,
        in_specs=[HBM] * len(given), out_specs=(VMEM,) * 7 + (SMEM,) * 2, compiler_params=params(), name="rim",
        scratch_shapes=[pltpu.VMEM(completeness.shape, F32), pltpu.SemaphoreType.DMA((len(given) + 3,))],
    )(*[pltpu.with_memory_space_constraint(x, pltpu.HBM) for x in given])
    tables = (vm((stencil.shape[0] * bands, ny), F32), vm((5 * RIM, n), F32))
    rim, taps, lane_taps = call(
        functools.partial(ahead_kernel, bands, nx, ny), (vm((RIM, 128), BF16), *tables), (rim, stencil), (),
        [pltpu.VMEM((32, 128), F32)], "ahead",
    )
    d_odd, d_even = exchange("dec", rim, rim)
    f_odd, f_even = exchange("dec", features, features)
    taps, lane_taps = call(
        functools.partial(ready_kernel, bands, nx, ny), tables, (stencil,), (rim, taps, lane_taps),
        [pltpu.VMEM((32, 128), F32)], "ready", {2: 0, 3: 1},
    )
    inner = call(
        functools.partial(inner_kernel, bands), vm((n, ny), F32), (rows, taps), (), (), "inner",
    )
    to_odd, to_even = call(
        row_kernel, (vm((two + RIM, ny), BF16),) * 2, (rows, d_odd, d_even), (inner,), name="rows", cost=LONG
    )
    r_odd, r_even = exchange("ra", to_odd, to_even)
    even_side = call(
        functools.partial(even_side_kernel, bands), vm((8, galaxies), F32),
        (inner, d_odd, d_even, r_even, taps, lane_taps, hit, cells), (),
        [pltpu.VMEM((n, ny), F32)], "even_side",
    )
    column = call(stack_rows_kernel, vm((3 * feats, galaxies), BF16), (features, f_odd, f_even), (even_side,), name="stack_features")
    c_even = swap("ra", 0, column)
    c_odd = swap("ra", 1, column)

    blocks = vm((9 * nblk, 2 * nfreq, blk), BF16)
    scratch = [pltpu.VMEM((nfreq, feats), BF16)]
    table, code = call(
        functools.partial(own_basis_kernel, nblk), (blocks, sm((nblk * (FIRST + slots) + 2,))), (frequencies, features), (column,),
        scratch + [pltpu.SMEM((9,), jnp.int32)], "own_basis", scalars=(pair_src, pair_count),
    )

    def basis(part, tiles, array, buffer, after):
        def body(freq_ref, feat_ref, *refs):
            basis_kernel(3 * part * nblk, tiles, nblk, freq_ref, feat_ref, *refs[-2:])

        return call(body, blocks, (frequencies, array), (after, buffer), scratch, "basis%d" % part, {3: 0})

    weight, table = call(
        functools.partial(weight_kernel, bands), (vm((3 * nblk + 15 & -16, blk), BF16), blocks),
        (even_side, r_odd, taps, lane_taps, hit, cells), (table,),
        [pltpu.VMEM((two, ny), F32)], "weight", {6: 1}, LONG,
    )
    w_odd, w_even = exchange("dec", weight, weight)
    table = basis(0, (1, 2), column, table, weight)
    table = basis(1, (0, 1, 2), c_even, table, weight)
    w_column, table = call(
        functools.partial(stack_weight_kernel, nblk), (vm(weight.shape, BF16), blocks), (weight, w_odd, w_even), (table,), name="stack_weights",
        aliases={3: 1},
    )
    x_odd, x_even = exchange("ra", w_column, w_column)
    early = call(
        early_kernel, vm((nblk, 2 * nfreq, blk), F32), (pip, table, w_column, x_even), (w_column,),
        [pltpu.VMEM((9 * nblk + 4, blk), F32)], "early_pairs", scalars=(code,),
    )
    table = basis(2, (0, 1, 2), c_odd, table, early)
    return pl.pallas_call(
        pair_kernel, out_shape=jax.ShapeDtypeStruct((nfreq, galaxies), BF16), in_specs=[SMEM] + [VMEM] * 6, out_specs=ANY,
        scratch_shapes=[
            pltpu.VMEM((9 * nblk + 4, blk), F32), pltpu.VMEM((nblk, 2 * nfreq, blk), F32),
            pltpu.VMEM((nblk, nfreq, blk), BF16), pltpu.SemaphoreType.DMA((nblk,)),
        ],
        compiler_params=params(), name="pairs",
    )(code, pip, table, early, w_column, x_even, x_odd)


def solution(mesh):
    in_specs = (
        P(None, "ra", "dec"),
        P(),
        P(None, ("ra", "dec")),
        P(),
        P(("ra", "dec")),
        P(("ra", "dec"), None, None, None),
        P(("ra", "dec"), None),
        P(("ra", "dec")),
    )
    out_specs = P(None, ("ra", "dec"))
    return jax.shard_map(per_device, mesh=mesh, in_specs=in_specs, out_specs=out_specs, check_vma=False)
```

```python
import functools
import math

import jax
import jax.numpy as jnp
from jax import lax
from jax.experimental import pallas as pl
from jax.experimental.pallas import tpu as pltpu
from jax.sharding import PartitionSpec as P

BF16 = jnp.bfloat16
F32 = jnp.float32
LONG = 1 << 36
FIRST = 8
RIM = 16

VMEM = pl.BlockSpec(memory_space=pltpu.VMEM)
SMEM = pl.BlockSpec(memory_space=pltpu.SMEM)
ANY = pl.BlockSpec(memory_space=pl.ANY)
HBM = pl.BlockSpec(memory_space=pltpu.HBM)

COS = (0.99995979, -19.73104169, 64.67343113, -82.40355036, 45.64655658)
SIN = (6.2830558, -41.33121431, 81.36681529, -74.47800454, 32.7814008)


def params(limit=None, **kw):
    return pltpu.CompilerParams(vmem_limit_bytes=limit or (16 << 20), **kw)


def swap(axis, odd, payload):
    ra, dec = lax.axis_size("ra"), lax.axis_size("dec")
    here = (lambda r, d: r * dec + d) if axis == "ra" else (lambda d, r: r * dec + d)
    count, other = (ra, dec) if axis == "ra" else (dec, ra)
    pairs = [(here(i, k), here(i + 1, k)) for i in range(odd, count - 1, 2) for k in range(other)]
    busy = {i for pair in pairs for i in pair}
    for i in (0, count - 1):
        ends = [(here(i, k), here(i, k + 1)) for k in range(0, other - 1, 2)]
        pairs += [pair for pair in ends if not busy & set(pair)]
    return lax.ppermute(payload, ("ra", "dec"), sorted(pairs + [(b, a) for a, b in pairs]))


def exchange(axis, odd_payload, even_payload):
    if axis == "ra":
        even = swap(axis, 0, even_payload)
        return swap(axis, 1, odd_payload), even
    odd = swap(axis, 1, odd_payload)
    return odd, swap(axis, 0, even_payload)


def sides(axis):
    i, n = lax.axis_index(axis), lax.axis_size(axis)
    odd = lax.rem(i, 2) == 1
    return odd, jnp.logical_and(i > 0, jnp.logical_not(jnp.logical_and(odd, i == n - 1)))


def dot(a, b, ca, cb):
    return lax.dot_general(a, b, (((ca,), (cb,)), ((), ())), preferred_element_type=F32)


def rim_kernel(*refs):
    count = (len(refs) - 4) // 2
    given, (rim_ref, rows_ref, hit_ref), kept = refs[:count], refs[count : count + 3], refs[count + 3 : -2]
    comp_ref, sems = refs[-2:]
    bands, nx, ny = comp_ref.shape
    parts = [pl.ds(at, bands // 4) for at in range(0, bands, bands // 4)]
    others = list(zip(given[1:], kept, strict=True))
    pairs = others[:1] + [(given[0].at[part], comp_ref.at[part]) for part in parts] + others[1:]
    copies = [pltpu.make_async_copy(a, b, sems.at[i]) for i, (a, b) in enumerate(pairs)]
    for copy in copies:
        copy.start()
    row = lax.broadcasted_iota(jnp.int32, (8, ny), 0)
    lane = lax.broadcasted_iota(jnp.int32, (8, ny), 1)
    pick = ((row < 2) & (lane == row)) | ((row >= 2) & (row < 4) & (lane == row + ny - 4))
    copies[0].wait()
    cell = kept[0][...]
    slot = (cell // ny % nx) * bands + cell // (nx * ny)
    hit = lax.broadcasted_iota(jnp.int32, hit_ref.shape, 0) == slot
    hit_ref[...] = jnp.where(hit, 1.0, 0.0).astype(BF16)
    for copy, part in zip(copies[1:], parts):
        copy.wait()
        for x in range(nx):
            at = x * bands + part.start
            rows_ref[at : at + part.size, :] = comp_ref[part.start : part.start + part.size, x, :]
    rim = dot(pick.astype(F32).astype(BF16), rows_ref[...].astype(BF16), 1, 1)
    rim_ref[...] = jnp.concatenate([rim[0:4, at : at + 128] for at in range(0, bands * nx, 128)], 0).astype(BF16)
    for copy in copies[len(parts) + 1 :]:
        copy.wait()


def list_slots(nblk, src_ref, count_ref, code_ref, tile_ref):
    own, slots = src_ref.shape
    blocks, half = 9 * nblk, own * FIRST
    ra_odd, _ = sides("ra")
    dec_odd, _ = sides("dec")
    ra_up, dec_up = jnp.where(ra_odd, 2, 1), jnp.where(dec_odd, 1, 2)
    ra, dec = lax.axis_index("ra"), lax.axis_index("dec")
    last_ra, last_dec = lax.axis_size("ra") - 1, lax.axis_size("dec") - 1
    for i, (ra_at, ra_in) in enumerate(((3 - ra_up, ra > 0), (0, ra >= 0), (ra_up, ra < last_ra))):
        for j, (dec_at, dec_in) in enumerate(((3 - dec_up, dec > 0), (0, dec >= 0), (dec_up, dec < last_dec))):
            tile_ref[3 * i + j] = jnp.where(jnp.logical_and(ra_in, dec_in), (3 * ra_at + dec_at) * nblk, -blocks)
    for i in range(half + own * slots):
        code_ref[i] = blocks * 65536
    steps = jnp.int32(0)
    for a in range(own):
        early, late = jnp.int32(0), jnp.int32(0)
        for p in range(slots):
            s = src_ref[a, p]
            at = tile_ref[lax.div(s, nblk)] + lax.rem(s, nblk)
            live = jnp.logical_and(p < count_ref[a], at >= 0)
            soon = jnp.logical_and(at < 6 * nblk, early < FIRST)
            to = jnp.where(soon, a * FIRST + early, half + a * slots + late)
            code_ref[jnp.where(live, to, half + own * slots + 1)] = p + at * (256 + 65536)
            early = early + jnp.where(jnp.logical_and(live, soon), 1, 0)
            late = late + jnp.where(jnp.logical_and(live, jnp.logical_not(soon)), 1, 0)
        steps = jnp.maximum(steps, lax.div(late + 1, 2))
    code_ref[half + own * slots] = steps


def leads():
    return jnp.logical_and(lax.axis_index("ra") < 2, lax.axis_index("dec") == 0)


def ahead_kernel(bands, nx, ny, rim_in_ref, stencil_ref, rim_ref, taps_ref, lane_taps_ref, st_ref):
    rim_ref[...] = rim_in_ref[...]
    pl.when(leads())(lambda: ready(bands, nx, ny, stencil_ref, taps_ref, lane_taps_ref, st_ref))


def ready_kernel(bands, nx, ny, stencil_ref, rim_ref, taps_in_ref, lane_taps_in_ref, taps_ref, lane_taps_ref, st_ref):
    late = jnp.logical_not(leads())
    pl.when(late)(lambda: ready(bands, nx, ny, stencil_ref, taps_ref, lane_taps_ref, st_ref))


def ready(bands, nx, ny, stencil_ref, taps_ref, lane_taps_ref, st_ref):
    st_ref[...] = jnp.zeros_like(st_ref)
    count = stencil_ref.shape[0]
    st_ref[0:count, 0:bands] = stencil_ref[...]
    st_ref[0:count, bands : 2 * bands] = stencil_ref[...]
    by_band = st_ref[...].T
    for k in range(count):
        taps_ref[k * bands : (k + 1) * bands, :] = jnp.broadcast_to(by_band[0:bands, k : k + 1], (bands, ny))
    along = jnp.concatenate([st_ref[...]] * (nx // 2), 1)
    lane_taps_ref[...] = jnp.zeros_like(lane_taps_ref)
    for a in range(5):
        for row, c in ((0, 0), (1, 0), (2, 4), (3, 3), (8, 1), (11, 4)):
            lane_taps_ref[16 * a + row : 16 * a + row + 1, :] = along[5 * a + c : 5 * a + c + 1, :]


def row_kernel(rows_ref, odd_ref, even_ref, after_ref, to_odd_ref, to_even_ref):
    n = rows_ref.shape[0]
    two = to_odd_ref.shape[0] - RIM
    is_odd, _ = sides("ra")

    def put(ref, start):
        ref[0:two, :] = rows_ref[start : start + two, :].astype(BF16)
        at = start // 128 * 4
        edges = [r[...].astype(F32)[at : at + 4] for r in (odd_ref, even_ref)]
        ref[two:, :] = jnp.concatenate([*edges, jnp.zeros((RIM - 8, 128), F32)], 0).astype(BF16)

    @pl.when(is_odd)
    def _():
        put(to_odd_ref, n - two)
        put(to_even_ref, 0)

    @pl.when(jnp.logical_not(is_odd))
    def _():
        put(to_odd_ref, 0)
        put(to_even_ref, n - two)


def beside(odd, even):
    dec_odd, has_odd = sides("dec")
    odd = jnp.where(has_odd, odd, 0.0)
    before, after = jnp.where(dec_odd, even, odd), jnp.where(dec_odd, odd, even)
    none = jnp.zeros_like(before)
    return jnp.concatenate([before[2:4], after[0:1], after[0:1], none, before[3:4], none[0:2], after[1:2], none], 0)


def columns_of(rim):
    return jnp.concatenate([rim[at : at + 4] for at in range(0, RIM, 4)], 1)


def edge_sums(lane_taps_ref, bands, columns):
    width = columns.shape[1]
    size = lane_taps_ref.shape[1]
    total = jnp.zeros((RIM, size), F32)
    for a in range(5):
        moved = columns if a == 0 else pltpu.roll(columns, width - a * bands, 1)
        total = total + lane_taps_ref[16 * a : 16 * a + 16, :] * moved[:, 0:size]
    return total[0:8] + total[8:16]


def shifts(cells):
    ny = cells.shape[1]
    at = lax.broadcasted_iota(jnp.int32, cells.shape, 1)
    return (
        jnp.where(at < 2, 0.0, pltpu.roll(cells, 2, 1)),
        jnp.where(at < 1, 0.0, pltpu.roll(cells, 1, 1)),
        cells,
        jnp.where(at > ny - 2, 0.0, pltpu.roll(cells, ny - 1, 1)),
        jnp.where(at > ny - 3, 0.0, pltpu.roll(cells, ny - 2, 1)),
    )


def split(x):
    high = x.astype(BF16)
    return high, (x - high.astype(F32)).astype(BF16)


def at_column(table, hits, cell):
    high, low = split(table)
    found = dot(high, hits, 0, 0) + dot(low, hits, 0, 0)
    at = lax.broadcasted_iota(jnp.int32, found.shape, 0) == cell % table.shape[1]
    return jnp.sum(jnp.where(at, found, 0.0), axis=0, keepdims=True)


def at_edge(edges, hits, cell, ny):
    found = dot(jnp.concatenate(split(edges), 0), hits, 1, 0)
    found = found[0:8] + found[8:16]
    y = cell % ny
    row = jnp.where(y < 2, y, jnp.where(y > ny - 3, y - (ny - 4), 8))
    return jnp.sum(jnp.where(lax.broadcasted_iota(jnp.int32, found.shape, 0) == row, found, 0.0), axis=0, keepdims=True)


def inner_kernel(bands, rows_ref, taps_ref, out_ref):
    n, ny = rows_ref.shape
    nx = n // bands
    for g in range(0, bands, 8):
        cells = [shifts(rows_ref[x * bands + g : x * bands + g + 8, :]) for x in range(nx)]
        accs = [jnp.zeros((8, ny), F32) for _ in range(nx)]
        for c in range(5):
            for a in range(5):
                w = taps_ref[(5 * a + c) * bands + g : (5 * a + c) * bands + g + 8, :]
                for x in range(nx):
                    if 0 <= x + a - 2 < nx:
                        accs[x] = accs[x] + w * cells[x + a - 2][c]
        for x in range(nx):
            out_ref[x * bands + g : x * bands + g + 8, :] = accs[x]


def side_sums(rows_ref, taps_ref, bands, up, there, put):
    parts = (((4, 0),), ((3, 0), (4, 1))) if up else (((0, 0), (1, 1)), ((0, 1),))
    for g in range(0, bands, 16):
        pairs = [rows_ref[e * bands + g : e * bands + g + 16, :].astype(F32) for e in range(2)]
        for h in (0, 8):
            cells = [shifts(jnp.where(there, pair[h : h + 8], 0.0)) for pair in pairs]
            for x, terms in enumerate(parts):
                acc = None
                for a, e in terms:
                    for c in range(5):
                        tap = (5 * a + c) * bands + g + h
                        term = taps_ref[tap : tap + 8, :] * cells[e][c]
                        acc = term if acc is None else acc + term
                put(x * bands + g + h, acc)


def even_side_kernel(bands, inner_ref, odd_ref, even_ref, rows_ref, taps_ref, lane_taps_ref, hit_ref, cell_ref, out_ref, sum_ref):
    n, ny = inner_ref.shape
    two = 2 * bands
    ra_odd, _ = sides("ra")
    sum_ref[...] = inner_ref[...]

    def add_from(start):
        def put(at, value):
            sum_ref[start + at : start + at + 8, :] += value

        return put

    pl.when(ra_odd)(lambda: side_sums(rows_ref, taps_ref, bands, False, True, add_from(0)))
    pl.when(jnp.logical_not(ra_odd))(lambda: side_sums(rows_ref, taps_ref, bands, True, True, add_from(n - two)))

    own = beside(columns_of(odd_ref[...].astype(F32)), columns_of(even_ref[...].astype(F32)))
    rims = rows_ref[two : two + RIM, :].astype(F32)
    side = beside(rims[0:4], rims[4:8])
    columns = jnp.concatenate([jnp.where(ra_odd, side, 0.0), own, jnp.where(ra_odd, 0.0, side)], 1)
    edges = edge_sums(lane_taps_ref, bands, columns)
    cell = cell_ref[...]
    value = at_column(sum_ref[...], hit_ref[...], cell) + at_edge(edges, hit_ref[...], cell, ny)
    out_ref[...] = jnp.broadcast_to(value, out_ref.shape)


def weight_kernel(bands, even_side_ref, rows_ref, taps_ref, lane_taps_ref, hit_ref, cell_ref, basis_in_ref, out_ref, basis_ref, sum_ref):
    two, ny = sum_ref.shape
    n = hit_ref.shape[0]
    ra_odd, has_odd = sides("ra")

    def put(at, value):
        sum_ref[at : at + 8, :] = value

    pl.when(ra_odd)(lambda: side_sums(rows_ref, taps_ref, bands, True, has_odd, put))
    pl.when(jnp.logical_not(ra_odd))(lambda: side_sums(rows_ref, taps_ref, bands, False, has_odd, put))

    rims = rows_ref[two : two + RIM, :].astype(F32)
    side = jnp.where(has_odd, beside(rims[0:4], rims[4:8]), 0.0)
    columns = jnp.concatenate([jnp.where(ra_odd, 0.0, side), jnp.zeros((RIM, n), F32), jnp.where(ra_odd, side, 0.0)], 1)
    edges = edge_sums(lane_taps_ref, bands, columns)
    edges = jnp.where(ra_odd, edges[:, n - two :], edges[:, 0:two])
    hits = hit_ref[pl.ds(pl.multiple_of(jnp.where(ra_odd, n - two, 0), two), two), :]
    cell = cell_ref[...]
    value = even_side_ref[0:1, :] + at_column(sum_ref[...], hits, cell) + at_edge(edges, hits, cell, ny)
    weights = lax.rsqrt(value)
    blk = out_ref.shape[1]
    rows = [weights[:, at : at + blk] for at in range(0, weights.shape[1], blk)]
    out_ref[...] = jnp.concatenate([*rows, jnp.zeros((out_ref.shape[0] - len(rows), blk), F32)], 0).astype(BF16)


def stack_weight_kernel(nblk, own_ref, odd_ref, even_ref, basis_in_ref, out_ref, basis_ref):
    _, has_odd = sides("dec")
    own, odd, even = (ref[...].astype(F32)[0:nblk] for ref in (own_ref, odd_ref, even_ref))
    none = jnp.zeros((out_ref.shape[0] - 3 * nblk, out_ref.shape[1]), F32)
    out_ref[...] = jnp.concatenate([own, jnp.where(has_odd, odd, 0.0), even, none], 0).astype(BF16)


def stack_rows_kernel(a_ref, b_ref, c_ref, after_ref, out_ref):
    n = a_ref.shape[0]
    out_ref[0:n, :] = a_ref[...]
    out_ref[n : 2 * n, :] = b_ref[...]
    out_ref[2 * n :, :] = c_ref[...]


def sincos(theta):
    turns = theta * (0.5 / math.pi)
    magic = 12582912.0
    r = turns - ((turns + magic) - magic)
    z = r * r
    c = jnp.full_like(z, COS[-1])
    for k in COS[-2::-1]:
        c = c * z + k
    s = jnp.full_like(z, SIN[-1])
    for k in SIN[-2::-1]:
        s = s * z + k
    return c, s * r


def basis_kernel(first, tiles, nblk, freq_ref, feat_ref, out_ref, ft_ref):
    feats, nfreq = freq_ref.shape
    blk = out_ref.shape[2]
    ft_ref[...] = freq_ref[...].astype(F32).T.astype(BF16)

    def work(t):
        for b in range(nblk):
            c, s = sincos(dot(ft_ref[...], feat_ref[t * feats : (t + 1) * feats, b * blk : (b + 1) * blk], 1, 0))
            out_ref[first + t * nblk + b, 0:nfreq, :] = c.astype(BF16)
            out_ref[first + t * nblk + b, nfreq:, :] = s.astype(BF16)

    def inside():
        for t in tiles:
            if t != 1:
                work(t)
        if 1 in tiles:
            pl.when(sides("dec")[1])(functools.partial(work, 1))

    if first == 6 * nblk:
        pl.when(sides("ra")[1])(inside)
    else:
        inside()


def own_basis_kernel(nblk, src_ref, count_ref, freq_ref, feat_ref, after_ref, out_ref, code_ref, ft_ref, tile_ref):
    list_slots(nblk, src_ref, count_ref, code_ref, tile_ref)
    basis_kernel(0, (0,), nblk, freq_ref, feat_ref, out_ref, ft_ref)


def pair_sums(code_ref, pip_ref, basis_ref, w_ref, at, a):
    lhs, rhs = [], []
    for k in range(2):
        code = code_ref[at + k]
        lhs.append(basis_ref[lax.rem(lax.div(code, 256), 256)])
        w = w_ref[pl.ds(lax.div(code, 65536), 1), :]
        rhs.append((pip_ref[a, lax.rem(code, 256)].astype(F32) * w).astype(BF16))
    return dot(jnp.concatenate(lhs, 1), jnp.concatenate(rhs, 1), 1, 1)


def spread_weights(w_ref, *refs):
    rows = w_ref.shape[0] // 9 * 3
    w_ref[3 * rows :, :] = jnp.zeros((w_ref.shape[0] - 3 * rows, w_ref.shape[1]), F32)
    for i, ref in enumerate(refs):
        w = ref[...].astype(F32)[0:rows]
        w_ref[i * rows : (i + 1) * rows, :] = w if i < 2 else jnp.where(sides("ra")[1], w, 0.0)


def early_kernel(code_ref, pip_ref, basis_ref, w_own_ref, w_even_ref, after_ref, sum_ref, w_ref):
    nblk, _, blk, _ = pip_ref.shape
    spread_weights(w_ref, w_own_ref, w_even_ref)
    for a in range(nblk):
        total = None
        for p in range(0, FIRST, 2):
            part = pair_sums(code_ref, pip_ref, basis_ref, w_ref, a * FIRST + p, a)
            total = part if total is None else total + part
        sum_ref[a] = total


def pair_kernel(code_ref, pip_ref, basis_ref, early_ref, w_own_ref, w_even_ref, w_odd_ref, out_ref, w_ref, sum_ref, done_ref, sems):
    nblk, slots, blk, _ = pip_ref.shape
    nfreq = out_ref.shape[0]
    half, steps = nblk * FIRST, (slots - FIRST) // 2
    spread_weights(w_ref, w_own_ref, w_even_ref, w_odd_ref)
    many = code_ref[half + nblk * slots]

    def finish(start_ref, count):
        copies = []
        for a in range(nblk):
            total = start_ref[a]
            for t in range(count):
                total = total + pair_sums(code_ref, pip_ref, basis_ref, w_ref, half + a * slots + 2 * t, a)
            own = basis_ref[a].astype(F32)
            folded = own[:nfreq] * total[:nfreq] + own[nfreq:] * total[nfreq:]
            done_ref[a] = (folded * w_ref[a : a + 1, :]).astype(BF16)
            copies.append(pltpu.make_async_copy(done_ref.at[a], out_ref.at[:, a * blk : (a + 1) * blk], sems.at[a]))
            copies[-1].start()
        for copy in copies:
            copy.wait()

    @pl.when(many > steps + 2)
    def _():
        sum_ref[...] = early_ref[...]

        def step(t, _):
            for a in range(nblk):
                sum_ref[a] += pair_sums(code_ref, pip_ref, basis_ref, w_ref, half + a * slots + 2 * t, a)
            return _

        lax.fori_loop(steps, many, step, 0)
        finish(sum_ref, steps)

    for count in range(steps + 3):
        pl.when(many == count)(functools.partial(finish, early_ref, count))


def vm(shape, dtype):
    return pltpu.VMEM(shape, dtype)


def sm(shape):
    return pltpu.SMEM(shape, jnp.int32)


def per_device(completeness, stencil, features, frequencies, gal_cell, pip, pair_src, pair_count):
    bands, nx, ny = completeness.shape
    feats, galaxies = features.shape
    nfreq = frequencies.shape[1]
    nblk, slots, blk, _ = pip.shape
    n = bands * nx
    two = 2 * bands

    def call(body, out, args, anys=(), scratch=(), name=None, aliases=None, cost=1, scalars=()):
        return pl.pallas_call(
            body, out_shape=out, in_specs=[SMEM] * len(scalars) + [VMEM] * len(args) + [ANY] * len(anys),
            out_specs=jax.tree.map(lambda x: SMEM if x.memory_space == pltpu.SMEM else VMEM, out),
            scratch_shapes=scratch, compiler_params=params(), input_output_aliases=aliases or {}, name=name,
            cost_estimate=pl.CostEstimate(flops=cost, bytes_accessed=1, transcendentals=0),
        )(*scalars, *args, *anys)

    cells = gal_cell.reshape(1, galaxies)
    given = (completeness, cells, stencil, features, frequencies, pair_src, pair_count)
    kept = tuple(vm(x.shape, x.dtype) for x in given[1:5]) + tuple(sm(x.shape) for x in given[5:])
    rim, rows, hit, cells, stencil, features, frequencies, pair_src, pair_count = pl.pallas_call(
        rim_kernel, out_shape=(vm((RIM, 128), BF16), vm((n, ny), F32), vm((n, galaxies), BF16)) + kept,
        in_specs=[HBM] * len(given), out_specs=(VMEM,) * 7 + (SMEM,) * 2, compiler_params=params(), name="rim",
        scratch_shapes=[pltpu.VMEM(completeness.shape, F32), pltpu.SemaphoreType.DMA((len(given) + 3,))],
    )(*[pltpu.with_memory_space_constraint(x, pltpu.HBM) for x in given])
    tables = (vm((stencil.shape[0] * bands, ny), F32), vm((5 * RIM, n), F32))
    rim, taps, lane_taps = call(
        functools.partial(ahead_kernel, bands, nx, ny), (vm((RIM, 128), BF16), *tables), (rim, stencil), (),
        [pltpu.VMEM((32, 128), F32)], "ahead",
    )
    d_odd, d_even = exchange("dec", rim, rim)
    f_odd, f_even = exchange("dec", features, features)
    taps, lane_taps = call(
        functools.partial(ready_kernel, bands, nx, ny), tables, (stencil,), (rim, taps, lane_taps),
        [pltpu.VMEM((32, 128), F32)], "ready", {2: 0, 3: 1},
    )
    inner = call(
        functools.partial(inner_kernel, bands), vm((n, ny), F32), (rows, taps), (), (), "inner",
    )
    to_odd, to_even = call(
        row_kernel, (vm((two + RIM, ny), BF16),) * 2, (rows, d_odd, d_even), (inner,), name="rows", cost=LONG
    )
    r_odd, r_even = exchange("ra", to_odd, to_even)
    even_side = call(
        functools.partial(even_side_kernel, bands), vm((8, galaxies), F32),
        (inner, d_odd, d_even, r_even, taps, lane_taps, hit, cells), (),
        [pltpu.VMEM((n, ny), F32)], "even_side",
    )
    column = call(stack_rows_kernel, vm((3 * feats, galaxies), BF16), (features, f_odd, f_even), (even_side,), name="stack_features")
    c_even = swap("ra", 0, column)
    c_odd = swap("ra", 1, column)

    blocks = vm((9 * nblk, 2 * nfreq, blk), BF16)
    scratch = [pltpu.VMEM((nfreq, feats), BF16)]
    table, code = call(
        functools.partial(own_basis_kernel, nblk), (blocks, sm((nblk * (FIRST + slots) + 2,))), (frequencies, features), (column,),
        scratch + [pltpu.SMEM((9,), jnp.int32)], "own_basis", scalars=(pair_src, pair_count),
    )

    def basis(part, tiles, array, buffer, after):
        def body(freq_ref, feat_ref, *refs):
            basis_kernel(3 * part * nblk, tiles, nblk, freq_ref, feat_ref, *refs[-2:])

        return call(body, blocks, (frequencies, array), (after, buffer), scratch, "basis%d" % part, {3: 0})

    weight, table = call(
        functools.partial(weight_kernel, bands), (vm((3 * nblk + 15 & -16, blk), BF16), blocks),
        (even_side, r_odd, taps, lane_taps, hit, cells), (table,),
        [pltpu.VMEM((two, ny), F32)], "weight", {6: 1}, LONG,
    )
    w_odd, w_even = exchange("dec", weight, weight)
    table = basis(0, (1, 2), column, table, weight)
    table = basis(1, (0, 1, 2), c_even, table, weight)
    w_column, table = call(
        functools.partial(stack_weight_kernel, nblk), (vm(weight.shape, BF16), blocks), (weight, w_odd, w_even), (table,), name="stack_weights",
        aliases={3: 1},
    )
    x_odd, x_even = exchange("ra", w_column, w_column)
    early = call(
        early_kernel, vm((nblk, 2 * nfreq, blk), F32), (pip, table, w_column, x_even), (w_column,),
        [pltpu.VMEM((9 * nblk + 4, blk), F32)], "early_pairs", scalars=(code,),
    )
    table = basis(2, (0, 1, 2), c_odd, table, early)
    return pl.pallas_call(
        pair_kernel, out_shape=jax.ShapeDtypeStruct((nfreq, galaxies), BF16), in_specs=[SMEM] + [VMEM] * 6, out_specs=ANY,
        scratch_shapes=[
            pltpu.VMEM((9 * nblk + 4, blk), F32), pltpu.VMEM((nblk, 2 * nfreq, blk), F32),
            pltpu.VMEM((nblk, nfreq, blk), BF16), pltpu.SemaphoreType.DMA((nblk,)),
        ],
        compiler_params=params(), name="pairs",
    )(code, pip, table, early, w_column, x_even, x_odd)


def solution(mesh):
    in_specs = (
        P(None, "ra", "dec"),
        P(),
        P(None, ("ra", "dec")),
        P(),
        P(("ra", "dec")),
        P(("ra", "dec"), None, None, None),
        P(("ra", "dec"), None),
        P(("ra", "dec")),
    )
    out_specs = P(None, ("ra", "dec"))
    return jax.shard_map(per_device, mesh=mesh, in_specs=in_specs, out_specs=out_specs, check_vma=False)
```
